128 devices in a mesh: seq: 32 (over y, z, core), head: 4 (over x).
Axes of the slice: x: 4, y: 4, z: 4, core: 2. Of those that a mesh axis runs over, the one named last changes fastest.
Arguments:
- queries: bfloat16 [32768, 16, 128], P('seq', 'head'), may hold values from -8 to 8
- key_rows: bfloat16 [32768, 16, 128], P('seq', 'head'), may hold values from -8 to 8
- value_rows: bfloat16 [32768, 16, 128], P('seq', 'head'), may hold values from -6 to 6
- out_grad: bfloat16 [32768, 16, 128], P('seq', 'head'), may hold values from -6 to 6
- bucket_id: int32 [32768, 16], P('seq', 'head'), may hold values from 0 to 63, as said below
- bucket_slot: int32 [32768, 16], P('seq', 'head'), may hold values from 0 to 31, as said below
Outputs:
- attended: bfloat16 [32768, 16, 128], P('seq', 'head')
- grad_query: bfloat16 [32768, 16, 128], P('seq', 'head')
- grad_key: bfloat16 [32768, 16, 128], P('seq', 'head')
- grad_value: bfloat16 [32768, 16, 128], P('seq', 'head')
The draws below stay inside these ranges and needn't reach their ends.
Inputs may be any that keep to these rules, and one draw needn't show every extreme that they name: `bucket_id`: for each head and each device's 1024 tokens, at most 32 tokens name one bucket; in every head one bucket is named by exactly 32 tokens of every device. `bucket_slot`: tokens of one device with the same head and bucket have distinct slots, increasing with the token index.
All inputs are finite; a program needn't handle non-finite values.
Results may differ from the reference program's by a relative error of at most 0.013.
The reference program's roundings to bfloat16 on the way (of `rounded` and `dscore`) count: a program that leaves them out, or rounds other values in their place, can miss the bound.
Values may be sent and summed in bfloat16 or wider, within the bound.
A program may use at most 128 MiB of HBM per device.

```python
import math
import jax
import jax.numpy as jnp
from jax import lax

HEADS = 16
HD = 128
TOK_DEV = 1024
SLOTS_PER_SOURCE = 32
TOKENS = 32768
BUCKETS_PER_HEAD = 64
CAP = 1024


def bucket_pair(key):
    key = jax.random.fold_in(key, 101)
    slot_total = BUCKETS_PER_HEAD * SLOTS_PER_SOURCE
    peers = TOKENS // TOK_DEV
    keys = jax.random.split(key, peers * HEADS + HEADS)
    sorted_index = jnp.arange(slot_total, dtype=jnp.int32)
    tok_order = jnp.arange(TOK_DEV, dtype=jnp.int32)

    def one_source(sub):
        leading_entry, second = jax.random.split(sub)
        random_jitter = jax.random.randint(leading_entry, (slot_total,), 0, 1024, dtype=jnp.int32)
        rank_positions = jnp.where(sorted_index < SLOTS_PER_SOURCE, sorted_index - slot_total, random_jitter * slot_total + sorted_index)
        picked = jnp.argsort(rank_positions)[:TOK_DEV].astype(jnp.int32)
        mixed = jax.random.permutation(second, picked)
        owner_bucket = mixed // SLOTS_PER_SOURCE
        token_rank = jnp.argsort(owner_bucket * TOK_DEV + tok_order).astype(jnp.int32)
        ascending = jnp.sort(picked).astype(jnp.int32)
        placed = jnp.zeros((TOK_DEV,), jnp.int32).at[token_rank].set(ascending)
        return (placed // SLOTS_PER_SOURCE, placed % SLOTS_PER_SOURCE)
    raw, slots = jax.vmap(one_source)(keys[:peers * HEADS])
    relabel = jax.vmap(lambda sub: jax.random.permutation(sub, BUCKETS_PER_HEAD).astype(jnp.int32))(keys[peers * HEADS:])
    raw = raw.reshape(peers, HEADS, TOK_DEV)
    slots = slots.reshape(peers, HEADS, TOK_DEV)
    heads = jnp.arange(HEADS, dtype=jnp.int32)[None, :, None]
    buckets = relabel[heads, raw]
    buckets = jnp.transpose(buckets, (0, 2, 1)).reshape(TOKENS, HEADS)
    slots = jnp.transpose(slots, (0, 2, 1)).reshape(TOKENS, HEADS)
    return (buckets.astype(jnp.int32), slots.astype(jnp.int32))


def draw_bucket_id(key, part):
    buckets, slots = bucket_pair(key)
    return buckets


def draw_bucket_slot(key, part):
    buckets, slots = bucket_pair(key)
    return slots


def draw_queries(key, part):
    key = jax.random.fold_in(key, 11)
    second = jax.random.fold_in(key, 1)
    values = jnp.clip(jax.random.normal(second, (TOKENS, HEADS, HD), jnp.float32), -6.0, 6.0)
    return values.astype(jnp.bfloat16)


def draw_key_rows(key, part):
    key = jax.random.fold_in(key, 13)
    second = jax.random.fold_in(key, 1)
    values = jnp.clip(jax.random.normal(second, (TOKENS, HEADS, HD), jnp.float32), -6.0, 6.0)
    return values.astype(jnp.bfloat16)


def steps_of(own_key, extent, cuts, least, top_value):
    def one(axis_at, shards_of):
        steps = jax.random.uniform(jax.random.fold_in(jax.random.fold_in(own_key, 6), axis_at), (shards_of,), jnp.float32, least / len(cuts), top_value / len(cuts))
        return jnp.repeat(jnp.exp(steps), extent[axis_at] // shards_of).reshape((-1,) + (1,) * (len(extent) - axis_at - 1))

    level = one(*cuts[0])
    for cut in cuts[1:]:
        level = level * one(*cut)
    return level


def noise(own_key, extent, scale, reach, cuts=(), held_as=jnp.bfloat16):
    values = jax.random.normal(own_key, extent, jnp.float32) * scale
    if len(cuts) > 0:
        values = steps_of(own_key, extent, cuts, -0.22, 0.18) * values
    return jnp.clip(values, min=-reach, max=reach).astype(held_as)


def setup_inputs(seed: int = 0) -> dict:
    splits = jax.random.split(jax.random.key(seed), 7)
    queries = draw_queries(jax.random.fold_in(splits[6], 71), 0)
    key_rows = draw_key_rows(jax.random.fold_in(splits[6], 71), 0)
    value_rows = noise(splits[2], (TOKENS, HEADS, HD), 1.0, 6.0, ((0, 32), (1, 4)))
    out_grad = noise(splits[3], (TOKENS, HEADS, HD), 1.0, 6.0, ((0, 32), (1, 4)))
    bucket_id = draw_bucket_id(jax.random.fold_in(splits[6], 71), 0)
    bucket_slot = draw_bucket_slot(jax.random.fold_in(splits[6], 71), 0)
    return dict(queries=queries, key_rows=key_rows, value_rows=value_rows, out_grad=out_grad, bucket_id=bucket_id, bucket_slot=bucket_slot)


def bucket_all(block, valid, width):
    span = block.shape[0]
    scale = 1.0 / math.sqrt(width)
    q_part = block[:, :width]
    k_part = block[:, width:2 * width]
    v_part = block[:, 2 * width:3 * width]
    d_part = block[:, 3 * width:]
    sorted_index = jnp.arange(span, dtype=jnp.int32)
    allowed = (sorted_index[None, :] <= sorted_index[:, None]) & ((valid[None, :] > 0) | (sorted_index[None, :] == sorted_index[:, None]))
    scores = jnp.dot(q_part, k_part.T, preferred_element_type=jnp.float32) * scale
    scores = jnp.where(allowed, scores, jnp.float32(-1e+30))
    top = lax.optimization_barrier(jnp.max(scores, axis=1, keepdims=True))
    expd = jnp.where(allowed, jnp.exp(scores - top), jnp.float32(0.0))
    weights = expd / lax.optimization_barrier(jnp.sum(expd, axis=1, keepdims=True))
    rounded = weights.astype(jnp.bfloat16)
    attended = jnp.dot(rounded, v_part, preferred_element_type=jnp.float32).astype(jnp.bfloat16)
    dprob = jnp.dot(d_part, v_part.T, preferred_element_type=jnp.float32)
    delta = lax.optimization_barrier(jnp.sum(weights * dprob, axis=1, keepdims=True))
    dscore = (weights * (dprob - delta)).astype(jnp.bfloat16)
    grad_q = (jnp.dot(dscore, k_part, preferred_element_type=jnp.float32) * scale).astype(jnp.bfloat16)
    grad_k = (jnp.dot(dscore.T, q_part, preferred_element_type=jnp.float32) * scale).astype(jnp.bfloat16)
    grad_v = jnp.dot(rounded.T, d_part, preferred_element_type=jnp.float32).astype(jnp.bfloat16)
    return jnp.concatenate([attended, grad_q, grad_k, grad_v], axis=1)

def reference(queries, key_rows, value_rows, out_grad, bucket_id, bucket_slot):
    width = queries.shape[2]
    source = (jnp.arange(TOKENS, dtype=jnp.int32) // TOK_DEV).astype(jnp.int32)
    results = []
    for head_index in range(HEADS):
        joined = jnp.concatenate([queries[:, head_index], key_rows[:, head_index], value_rows[:, head_index], out_grad[:, head_index]], axis=1)
        flat = (bucket_id[:, head_index] * CAP + source * SLOTS_PER_SOURCE + bucket_slot[:, head_index]).astype(jnp.int32)
        buffer = jnp.zeros((BUCKETS_PER_HEAD * CAP, 4 * width), jnp.bfloat16).at[flat].set(joined)
        marks = jnp.zeros((BUCKETS_PER_HEAD * CAP,), jnp.bfloat16).at[flat].set(jnp.bfloat16(1.0))
        done = lax.map(lambda item: bucket_all(item[0], item[1], width), (buffer.reshape(BUCKETS_PER_HEAD, CAP, 4 * width), marks.reshape(BUCKETS_PER_HEAD, CAP)))
        results.append(done.reshape(BUCKETS_PER_HEAD * CAP, 4 * width)[flat])
    stacked = jnp.stack(results, axis=1)
    return (stacked[:, :, :width], stacked[:, :, width:2 * width], stacked[:, :, 2 * width:3 * width], stacked[:, :, 3 * width:])
```

```python
import functools
import math

import jax
import jax.numpy as jnp
from jax import lax
from jax.experimental import pallas as pl
from jax.experimental.pallas import tpu as pltpu
from jax.sharding import PartitionSpec as P

SLOTS_PER_SOURCE = 32
BUCKETS_PER_HEAD = 64
PEERS = 32
ROWS = 96
SPAN = PEERS * ROWS
HOT_ROWS = PEERS * SLOTS_PER_SOURCE
HOT_AT = (0, 10, 20, 30)
TQ, TK = 256, 512
FAR = 2.0**100
MESH = pl.DeviceIdType.MESH
F32, BF16, I32 = jnp.float32, jnp.bfloat16, jnp.int32


def both(chips):
    return [(dy, dz, dc) for dy, dz in chips for dc in (0, 1)]


FAR_MIX = [(1, 2), (3, 2), (2, 1), (2, 3)]
NEAR = [(1, 0), (3, 0), (0, 1), (0, 3)]
ROUNDS = [
    [(dy, dz, 0) for dy, dz in FAR_MIX],
    [(dy, dz, 1) for dy, dz in FAR_MIX],
    both([(2, 2)]),
    both([(1, 3), (3, 1)]),
    both([(1, 1), (3, 3)]),
    both([(2, 0), (0, 2)]),
    [(dy, dz, 0) for dy, dz in NEAR],
    [(dy, dz, 1) for dy, dz in NEAR] + [(0, 0, 1)],
]
OFFSETS = [o for r in ROUNDS for o in r]
FIRST = [sum(len(r) for r in ROUNDS[:i]) for i in range(len(ROUNDS))]
LAG = 2


def iota(shape, dim):
    return lax.broadcasted_iota(I32, shape, dim)


def dot(a, b, dims=((1,), (0,))):
    return lax.dot_general(a, b, (dims, ((), ())), preferred_element_type=F32)


def kernel(
    q_ref, k_ref, v_ref, d_ref, bid_ref,
    o_q, o_k, o_v, o_d, flag_out,
    wide, x, send, send_hot, recv, recv_hot, ret, ret_hot, meta, meta_in, flags,
    pos_row, pos_col, aug_q, aug_k, kt, vt, dk, dv, s_buf, p_buf, acc_o, acc_q,
    send_sem, recv_sem, meta_ssem, meta_rsem, hot_ssem, hot_rsem, back_ssem, back_rsem,
    flag_ssem, flag_rsem, own_sem,
):
    me = lax.axis_index("seq")
    col = lax.axis_index("head")
    y, z, c = me // 8, lax.rem(me // 2, 4), lax.rem(me, 2)
    scale = 1.0 / math.sqrt(128)
    to_exp2 = scale * math.log2(math.e)

    def peer(o, sign=1):
        return (
            lax.rem(y + sign * o[0] + 4, 4) * 8
            + lax.rem(z + sign * o[1] + 4, 4) * 2
            + lax.rem(c + o[2], 2)
        )

    barrier = pltpu.get_barrier_semaphore()
    for o in OFFSETS:
        pl.semaphore_signal(barrier, inc=1, device_id={"seq": peer(o)}, device_id_type=MESH)
    for step in (1, 2, 3):
        pl.semaphore_signal(
            barrier, inc=1, device_id={"head": lax.rem(col + step, 4)}, device_id_type=MESH
        )

    for a, ref in enumerate((q_ref, k_ref, v_ref, d_ref)):
        wide[...] = ref[...].astype(F32)
        for h in range(4):
            x[h // 2, pl.ds(h % 2 * 1024, 1024), a * 128 : a * 128 + 128] = wide[
                pl.ds(h, 1024, stride=4), :
            ].astype(BF16)

    def row_facts(shape):
        r = iota(shape, 0)
        return r // 64, lax.rem(r, 64)

    named = jnp.concatenate(
        [(iota((64, 1024), 0) == bid_ref[h : h + 1, :]).astype(F32) for h in range(4)], axis=0
    )
    earlier = (iota((1024, 1024), 0) < iota((1024, 1024), 1)).astype(F32).astype(BF16)
    rank = dot(named.astype(BF16), earlier)
    count = jnp.sum(named, axis=1, keepdims=True)
    full = (count == 32.0).astype(F32)
    count = count * (1.0 - full)
    bad = jnp.float32(0.0)
    for h in range(4):
        n_full = jnp.sum(full[h * 64 : h * 64 + 64])
        bad = jnp.maximum(bad, (n_full != 1.0).astype(F32))
    r0, r1 = iota((256, 256), 0), iota((256, 256), 1)

    def code_of(r):
        return lax.rem(r // 64, 2) * 2 + lax.rem(r, 2)

    def place_of(r):
        return (r // 128) * 32 + lax.rem(r, 64) // 2

    before = ((place_of(r0) == place_of(r1)) & (code_of(r1) < code_of(r0))).astype(F32).astype(BF16)
    lanes = jnp.broadcast_to(count, (256, 128))
    start = dot(before, lanes.astype(BF16))[:, :1]
    rows = iota((256, 1), 0)
    base = (lax.rem(rows, 64) // 2 * ROWS).astype(F32) + start
    hot_base = (SPAN + lax.rem(rows // 64, 2) * 32).astype(F32)
    base = jnp.where(full > 0, hot_base, base)
    landed = named * (rank + base)
    place = jnp.concatenate(
        [jnp.sum(landed[h * 64 : h * 64 + 64], axis=0, keepdims=True) for h in range(4)]
        + [jnp.zeros((124, 1024), F32)],
        axis=0,
    )
    pos_row[...] = place[:8].astype(I32)
    pos_col[...] = place.T.astype(I32)

    lane = iota((256, 128), 1)
    code = code_of(iota((256, 128), 0))
    w_start = jnp.where((lane <= 4) & (code < lane), lanes, 0.0).astype(BF16)
    w_end = jnp.where((lane < 4) & (code <= lane), lanes, 0.0).astype(BF16)
    mr, mc = iota((512, 256), 0), iota((512, 256), 1)
    mine = mr // 16 == lax.rem(mc, 64) // 2
    pick_start = (mine & (lax.rem(mr, 16) == mc // 128 * 2)).astype(F32).astype(BF16)
    pick_end = (mine & (lax.rem(mr, 16) == mc // 128 * 2 + 1)).astype(F32).astype(BF16)
    starts = dot(pick_start, w_start)
    bad = jnp.maximum(bad, (jnp.max(starts) > ROWS).astype(F32))
    kind, ml = lax.rem(iota((512, 128), 0), 16), iota((512, 128), 1)
    tail = jnp.where(((kind == 1) | (kind == 3)) & (ml == 4), jnp.float32(ROWS), 0.0)
    tail = tail + jnp.where(kind == 4, bad, 0.0)
    meta[...] = (starts + dot(pick_end, w_end) + tail).astype(BF16)

    pl.semaphore_wait(barrier, len(OFFSETS) + 3)

    def meta_copy(k):
        return pltpu.make_async_remote_copy(
            src_ref=meta.at[pl.ds(pl.multiple_of(peer(OFFSETS[k]) * 16, 16), 16)],
            dst_ref=meta_in.at[pl.ds(pl.multiple_of(me * 16, 16), 16)],
            send_sem=meta_ssem.at[k],
            recv_sem=meta_rsem.at[k],
            device_id={"seq": peer(OFFSETS[k])},
            device_id_type=MESH,
        )

    for k in range(len(OFFSETS)):
        meta_copy(k).start()
    own_meta = pl.ds(pl.multiple_of(me * 16, 16), 16)
    meta_in[own_meta, :] = meta[own_meta, :]

    own = pl.ds(pl.multiple_of(me * ROWS, ROWS), ROWS)

    def copy(phase, k):
        other = peer(OFFSETS[k])
        theirs = pl.ds(pl.multiple_of(other * ROWS, ROWS), ROWS)
        g = phase % 2
        src, dst = (send, recv) if phase < 2 else (recv, ret)
        return pltpu.make_async_remote_copy(
            src_ref=src.at[g, theirs],
            dst_ref=dst.at[g, own],
            send_sem=send_sem.at[phase, k],
            recv_sem=recv_sem.at[phase, k],
            device_id={"seq": other},
            device_id_type=MESH,
        )

    def own_copy(phase):
        g = phase % 2
        src, dst = (send, recv) if phase < 2 else (recv, ret)
        return pltpu.make_async_copy(src.at[g, own], dst.at[g, own], own_sem.at[phase])

    def hot_copy(h):
        return pltpu.make_async_remote_copy(
            src_ref=send_hot.at[h // 2, pl.ds(h % 2 * 32, 32)],
            dst_ref=recv_hot.at[pl.ds(pl.multiple_of(me * 32, 32), 32)],
            send_sem=hot_ssem.at[h],
            recv_sem=hot_rsem.at[me],
            device_id={"seq": HOT_AT[h]},
            device_id_type=MESH,
        )

    def hot_from(h, s):
        return pltpu.make_async_remote_copy(
            src_ref=send_hot.at[h // 2, pl.ds(h % 2 * 32, 32)],
            dst_ref=recv_hot.at[pl.ds(s * 32, 32)],
            send_sem=hot_ssem.at[h],
            recv_sem=hot_rsem.at[s],
            device_id={"seq": HOT_AT[h]},
            device_id_type=MESH,
        )

    def hot_own(h):
        return pltpu.make_async_copy(
            send_hot.at[h // 2, pl.ds(h % 2 * 32, 32)],
            recv_hot.at[pl.ds(HOT_AT[h] * 32, 32)],
            hot_ssem.at[h],
        )

    def back_copy(h, s):
        return pltpu.make_async_remote_copy(
            src_ref=recv_hot.at[pl.ds(s * 32, 32)],
            dst_ref=ret_hot.at[h // 2, pl.ds(h % 2 * 32, 32)],
            send_sem=back_ssem.at[s],
            recv_sem=back_rsem.at[h],
            device_id={"seq": s},
            device_id_type=MESH,
        )

    def back_own(h):
        return pltpu.make_async_copy(
            recv_hot.at[pl.ds(HOT_AT[h] * 32, 32)],
            ret_hot.at[h // 2, pl.ds(h % 2 * 32, 32)],
            back_rsem.at[h],
        )

    def issue(phase, r):
        if r >= LAG:
            for k in range(FIRST[r - LAG], FIRST[r - LAG] + len(ROUNDS[r - LAG])):
                copy(phase, k).wait_send()
        if r == 0:
            own_copy(phase).start()
        for k in range(FIRST[r], FIRST[r] + len(ROUNDS[r])):
            copy(phase, k).start()
        if r == len(ROUNDS) - 1:
            g = phase % 2
            for h in (2 * g, 2 * g + 1):
                if phase < 2:

                    @pl.when(me != HOT_AT[h])
                    def _():
                        hot_copy(h).start()

                    @pl.when(me == HOT_AT[h])
                    def _():
                        hot_own(h).start()

                else:

                    @pl.when(me == HOT_AT[h])
                    def _():
                        for s in range(PEERS):
                            if s != HOT_AT[h]:
                                back_copy(h, s).start()
                        back_own(h).start()

    def drain_sends(phase):
        for r in range(len(ROUNDS) - LAG, len(ROUNDS)):
            for k in range(FIRST[r], FIRST[r] + len(ROUNDS[r])):
                copy(phase, k).wait_send()
        g = phase % 2
        for h in (2 * g, 2 * g + 1):
            if phase < 2:

                @pl.when(me != HOT_AT[h])
                def _():
                    hot_copy(h).wait_send()

            else:

                @pl.when(me == HOT_AT[h])
                def _():
                    for s in range(PEERS):
                        if s != HOT_AT[h]:
                            back_copy(h, s).wait_send()

    def arrive(phase):
        for k in range(len(OFFSETS)):
            copy(phase, k).wait_recv()
        own_copy(phase).wait()

    def hot_arrive(h):
        for s in range(PEERS):
            if s != HOT_AT[h]:
                hot_from(h, s).wait_recv()
        hot_own(h).wait()

    def back_arrive(g):
        for h in (2 * g, 2 * g + 1):

            @pl.when(me != HOT_AT[h])
            def _():
                back_copy(h, 0).wait_recv()

            @pl.when(me == HOT_AT[h])
            def _():
                back_own(h).wait()

    def pack_hot(g):
        at = jnp.concatenate([pos_row[2 * g : 2 * g + 1, :], pos_row[2 * g + 1 : 2 * g + 2, :]], axis=1)
        pick = (iota((64, 2048), 0) + SPAN == at).astype(F32).astype(BF16)
        send_hot[g] = dot(pick, x[g]).astype(BF16)

    def pack(g, m):
        at = jnp.concatenate([pos_row[2 * g : 2 * g + 1, :], pos_row[2 * g + 1 : 2 * g + 2, :]], axis=1)
        pick = (iota((384, 2048), 0) == at - m * 384).astype(F32).astype(BF16)
        send[g, pl.ds(pl.multiple_of(m * 384, 384), 384), :] = dot(pick, x[g]).astype(BF16)

    def unpack(g, m):
        h = m // 4
        t = pl.ds(pl.multiple_of(lax.rem(m, 4) * 256, 256), 256)
        at = jnp.where(h == 0, pos_col[t, 2 * g : 2 * g + 1], pos_col[t, 2 * g + 1 : 2 * g + 2])
        pick = (iota((256, SPAN), 1) == at).astype(F32).astype(BF16)
        hot_pick = (iota((256, 64), 1) + SPAN == at).astype(F32).astype(BF16)
        got = dot(pick, ret[g]) + dot(hot_pick, ret_hot[g])
        x[g, pl.ds(pl.multiple_of(m * 256, 256), 256), :] = got.astype(BF16)

    def attend(rows_ref, span, coded, between):
        def body(i, _):
            between(i)
            qs = pl.ds(pl.multiple_of(i * TQ, TQ), TQ)
            q_i = rows_ref[qs, 0:128]
            d_i = rows_ref[qs, 384:512]
            q_a = jnp.concatenate([q_i, aug_q[qs, :]], axis=1) if coded else q_i
            tiles = (i * TQ) // TK + 1

            def score(j, top):
                ks = pl.ds(pl.multiple_of(j * TK, TK), TK)
                k_j = rows_ref[ks, 128:256]
                if coded:
                    k_j = jnp.concatenate([k_j, aug_k[ks, :]], axis=1)
                s = dot(k_j, q_a, ((1,), (1,)))
                gap = iota((TK, TQ), 0) - iota((TK, TQ), 1)
                s = jnp.where(gap <= i * TQ - j * TK, s, -1e30)
                s_buf[ks, :] = s
                return jnp.maximum(top, jnp.max(s, axis=0, keepdims=True))

            top = lax.fori_loop(0, tiles, score, jnp.full((1, TQ), -1e30, F32))

            def weigh(j, sums):
                total, delta = sums
                ks = pl.ds(pl.multiple_of(j * TK, TK), TK)
                p = jnp.exp2((s_buf[ks, :] - top) * to_exp2)
                dp = dot(rows_ref[ks, 256:384], d_i, ((1,), (1,)))
                s_buf[ks, :] = p
                p_buf[ks, :] = dp
                return (
                    total + jnp.sum(p, axis=0, keepdims=True),
                    delta + jnp.sum(p * dp, axis=0, keepdims=True),
                )

            none = jnp.zeros((1, TQ), F32)
            total, delta = lax.fori_loop(0, tiles, weigh, (none, none))
            inv = 1.0 / total
            delta = delta * inv
            acc_o[...] = jnp.zeros_like(acc_o)
            acc_q[...] = jnp.zeros_like(acc_q)

            def spread(j, _):
                ks = pl.ds(pl.multiple_of(j * TK, TK), TK)
                w = s_buf[ks, :] * inv
                rounded = w.astype(BF16)
                ds = (w * (p_buf[ks, :] - delta)).astype(BF16)
                acc_o[...] += dot(vt[:, ks], rounded)
                acc_q[...] += dot(kt[:, ks], ds)
                dv[ks, :] += dot(rounded, d_i)
                dk[ks, :] += dot(ds, q_i)
                return 0

            lax.fori_loop(0, tiles, spread, 0)
            rows_ref[qs, 0:128] = acc_o[...].T.astype(BF16)
            rows_ref[qs, 384:512] = (acc_q[...] * scale).T.astype(BF16)
            return 0

        def ready(j, _):
            ks = pl.ds(pl.multiple_of(j * TK, TK), TK)
            kt[:, ks] = rows_ref[ks, 128:256].astype(F32).T.astype(BF16)
            vt[:, ks] = rows_ref[ks, 256:384].astype(F32).T.astype(BF16)
            dk[ks, :] = jnp.zeros((TK, 128), F32)
            dv[ks, :] = jnp.zeros((TK, 128), F32)
            return 0

        lax.fori_loop(0, span // TK, ready, 0)
        lax.fori_loop(0, span // TQ, body, 0)

        def finish(j, _):
            ks = pl.ds(pl.multiple_of(j * TK, TK), TK)
            rows_ref[ks, 128:256] = (dk[ks, :] * scale).astype(BF16)
            rows_ref[ks, 256:384] = dv[ks, :].astype(BF16)
            return 0

        lax.fori_loop(0, span // TK, finish, 0)

    def codes(g):
        def body(s, _):
            note = meta_in[pl.ds(pl.multiple_of(s * 16, 16), 16), :].astype(F32)
            r = iota((ROWS, 128), 0).astype(F32)
            inside = (r >= note[2 * g : 2 * g + 1]) & (r < note[2 * g + 1 : 2 * g + 2])
            known = iota((ROWS, 128), 1) <= 4
            at = pl.ds(pl.multiple_of(s * ROWS, ROWS), ROWS)
            aug_q[at, :] = jnp.where(inside, 1.0, 0.0).astype(BF16)
            aug_k[at, :] = jnp.where(known & ~inside, -FAR, 0.0).astype(BF16)
            return 0

        lax.fori_loop(0, PEERS, body, 0)

    n_rounds = len(ROUNDS)

    def hot_work(g):
        for h in (2 * g, 2 * g + 1):

            @pl.when(me == HOT_AT[h])
            def _():
                hot_arrive(h)
                attend(recv_hot, HOT_ROWS, False, lambda i: None)

    def pack_body(g):
        def body(m, _):
            pack(g, m)
            return 0

        lax.fori_loop(0, 8, body, 0)
        pack_hot(g)

    pack_body(0)
    issue(0, 0)
    issue(0, 1)

    def pack_send(m, _):
        pack(1, m)
        for r in range(2, n_rounds):

            @pl.when(m == r)
            def _():
                issue(0, r)

        return 0

    lax.fori_loop(0, 8, pack_send, 0)
    pack_hot(1)

    for k in range(len(OFFSETS)):
        meta_copy(k).wait()
    noted = meta_in[...].astype(F32)
    noted = jnp.where(lax.rem(iota((512, 128), 0), 16) == 4, noted, 0.0)
    flags[0] = jnp.broadcast_to(jnp.max(noted, axis=0, keepdims=True), (16, 128)).astype(BF16)

    def flag_copy(step):
        return pltpu.make_async_remote_copy(
            src_ref=flags.at[0],
            dst_ref=flags.at[step],
            send_sem=flag_ssem.at[step],
            recv_sem=flag_rsem.at[step],
            device_id={"head": lax.rem(col + step, 4)},
            device_id_type=MESH,
        )

    for step in (1, 2, 3):
        flag_copy(step).start()

    codes(0)
    issue(1, 0)
    issue(1, 1)
    arrive(0)
    drain_sends(0)

    def between_to(phase):
        def between(i):
            for r in range(2, n_rounds):

                @pl.when(i == r + 1)
                def _():
                    issue(phase, r)

        return between

    attend(recv.at[0], SPAN, True, between_to(1))
    hot_work(0)
    codes(1)
    issue(2, 0)
    issue(2, 1)
    arrive(1)
    drain_sends(1)
    attend(recv.at[1], SPAN, True, between_to(2))
    hot_work(1)
    issue(3, 0)
    issue(3, 1)
    arrive(2)
    back_arrive(0)
    drain_sends(2)

    def unpack_send(m, _):
        unpack(0, m)
        for r in range(2, n_rounds):

            @pl.when(m == r)
            def _():
                issue(3, r)

        return 0

    lax.fori_loop(0, 8, unpack_send, 0)
    for step in (1, 2, 3):
        flag_copy(step).wait()
    any_flag = jnp.maximum(
        jnp.maximum(flags[0].astype(F32), flags[1].astype(F32)),
        jnp.maximum(flags[2].astype(F32), flags[3].astype(F32)),
    )
    flag_out[...] = any_flag[:8]
    arrive(3)
    back_arrive(1)
    drain_sends(3)

    def unpack_last(m, _):
        unpack(1, m)
        return 0

    lax.fori_loop(0, 8, unpack_last, 0)
    for a, ref in ((0, o_q), (3, o_k), (1, o_v), (2, o_d)):
        for h in range(4):
            wide[pl.ds(h, 1024, stride=4), :] = x[
                h // 2, pl.ds(h % 2 * 1024, 1024), a * 128 : a * 128 + 128
            ].astype(F32)
        ref[...] = wide[...].astype(BF16)


def quick(queries, key_rows, value_rows, out_grad, bucket_id):
    rows = [a.reshape(4096, 128) for a in (queries, key_rows, value_rows, out_grad)]
    vmem = pl.BlockSpec(memory_space=pltpu.VMEM)
    n = len(OFFSETS)
    dma = pltpu.SemaphoreType.DMA
    outs = pl.pallas_call(
        kernel,
        out_shape=[jax.ShapeDtypeStruct((4096, 128), BF16)] * 4
        + [jax.ShapeDtypeStruct((8, 128), F32)],
        in_specs=[vmem] * 5,
        out_specs=[vmem] * 5,
        scratch_shapes=[
            pltpu.VMEM((4096, 128), F32),
            pltpu.VMEM((2, 2048, 512), BF16),
            pltpu.VMEM((2, SPAN, 512), BF16),
            pltpu.VMEM((2, 64, 512), BF16),
            pltpu.VMEM((2, SPAN, 512), BF16),
            pltpu.VMEM((HOT_ROWS, 512), BF16),
            pltpu.VMEM((2, SPAN, 512), BF16),
            pltpu.VMEM((2, 64, 512), BF16),
            pltpu.VMEM((512, 128), BF16),
            pltpu.VMEM((512, 128), BF16),
            pltpu.VMEM((4, 16, 128), BF16),
            pltpu.VMEM((8, 1024), I32),
            pltpu.VMEM((1024, 128), I32),
            pltpu.VMEM((SPAN, 128), BF16),
            pltpu.VMEM((SPAN, 128), BF16),
            pltpu.VMEM((128, SPAN), BF16),
            pltpu.VMEM((128, SPAN), BF16),
            pltpu.VMEM((SPAN, 128), F32),
            pltpu.VMEM((SPAN, 128), F32),
            pltpu.VMEM((SPAN, TQ), F32),
            pltpu.VMEM((SPAN, TQ), F32),
            pltpu.VMEM((128, TQ), F32),
            pltpu.VMEM((128, TQ), F32),
            dma((4, n)), dma((4, n)), dma((n,)), dma((n,)), dma((4,)), dma((PEERS,)),
            dma((PEERS,)), dma((4,)), dma((4,)), dma((4,)), dma((4,)),
        ],
        compiler_params=pltpu.CompilerParams(
            collective_id=0, has_side_effects=True, vmem_limit_bytes=60 * 2**20
        ),
        name="bucket_layer",
    )(*rows, bucket_id.T)
    return [a.reshape(1024, 4, 128) for a in outs[:4]], outs[4][0, 0] > 0


def bucket_weights(q_part, k_part, valid, scale):
    span = q_part.shape[0]
    sorted_index = jnp.arange(span, dtype=I32)
    allowed = (sorted_index[None, :] <= sorted_index[:, None]) & (
        (valid[None, :] > 0) | (sorted_index[None, :] == sorted_index[:, None])
    )
    scores = jnp.dot(q_part, k_part.T, preferred_element_type=F32) * scale
    scores = jnp.where(allowed, scores, F32(-1e30))
    top = jnp.max(scores, axis=1, keepdims=True)
    expd = jnp.where(allowed, jnp.exp(scores - top), F32(0.0))
    return expd / jnp.sum(expd, axis=1, keepdims=True)


def bucket_forward(block, valid, width):
    scale = 1.0 / math.sqrt(width)
    weights = bucket_weights(block[:, :width], block[:, width : 2 * width], valid, scale)
    rounded = weights.astype(BF16)
    return jnp.dot(rounded, block[:, 2 * width :], preferred_element_type=F32).astype(
        BF16
    )


def bucket_backward(block, d_part, valid, width):
    scale = 1.0 / math.sqrt(width)
    q_part = block[:, :width]
    k_part = block[:, width : 2 * width]
    v_part = block[:, 2 * width : 3 * width]
    weights = bucket_weights(q_part, k_part, valid, scale)
    rounded = weights.astype(BF16)
    dprob = jnp.dot(d_part, v_part.T, preferred_element_type=F32)
    delta = jnp.sum(weights * dprob, axis=1, keepdims=True)
    dscore = (weights * (dprob - delta)).astype(BF16)
    grad_q = (jnp.dot(dscore, k_part, preferred_element_type=F32) * scale).astype(
        BF16
    )
    grad_k = (jnp.dot(dscore.T, q_part, preferred_element_type=F32) * scale).astype(
        BF16
    )
    grad_v = jnp.dot(rounded.T, d_part, preferred_element_type=F32).astype(BF16)
    return (rounded, v_part, grad_q, grad_k, grad_v)


def bucket_grads(block, d_part, valid, width):
    rounded, v_part, grad_q, grad_k, grad_v = bucket_backward(block, d_part, valid, width)
    return jnp.concatenate([grad_q, grad_k, grad_v], axis=1)


def slow(queries, key_rows, value_rows, out_grad, bucket_id, bucket_slot):
    peers = lax.axis_size("seq")
    tok_count, group, width = queries.shape
    per_owner = BUCKETS_PER_HEAD // peers
    span = peers * SLOTS_PER_SOURCE
    total = group * per_owner * span
    owner = bucket_id // per_owner
    local_bucket = bucket_id % per_owner
    head_index = jnp.arange(group, dtype=I32)[None, :]
    flat = (
        (head_index * per_owner + local_bucket) * span + owner * SLOTS_PER_SOURCE + bucket_slot
    ).reshape(-1)
    marks = (
        jnp.zeros((total,), BF16)
        .at[flat]
        .set(BF16(1.0))
        .reshape(group, per_owner, span)
    )

    def spread(rows):
        columns = rows.shape[-1]
        placed = jnp.zeros((total, columns), rows.dtype).at[flat].set(rows.reshape(-1, columns))
        return placed.reshape(group, per_owner, span, columns)

    def collect(buffer):
        columns = buffer.shape[-1]
        return buffer.reshape(total, columns)[flat].reshape(tok_count, group, columns)

    joined = jnp.concatenate([queries, key_rows, value_rows], axis=2)
    blocks, valid = (
        lax.all_to_all(spread(joined), "seq", split_axis=2, concat_axis=2, tiled=True),
        lax.all_to_all(marks, "seq", split_axis=2, concat_axis=2, tiled=True),
    )
    flat_blocks = blocks.reshape(-1, span, 3 * width)
    flat_valid = valid.reshape(-1, span)
    attended = lax.map(
        lambda item: bucket_forward(item[0], item[1], width), (flat_blocks, flat_valid)
    )
    attended = lax.all_to_all(
        attended.reshape(group, per_owner, span, width),
        "seq",
        split_axis=2,
        concat_axis=2,
        tiled=True,
    )
    incoming = lax.all_to_all(spread(out_grad), "seq", split_axis=2, concat_axis=2, tiled=True)
    grads = lax.map(
        lambda item: bucket_grads(item[0], item[1], item[2], width),
        (flat_blocks, incoming.reshape(-1, span, width), flat_valid),
    )
    grads = lax.all_to_all(
        grads.reshape(group, per_owner, span, 3 * width),
        "seq",
        split_axis=2,
        concat_axis=2,
        tiled=True,
    )
    gathered = collect(grads)
    return (
        collect(attended),
        gathered[:, :, :width],
        gathered[:, :, width : 2 * width],
        gathered[:, :, 2 * width :],
    )


def shards(queries, key_rows, value_rows, out_grad, bucket_id, bucket_slot):
    fast, crowded = quick(queries, key_rows, value_rows, out_grad, bucket_id)
    return lax.cond(
        crowded,
        lambda: slow(queries, key_rows, value_rows, out_grad, bucket_id, bucket_slot),
        lambda: tuple(fast),
    )


def solution(mesh):
    in_specs = (
        P("seq", "head", None),
        P("seq", "head", None),
        P("seq", "head", None),
        P("seq", "head", None),
        P("seq", "head"),
        P("seq", "head"),
    )
    out_specs = (
        P("seq", "head", None),
        P("seq", "head", None),
        P("seq", "head", None),
        P("seq", "head", None),
    )
    return jax.shard_map(shards, mesh=mesh, in_specs=in_specs, out_specs=out_specs, check_vma=False)
```

```python
import functools
import math

import jax
import jax.numpy as jnp
from jax import lax
from jax.experimental import pallas as pl
from jax.experimental.pallas import tpu as pltpu
from jax.sharding import PartitionSpec as P

SLOTS_PER_SOURCE = 32
BUCKETS_PER_HEAD = 64
PEERS = 32
ROWS = 96
SPAN = PEERS * ROWS
HOT_ROWS = PEERS * SLOTS_PER_SOURCE
HOT_AT = (0, 10, 20, 30)
TQ, TK = 256, 512
HALF = ROWS // 2
WINDOWS = PEERS * 64
SECOND = ((2, 0), (2, 1), (1, 0), (3, 0), (1, 1), (3, 1), (0, 1))
SWITCH = 6
FAR = 2.0**100
MESH = pl.DeviceIdType.MESH
F32, BF16, I32 = jnp.float32, jnp.bfloat16, jnp.int32


def iota(shape, dim):
    return lax.broadcasted_iota(I32, shape, dim)


def dot(a, b, dims=((1,), (0,))):
    return lax.dot_general(a, b, (dims, ((), ())), preferred_element_type=F32)


def kernel(
    q_ref, k_ref, v_ref, d_ref, bid_ref,
    x, flag_out,
    wide, send, send_hot, recv, recv_hot, ret, ret_hot, mid, rows_buf, meta, meta_in, flags,
    pos_row, pos_col, aug_q, aug_k, kt, vt, dk, dv, p_buf, dp_buf, tops, acc_o, acc_q,
    one_ssem, one_rsem, two_ssem, two_rsem, own_sem, free_sem, meta_ssem, meta_rsem,
    hot_ssem, hot_rsem, back_ssem, back_rsem, flag_ssem, flag_rsem,
):
    me = lax.axis_index("seq")
    col = lax.axis_index("head")
    y, z, c = me // 8, lax.rem(me // 2, 4), lax.rem(me, 2)
    scale = 1.0 / math.sqrt(128)
    to_exp2 = scale * math.log2(math.e)

    def ya(d):
        return lax.rem(y + d, 4)

    def za(d):
        return lax.rem(z + d, 4)

    def dev(yy, zz, cc):
        return yy * 8 + zz * 2 + cc

    barrier = pltpu.get_barrier_semaphore()
    for k in range(1, PEERS):
        pl.semaphore_signal(
            barrier, inc=1, device_id={"seq": lax.rem(me + k, PEERS)}, device_id_type=MESH
        )
    for step in (1, 2, 3):
        pl.semaphore_signal(
            barrier, inc=1, device_id={"head": lax.rem(col + step, 4)}, device_id_type=MESH
        )

    for a, ref in enumerate((q_ref, k_ref, v_ref, d_ref)):
        wide[...] = ref[...].astype(F32)
        for h in range(4):
            x[h, :, a * 128 : a * 128 + 128] = wide[
                pl.ds(h, 1024, stride=4), :
            ].astype(BF16)

    named = jnp.concatenate(
        [(iota((64, 1024), 0) == bid_ref[h : h + 1, :]).astype(F32) for h in range(4)], axis=0
    )
    earlier = (iota((1024, 1024), 0) < iota((1024, 1024), 1)).astype(F32).astype(BF16)
    rank = dot(named.astype(BF16), earlier)
    count = jnp.sum(named, axis=1, keepdims=True)
    full = (count == 32.0).astype(F32)
    count = count * (1.0 - full)
    bad = jnp.float32(0.0)
    for h in range(4):
        n_full = jnp.sum(full[h * 64 : h * 64 + 64])
        bad = jnp.maximum(bad, (n_full != 1.0).astype(F32))
    r0, r1 = iota((256, 256), 0), iota((256, 256), 1)
    alike = r0 // 2 == r1 // 2
    lanes = jnp.broadcast_to(count, (256, 128))
    lanes16 = lanes.astype(BF16)
    start = dot((alike & (r1 < r0)).astype(F32).astype(BF16), lanes16)[:, :1]
    both = dot(alike.astype(F32).astype(BF16), lanes16)[:, :1]
    rows = iota((256, 1), 0)
    owner = lax.rem(rows, 64) // 2
    second = lax.rem(rows // 64, 2)
    inside = start + jnp.where(second == 1, ROWS - both, 0.0)
    at_hot = (second * 32).astype(F32)
    base = jnp.where(full > 0, SPAN + at_hot, (owner * ROWS).astype(F32) + inside)
    back = jnp.where(full > 0, WINDOWS + at_hot, (owner * 64 - second * 32).astype(F32) + inside)

    def per_head(table):
        landed = named * (rank + table)
        return jnp.concatenate(
            [jnp.sum(landed[h * 64 : h * 64 + 64], axis=0, keepdims=True) for h in range(4)],
            axis=0,
        )

    pos_row[0:4, :] = per_head(base).astype(I32)
    place = jnp.concatenate([per_head(back), jnp.zeros((124, 1024), F32)], axis=0)
    pos_col[...] = place.T.astype(I32)

    lane, r2 = iota((256, 128), 1), iota((256, 128), 0)
    code = lax.rem(r2 // 64, 2) * 2 + lax.rem(r2, 2)
    front, rear = code < 2, code >= 2
    low = (lane < 2) | (lane == 4)
    high = (lane == 2) | (lane == 3)
    w_start = jnp.where((low & front & (code < lane)) | (lane == 5), lanes, 0.0)
    w_start = w_start - jnp.where(high & rear & (code >= lane), lanes, 0.0)
    w_end = jnp.where((lane < 2) & front & (code <= lane), lanes, 0.0)
    w_end = w_end - jnp.where((high & (code > lane)) | (lane == 4) & rear, lanes, 0.0)
    mr, mc = iota((512, 256), 0), iota((512, 256), 1)
    mine = mr // 16 == lax.rem(mc, 64) // 2
    pick_start = (mine & (lax.rem(mr, 16) == mc // 128 * 2)).astype(F32).astype(BF16)
    pick_end = (mine & (lax.rem(mr, 16) == mc // 128 * 2 + 1)).astype(F32).astype(BF16)
    starts = dot(pick_start, w_start.astype(BF16))
    kind, ml = lax.rem(iota((512, 128), 0), 16), iota((512, 128), 1)
    bad = jnp.maximum(bad, (jnp.max(jnp.where(ml == 5, starts, 0.0)) > ROWS).astype(F32))
    high = (ml == 2) | (ml == 3)
    to_rows = ((kind == 0) | (kind == 2)) & high
    to_rows = to_rows | ((kind == 1) | (kind == 3)) & (high | (ml == 4))
    tail = jnp.where(to_rows, jnp.float32(ROWS), 0.0) + jnp.where(kind == 4, bad, 0.0)
    meta[...] = (starts + dot(pick_end, w_end.astype(BF16)) + tail).astype(BF16)

    pl.semaphore_wait(barrier, PEERS - 1 + 3)

    def meta_copy(k):
        other = lax.rem(me + k, PEERS)
        return pltpu.make_async_remote_copy(
            src_ref=meta.at[pl.ds(pl.multiple_of(other * 16, 16), 16)],
            dst_ref=meta_in.at[pl.ds(pl.multiple_of(me * 16, 16), 16)],
            send_sem=meta_ssem.at[k],
            recv_sem=meta_rsem.at[k],
            device_id={"seq": other},
            device_id_type=MESH,
        )

    for k in range(1, PEERS):
        meta_copy(k).start()
    own_meta = pl.ds(pl.multiple_of(me * 16, 16), 16)
    meta_in[own_meta, :] = meta[own_meta, :]

    def ends(phase):
        return (send, recv) if phase < 2 else (recv, ret)

    def one(phase, half, d):
        g, src = phase % 2, ends(phase)[0]
        if half == 0:
            from_, to, other = src.at[g, ya(d), :, :, 0:HALF], mid.at[g, 0, y], dev(ya(d), z, c)
        else:
            from_, to, other = src.at[g, :, za(d), :, HALF:ROWS], mid.at[g, 1, z], dev(y, za(d), c)
        return pltpu.make_async_remote_copy(
            src_ref=from_,
            dst_ref=to,
            send_sem=one_ssem.at[phase, half, d],
            recv_sem=one_rsem.at[phase, half, d],
            device_id={"seq": other},
            device_id_type=MESH,
        )

    def one_own(phase, half):
        g, src = phase % 2, ends(phase)[0]
        sem = own_sem.at[phase, half, 0]
        if half == 0:
            return pltpu.make_async_copy(src.at[g, y, :, :, 0:HALF], mid.at[g, 0, y], sem)
        return pltpu.make_async_copy(src.at[g, :, z, :, HALF:ROWS], mid.at[g, 1, z], sem)

    def two(phase, half, d, e):
        g, dst = phase % 2, ends(phase)[1]
        cc = lax.rem(c + e, 2)
        if half == 0:
            from_, to = mid.at[g, 0, :, za(d), cc], dst.at[g, :, z, c, 0:HALF]
            other = dev(y, za(d), cc)
        else:
            from_, to = mid.at[g, 1, :, ya(d), cc], dst.at[g, y, :, c, HALF:ROWS]
            other = dev(ya(d), z, cc)
        return pltpu.make_async_remote_copy(
            src_ref=from_,
            dst_ref=to,
            send_sem=two_ssem.at[phase, half, d * 2 + e],
            recv_sem=two_rsem.at[phase, half, d * 2 + e],
            device_id={"seq": other},
            device_id_type=MESH,
        )

    def two_own(phase, half):
        g, dst = phase % 2, ends(phase)[1]
        sem = own_sem.at[phase, half, 1]
        if half == 0:
            return pltpu.make_async_copy(mid.at[g, 0, :, z, c], dst.at[g, :, z, c, 0:HALF], sem)
        return pltpu.make_async_copy(mid.at[g, 1, :, y, c], dst.at[g, y, :, c, HALF:ROWS], sem)

    def hot_copy(h):
        return pltpu.make_async_remote_copy(
            src_ref=send_hot.at[h // 2, pl.ds(h % 2 * 32, 32)],
            dst_ref=recv_hot.at[pl.ds(pl.multiple_of(me * 32, 32), 32)],
            send_sem=hot_ssem.at[h],
            recv_sem=hot_rsem.at[me],
            device_id={"seq": HOT_AT[h]},
            device_id_type=MESH,
        )

    def hot_from(h, s):
        return pltpu.make_async_remote_copy(
            src_ref=send_hot.at[h // 2, pl.ds(h % 2 * 32, 32)],
            dst_ref=recv_hot.at[pl.ds(s * 32, 32)],
            send_sem=hot_ssem.at[h],
            recv_sem=hot_rsem.at[s],
            device_id={"seq": HOT_AT[h]},
            device_id_type=MESH,
        )

    def hot_own(h):
        return pltpu.make_async_copy(
            send_hot.at[h // 2, pl.ds(h % 2 * 32, 32)],
            recv_hot.at[pl.ds(HOT_AT[h] * 32, 32)],
            hot_ssem.at[h],
        )

    def back_copy(h, s):
        return pltpu.make_async_remote_copy(
            src_ref=recv_hot.at[pl.ds(s * 32, 32)],
            dst_ref=ret_hot.at[h // 2, pl.ds(h % 2 * 32, 32)],
            send_sem=back_ssem.at[s],
            recv_sem=back_rsem.at[h],
            device_id={"seq": s},
            device_id_type=MESH,
        )

    def back_own(h):
        return pltpu.make_async_copy(
            recv_hot.at[pl.ds(HOT_AT[h] * 32, 32)],
            ret_hot.at[h // 2, pl.ds(h % 2 * 32, 32)],
            back_rsem.at[h],
        )

    def start_one(phase):
        if phase >= 2:
            pl.semaphore_wait(free_sem.at[phase % 2], 6)
        for d in (2, 1, 3):
            for half in (0, 1):
                one(phase, half, d).start()
        for half in (0, 1):
            one_own(phase, half).start()
        g = phase % 2
        for h in (2 * g, 2 * g + 1):
            if phase < 2:

                @pl.when(me != HOT_AT[h])
                def _():
                    hot_copy(h).start()

                @pl.when(me == HOT_AT[h])
                def _():
                    hot_own(h).start()

    def start_two(phase):
        for half in (0, 1):
            for d in (1, 2, 3):
                one(phase, half, d).wait_recv()
            one_own(phase, half).wait()
            for d, e in SECOND:
                two(phase, half, d, e).start()
            two_own(phase, half).start()

    def arrive(phase):
        for half in (0, 1):
            for d, e in SECOND:
                two(phase, half, d, e).wait_recv()
            two_own(phase, half).wait()

    def drain(phase):
        for half in (0, 1):
            for d in (1, 2, 3):
                one(phase, half, d).wait_send()
            for d, e in SECOND:
                two(phase, half, d, e).wait_send()
        if phase < 2:
            g = phase % 2
            for d in (1, 2, 3):
                for other in (dev(ya(d), z, c), dev(y, za(d), c)):
                    pl.semaphore_signal(
                        free_sem.at[g], inc=1, device_id={"seq": other}, device_id_type=MESH
                    )
            for h in (2 * g, 2 * g + 1):

                @pl.when(me != HOT_AT[h])
                def _():
                    hot_copy(h).wait_send()

    def back_start(h):
        for s in range(PEERS):
            if s != HOT_AT[h]:
                back_copy(h, s).start()
        back_own(h).start()

    def back_drain(g):
        for h in (2 * g, 2 * g + 1):

            @pl.when(me == HOT_AT[h])
            def _():
                for s in range(PEERS):
                    if s != HOT_AT[h]:
                        back_copy(h, s).wait_send()

    def hot_arrive(h):
        for s in range(PEERS):
            if s != HOT_AT[h]:
                hot_from(h, s).wait_recv()
        hot_own(h).wait()

    def back_arrive(g):
        for h in (2 * g, 2 * g + 1):

            @pl.when(me != HOT_AT[h])
            def _():
                back_copy(h, 0).wait_recv()

            @pl.when(me == HOT_AT[h])
            def _():
                back_own(h).wait()

    def picked(shape, at, first):
        index = iota(shape, 0)
        return (index // 32 * ROWS + lax.rem(index, 32) == at - first).astype(F32).astype(BF16)

    def pack(g):
        a, b = pos_row[2 * g : 2 * g + 1, :], pos_row[2 * g + 1 : 2 * g + 2, :]

        def body(m, _):
            first = m * 16 * ROWS
            two_y = pl.ds(m * 2, 2)
            shape = (2, 4, 2, 32, 512)
            p = picked((512, 1024), a, first)
            send[g, two_y, :, :, 0:32, :] = dot(p, x[2 * g]).astype(BF16).reshape(shape)
            p = picked((512, 1024), b, first + 64)
            send[g, two_y, :, :, 64:96, :] = dot(p, x[2 * g + 1]).astype(BF16).reshape(shape)
            p = picked((512, 1024), a, first + 32)
            t = dot(p, x[2 * g])
            p = picked((512, 1024), b, first + 32)
            t = t + dot(p, x[2 * g + 1])
            send[g, two_y, :, :, 32:64, :] = t.astype(BF16).reshape(shape)
            return 0

        lax.fori_loop(0, 2, body, 0)
        for k, at in ((0, a), (1, b)):
            pick = (iota((32, 1024), 0) + (SPAN + k * 32) == at).astype(F32).astype(BF16)
            send_hot[g, k * 32 : k * 32 + 32] = dot(pick, x[2 * g + k]).astype(BF16)

    def unpack(g):
        def body(m, _):
            t = pl.ds(pl.multiple_of(m * 512, 512), 512)
            for k in (0, 1):
                at = pos_col[t, 2 * g + k : 2 * g + k + 1]
                pick = (iota((512, WINDOWS), 1) == at).astype(F32).astype(BF16)
                hot_pick = (iota((512, 64), 1) + WINDOWS == at).astype(F32).astype(BF16)
                got = ret[g, :, :, :, k * 32 : k * 32 + 64, :].reshape(WINDOWS, 512)
                x[2 * g + k, t, :] = (dot(pick, got) + dot(hot_pick, ret_hot[g])).astype(BF16)
            return 0

        lax.fori_loop(0, 2, body, 0)

    def attend(rows_ref, span, coded, between):
        def body(i, _):
            between(i)
            qs = pl.ds(pl.multiple_of(i * TQ, TQ), TQ)
            q_i = rows_ref[qs, 0:128]
            d_i = rows_ref[qs, 384:512]
            q_a = jnp.concatenate([q_i, aug_q[qs, :]], axis=1) if coded else q_i
            full_tiles = (i * TQ) // TK

            def weigh(j, sums, edge):
                top, total, delta = sums
                ks = pl.ds(pl.multiple_of(j * TK, TK), TK)
                k_j = rows_ref[ks, 128:256]
                if coded:
                    k_j = jnp.concatenate([k_j, aug_k[ks, :]], axis=1)
                s = dot(k_j, q_a, ((1,), (1,)))
                if edge:
                    gap = iota((TK, TQ), 0) - iota((TK, TQ), 1)
                    s = jnp.where(gap <= i * TQ - j * TK, s, -1e30)
                new = jnp.maximum(top, jnp.max(s, axis=0, keepdims=True))
                p = jnp.exp2((s - new) * to_exp2)
                dp = dot(rows_ref[ks, 256:384], d_i, ((1,), (1,)))
                p_buf[ks, :] = p
                dp_buf[ks, :] = dp
                tops[pl.ds(pl.multiple_of(j * 8, 8), 8), :] = jnp.broadcast_to(new, (8, TQ))
                keep = jnp.exp2((top - new) * to_exp2)
                return (
                    new,
                    total * keep + jnp.sum(p, axis=0, keepdims=True),
                    delta * keep + jnp.sum(p * dp, axis=0, keepdims=True),
                )

            none = jnp.zeros((1, TQ), F32)
            sums = (jnp.full((1, TQ), -1e30, F32), none, none)
            sums = lax.fori_loop(0, full_tiles, lambda j, a: weigh(j, a, False), sums)
            top, total, delta = weigh(full_tiles, sums, True)
            inv = 1.0 / total
            delta = delta * inv
            acc_o[...] = jnp.zeros_like(acc_o)
            acc_q[...] = jnp.zeros_like(acc_q)

            def spread(j, _):
                ks = pl.ds(pl.multiple_of(j * TK, TK), TK)
                here = tops[pl.ds(pl.multiple_of(j * 8, 8), 8), :][:1]
                w = p_buf[ks, :] * (jnp.exp2((here - top) * to_exp2) * inv)
                rounded = w.astype(BF16)
                ds = (w * (dp_buf[ks, :] - delta)).astype(BF16)
                acc_o[...] += dot(vt[:, ks], rounded)
                acc_q[...] += dot(kt[:, ks], ds)
                dv[ks, :] += dot(rounded, d_i)
                dk[ks, :] += dot(ds, q_i)
                return 0

            lax.fori_loop(0, full_tiles + 1, spread, 0)
            rows_ref[qs, 0:128] = acc_o[...].T.astype(BF16)
            rows_ref[qs, 384:512] = (acc_q[...] * scale).T.astype(BF16)
            return 0

        def ready(j, _):
            ks = pl.ds(pl.multiple_of(j * TK, TK), TK)
            kt[:, ks] = rows_ref[ks, 128:256].astype(F32).T.astype(BF16)
            vt[:, ks] = rows_ref[ks, 256:384].astype(F32).T.astype(BF16)
            dk[ks, :] = jnp.zeros((TK, 128), F32)
            dv[ks, :] = jnp.zeros((TK, 128), F32)
            return 0

        lax.fori_loop(0, span // TK, ready, 0)
        lax.fori_loop(0, span // TQ, body, 0)

        def finish(j, _):
            ks = pl.ds(pl.multiple_of(j * TK, TK), TK)
            rows_ref[ks, 128:256] = (dk[ks, :] * scale).astype(BF16)
            rows_ref[ks, 256:384] = dv[ks, :].astype(BF16)
            return 0

        lax.fori_loop(0, span // TK, finish, 0)

    def codes(g):
        def body(s, _):
            note = meta_in[pl.ds(pl.multiple_of(s * 16, 16), 16), :].astype(F32)
            r = iota((ROWS, 128), 0).astype(F32)
            inside = (r >= note[2 * g : 2 * g + 1]) & (r < note[2 * g + 1 : 2 * g + 2])
            known = iota((ROWS, 128), 1) <= 4
            at = pl.ds(pl.multiple_of(s * ROWS, ROWS), ROWS)
            aug_q[at, :] = jnp.where(inside, 1.0, 0.0).astype(BF16)
            aug_k[at, :] = jnp.where(known & ~inside, -FAR, 0.0).astype(BF16)
            return 0

        lax.fori_loop(0, PEERS, body, 0)

    def hot_work(g):
        for h in (2 * g, 2 * g + 1):

            @pl.when(me == HOT_AT[h])
            def _():
                hot_arrive(h)
                attend(recv_hot, HOT_ROWS, False, lambda i: None)
                back_start(h)

    def work(g, between):
        def load(yy, _):
            at = pl.ds(pl.multiple_of(yy * 768, 768), 768)
            rows_buf[at, :] = recv[g, yy].reshape(768, 512)
            return 0

        def store(yy, _):
            at = pl.ds(pl.multiple_of(yy * 768, 768), 768)
            recv[g, yy] = rows_buf[at, :].reshape(4, 2, ROWS, 512)
            return 0

        lax.fori_loop(0, 4, load, 0)
        attend(rows_buf, SPAN, True, between)
        lax.fori_loop(0, 4, store, 0)

    def at_block(index, act):
        def between(i):
            @pl.when(i == index)
            def _():
                act()

        return between

    pack(0)
    start_one(0)
    pack(1)
    start_two(0)
    start_one(1)

    for k in range(1, PEERS):
        meta_copy(k).wait()
    noted = meta_in[...].astype(F32)
    noted = jnp.where(lax.rem(iota((512, 128), 0), 16) == 4, noted, 0.0)
    flags[0] = jnp.broadcast_to(jnp.max(noted, axis=0, keepdims=True), (16, 128)).astype(BF16)

    def flag_copy(step):
        return pltpu.make_async_remote_copy(
            src_ref=flags.at[0],
            dst_ref=flags.at[step],
            send_sem=flag_ssem.at[step],
            recv_sem=flag_rsem.at[step],
            device_id={"head": lax.rem(col + step, 4)},
            device_id_type=MESH,
        )

    for step in (1, 2, 3):
        flag_copy(step).start()

    codes(0)
    arrive(0)
    drain(0)
    work(0, at_block(SWITCH, lambda: start_two(1)))
    start_one(2)
    hot_work(0)
    codes(1)
    arrive(1)
    drain(1)
    work(1, at_block(SWITCH, lambda: start_two(2)))
    start_one(3)
    hot_work(1)
    arrive(2)
    start_two(3)
    back_arrive(0)
    unpack(0)
    for step in (1, 2, 3):
        flag_copy(step).wait()
    any_flag = jnp.maximum(
        jnp.maximum(flags[0].astype(F32), flags[1].astype(F32)),
        jnp.maximum(flags[2].astype(F32), flags[3].astype(F32)),
    )
    flag_out[...] = any_flag[:8]
    drain(2)
    back_drain(0)
    arrive(3)
    back_arrive(1)
    unpack(1)
    drain(3)
    back_drain(1)


def settle_kernel(x, o_q, o_k, o_v, o_d, wide):
    for a, ref in ((0, o_q), (3, o_k), (1, o_v), (2, o_d)):
        for h in range(4):
            wide[pl.ds(h, 128, stride=4), :] = x[h, :, a * 128 : a * 128 + 128].astype(F32)
        ref[...] = wide[...].astype(BF16)


def settle(x):
    outs = pl.pallas_call(
        settle_kernel,
        grid=(8,),
        out_shape=[jax.ShapeDtypeStruct((4096, 128), BF16)] * 4,
        in_specs=[pl.BlockSpec((4, 128, 512), lambda i: (0, i, 0))],
        out_specs=[pl.BlockSpec((512, 128), lambda i: (i, 0))] * 4,
        scratch_shapes=[pltpu.VMEM((512, 128), F32)],
        name="settle",
    )(x)
    return tuple(a.reshape(1024, 4, 128) for a in outs)


def quick(queries, key_rows, value_rows, out_grad, bucket_id):
    rows = [a.reshape(4096, 128) for a in (queries, key_rows, value_rows, out_grad)]
    vmem = pl.BlockSpec(memory_space=pltpu.VMEM)
    dma = pltpu.SemaphoreType.DMA
    outs = pl.pallas_call(
        kernel,
        out_shape=[
            jax.ShapeDtypeStruct((4, 1024, 512), BF16),
            jax.ShapeDtypeStruct((8, 128), F32),
        ],
        in_specs=[vmem] * 5,
        out_specs=[vmem] * 2,
        scratch_shapes=[
            pltpu.VMEM((4096, 128), F32),
            pltpu.VMEM((2, 4, 4, 2, ROWS, 512), BF16),
            pltpu.VMEM((2, 64, 512), BF16),
            pltpu.VMEM((2, 4, 4, 2, ROWS, 512), BF16),
            pltpu.VMEM((HOT_ROWS, 512), BF16),
            pltpu.VMEM((2, 4, 4, 2, ROWS, 512), BF16),
            pltpu.VMEM((2, 64, 512), BF16),
            pltpu.VMEM((2, 2, 4, 4, 2, HALF, 512), BF16),
            pltpu.VMEM((SPAN, 512), BF16),
            pltpu.VMEM((512, 128), BF16),
            pltpu.VMEM((512, 128), BF16),
            pltpu.VMEM((4, 16, 128), BF16),
            pltpu.VMEM((8, 1024), I32),
            pltpu.VMEM((1024, 128), I32),
            pltpu.VMEM((SPAN, 128), BF16),
            pltpu.VMEM((SPAN, 128), BF16),
            pltpu.VMEM((128, SPAN), BF16),
            pltpu.VMEM((128, SPAN), BF16),
            pltpu.VMEM((SPAN, 128), F32),
            pltpu.VMEM((SPAN, 128), F32),
            pltpu.VMEM((SPAN, TQ), F32),
            pltpu.VMEM((SPAN, TQ), F32),
            pltpu.VMEM((SPAN // TK * 8, TQ), F32),
            pltpu.VMEM((128, TQ), F32),
            pltpu.VMEM((128, TQ), F32),
            dma((4, 2, 4)), dma((4, 2, 4)), dma((4, 2, 8)), dma((4, 2, 8)), dma((4, 2, 2)),
            pltpu.SemaphoreType.REGULAR((2,)), dma((PEERS,)), dma((PEERS,)),
            dma((4,)), dma((PEERS,)), dma((PEERS,)), dma((4,)), dma((4,)), dma((4,)),
        ],
        compiler_params=pltpu.CompilerParams(
            collective_id=0, has_side_effects=True, vmem_limit_bytes=60 * 2**20
        ),
        name="bucket_layer",
    )(*rows, bucket_id.T)
    return outs[0], outs[1][0, 0] > 0


def bucket_weights(q_part, k_part, valid, scale):
    span = q_part.shape[0]
    sorted_index = jnp.arange(span, dtype=I32)
    allowed = (sorted_index[None, :] <= sorted_index[:, None]) & (
        (valid[None, :] > 0) | (sorted_index[None, :] == sorted_index[:, None])
    )
    scores = jnp.dot(q_part, k_part.T, preferred_element_type=F32) * scale
    scores = jnp.where(allowed, scores, F32(-1e30))
    top = jnp.max(scores, axis=1, keepdims=True)
    expd = jnp.where(allowed, jnp.exp(scores - top), F32(0.0))
    return expd / jnp.sum(expd, axis=1, keepdims=True)


def bucket_forward(block, valid, width):
    scale = 1.0 / math.sqrt(width)
    weights = bucket_weights(block[:, :width], block[:, width : 2 * width], valid, scale)
    rounded = weights.astype(BF16)
    return jnp.dot(rounded, block[:, 2 * width :], preferred_element_type=F32).astype(
        BF16
    )


def bucket_backward(block, d_part, valid, width):
    scale = 1.0 / math.sqrt(width)
    q_part = block[:, :width]
    k_part = block[:, width : 2 * width]
    v_part = block[:, 2 * width : 3 * width]
    weights = bucket_weights(q_part, k_part, valid, scale)
    rounded = weights.astype(BF16)
    dprob = jnp.dot(d_part, v_part.T, preferred_element_type=F32)
    delta = jnp.sum(weights * dprob, axis=1, keepdims=True)
    dscore = (weights * (dprob - delta)).astype(BF16)
    grad_q = (jnp.dot(dscore, k_part, preferred_element_type=F32) * scale).astype(
        BF16
    )
    grad_k = (jnp.dot(dscore.T, q_part, preferred_element_type=F32) * scale).astype(
        BF16
    )
    grad_v = jnp.dot(rounded.T, d_part, preferred_element_type=F32).astype(BF16)
    return (rounded, v_part, grad_q, grad_k, grad_v)


def bucket_grads(block, d_part, valid, width):
    rounded, v_part, grad_q, grad_k, grad_v = bucket_backward(block, d_part, valid, width)
    return jnp.concatenate([grad_q, grad_k, grad_v], axis=1)


def slow(queries, key_rows, value_rows, out_grad, bucket_id, bucket_slot):
    peers = lax.axis_size("seq")
    tok_count, group, width = queries.shape
    per_owner = BUCKETS_PER_HEAD // peers
    span = peers * SLOTS_PER_SOURCE
    total = group * per_owner * span
    owner = bucket_id // per_owner
    local_bucket = bucket_id % per_owner
    head_index = jnp.arange(group, dtype=I32)[None, :]
    flat = (
        (head_index * per_owner + local_bucket) * span + owner * SLOTS_PER_SOURCE + bucket_slot
    ).reshape(-1)
    marks = (
        jnp.zeros((total,), BF16)
        .at[flat]
        .set(BF16(1.0))
        .reshape(group, per_owner, span)
    )

    def spread(rows):
        columns = rows.shape[-1]
        placed = jnp.zeros((total, columns), rows.dtype).at[flat].set(rows.reshape(-1, columns))
        return placed.reshape(group, per_owner, span, columns)

    def collect(buffer):
        columns = buffer.shape[-1]
        return buffer.reshape(total, columns)[flat].reshape(tok_count, group, columns)

    joined = jnp.concatenate([queries, key_rows, value_rows], axis=2)
    blocks, valid = (
        lax.all_to_all(spread(joined), "seq", split_axis=2, concat_axis=2, tiled=True),
        lax.all_to_all(marks, "seq", split_axis=2, concat_axis=2, tiled=True),
    )
    flat_blocks = blocks.reshape(-1, span, 3 * width)
    flat_valid = valid.reshape(-1, span)
    attended = lax.map(
        lambda item: bucket_forward(item[0], item[1], width), (flat_blocks, flat_valid)
    )
    attended = lax.all_to_all(
        attended.reshape(group, per_owner, span, width),
        "seq",
        split_axis=2,
        concat_axis=2,
        tiled=True,
    )
    incoming = lax.all_to_all(spread(out_grad), "seq", split_axis=2, concat_axis=2, tiled=True)
    grads = lax.map(
        lambda item: bucket_grads(item[0], item[1], item[2], width),
        (flat_blocks, incoming.reshape(-1, span, width), flat_valid),
    )
    grads = lax.all_to_all(
        grads.reshape(group, per_owner, span, 3 * width),
        "seq",
        split_axis=2,
        concat_axis=2,
        tiled=True,
    )
    gathered = collect(grads)
    return (
        collect(attended),
        gathered[:, :, :width],
        gathered[:, :, width : 2 * width],
        gathered[:, :, 2 * width :],
    )


def shards(queries, key_rows, value_rows, out_grad, bucket_id, bucket_slot):
    packed, crowded = quick(queries, key_rows, value_rows, out_grad, bucket_id)
    return lax.cond(
        crowded,
        lambda: slow(queries, key_rows, value_rows, out_grad, bucket_id, bucket_slot),
        lambda: settle(packed),
    )


def solution(mesh):
    in_specs = (
        P("seq", "head", None),
        P("seq", "head", None),
        P("seq", "head", None),
        P("seq", "head", None),
        P("seq", "head"),
        P("seq", "head"),
    )
    out_specs = (
        P("seq", "head", None),
        P("seq", "head", None),
        P("seq", "head", None),
        P("seq", "head", None),
    )
    return jax.shard_map(shards, mesh=mesh, in_specs=in_specs, out_specs=out_specs, check_vma=False)
```

```python
import functools
import math

import jax
import jax.numpy as jnp
from jax import lax
from jax.experimental import pallas as pl
from jax.experimental.pallas import tpu as pltpu
from jax.sharding import PartitionSpec as P

SLOTS_PER_SOURCE = 32
BUCKETS_PER_HEAD = 64
PEERS = 32
ROWS = 96
SPAN = PEERS * ROWS
HOT_ROWS = PEERS * SLOTS_PER_SOURCE
HOT_AT = (0, 10, 20, 30)
TQ, TK = 512, 512
HALF = ROWS // 2
WINDOWS = PEERS * 64
SECOND = ((2, 0), (2, 1), (1, 0), (3, 0), (1, 1), (3, 1), (0, 1))
SWITCH = (4, 4)
FAR = 2.0**100
MESH = pl.DeviceIdType.MESH
F32, BF16, I32 = jnp.float32, jnp.bfloat16, jnp.int32


def iota(shape, dim):
    return lax.broadcasted_iota(I32, shape, dim)


def dot(a, b, dims=((1,), (0,))):
    return lax.dot_general(a, b, (dims, ((), ())), preferred_element_type=F32)


def kernel(
    q_ref, k_ref, v_ref, d_ref, bid_ref,
    x, flag_out,
    send, send_hot, recv, recv_hot, ret, ret_hot, mid, rows_buf, meta, meta_in, flags,
    pos_row, pos_col, aug_q, aug_k, kt, vt, dkv, p_buf, dp_buf, tops, acc_o, acc_q,
    one_ssem, one_rsem, two_ssem, two_rsem, own_sem, free_sem, meta_ssem, meta_rsem,
    hot_ssem, hot_rsem, back_ssem, back_rsem, flag_ssem, flag_rsem, in_sem,
):
    me = lax.axis_index("seq")
    col = lax.axis_index("head")
    y, z, c = me // 8, lax.rem(me // 2, 4), lax.rem(me, 2)
    scale = 1.0 / math.sqrt(128)
    to_exp2 = scale * math.log2(math.e)

    def ya(d):
        return lax.rem(y + d, 4)

    def za(d):
        return lax.rem(z + d, 4)

    def dev(yy, zz, cc):
        return yy * 8 + zz * 2 + cc

    barrier = pltpu.get_barrier_semaphore()
    for k in range(1, PEERS):
        pl.semaphore_signal(
            barrier, inc=1, device_id={"seq": lax.rem(me + k, PEERS)}, device_id_type=MESH
        )
    for step in (1, 2, 3):
        pl.semaphore_signal(
            barrier, inc=1, device_id={"head": lax.rem(col + step, 4)}, device_id_type=MESH
        )

    inputs = (q_ref, k_ref, v_ref, d_ref)
    quarters = range(4)

    def load(a, part):
        return pltpu.make_async_copy(
            inputs[a].at[pl.ds(part * 1024, 1024)],
            rows_buf.at[pl.ds(a % 3 * 1024, 1024), pl.ds(part * 128, 128)],
            in_sem.at[a, part],
        )

    for a in range(3):
        for part in quarters:
            load(a, part).start()
    for a in range(4):
        for part in quarters:
            load(a, part).wait()
            dkv[part * 1024 : part * 1024 + 1024, :] = rows_buf[
                a % 3 * 1024 : a % 3 * 1024 + 1024, part * 128 : part * 128 + 128
            ].astype(F32)
        if a == 0:
            for part in quarters:
                load(3, part).start()
        for h in range(4):
            x[h, :, a * 128 : a * 128 + 128] = dkv[pl.ds(h, 1024, stride=4), :].astype(BF16)

    named = jnp.concatenate(
        [(iota((64, 1024), 0) == bid_ref[h : h + 1, :]).astype(F32) for h in range(4)], axis=0
    )
    named16 = named.astype(BF16)
    ranks = []
    for part in quarters:
        earlier = iota((1024, 256), 0) < iota((1024, 256), 1) + part * 256
        ranks.append(dot(named16, earlier.astype(F32).astype(BF16)))
    rank = jnp.concatenate(ranks, axis=1)
    count = jnp.sum(named, axis=1, keepdims=True)
    full = (count == 32.0).astype(F32)
    count = count * (1.0 - full)
    bad = jnp.float32(0.0)
    for h in range(4):
        n_full = jnp.sum(full[h * 64 : h * 64 + 64])
        bad = jnp.maximum(bad, (n_full != 1.0).astype(F32))
    r0, r1 = iota((256, 256), 0), iota((256, 256), 1)
    alike = r0 // 2 == r1 // 2
    lanes = jnp.broadcast_to(count, (256, 128))
    lanes16 = lanes.astype(BF16)
    start = dot((alike & (r1 < r0)).astype(F32).astype(BF16), lanes16)[:, :1]
    both = dot(alike.astype(F32).astype(BF16), lanes16)[:, :1]
    rows = iota((256, 1), 0)
    owner = lax.rem(rows, 64) // 2
    second = lax.rem(rows // 64, 2)
    inside = start + jnp.where(second == 1, ROWS - both, 0.0)
    at_hot = (second * 32).astype(F32)
    base = jnp.where(full > 0, SPAN + at_hot, (owner * ROWS).astype(F32) + inside)
    back = jnp.where(full > 0, WINDOWS + at_hot, (owner * 64 - second * 32).astype(F32) + inside)

    def per_head(table):
        landed = named * (rank + table)
        return jnp.concatenate(
            [jnp.sum(landed[h * 64 : h * 64 + 64], axis=0, keepdims=True) for h in range(4)],
            axis=0,
        )

    pos_row[0:4, :] = per_head(base).astype(I32)
    place = jnp.concatenate([per_head(back), jnp.zeros((124, 1024), F32)], axis=0)
    pos_col[...] = place.T.astype(I32)

    lane, r2 = iota((256, 128), 1), iota((256, 128), 0)
    code = lax.rem(r2 // 64, 2) * 2 + lax.rem(r2, 2)
    front, rear = code < 2, code >= 2
    low = (lane < 2) | (lane == 4)
    high = (lane == 2) | (lane == 3)
    w_start = jnp.where((low & front & (code < lane)) | (lane == 5), lanes, 0.0)
    w_start = w_start - jnp.where(high & rear & (code >= lane), lanes, 0.0)
    w_end = jnp.where((lane < 2) & front & (code <= lane), lanes, 0.0)
    w_end = w_end - jnp.where((high & (code > lane)) | (lane == 4) & rear, lanes, 0.0)
    mr, mc = iota((512, 256), 0), iota((512, 256), 1)
    mine = mr // 16 == lax.rem(mc, 64) // 2
    pick_start = (mine & (lax.rem(mr, 16) == mc // 128 * 2)).astype(F32).astype(BF16)
    pick_end = (mine & (lax.rem(mr, 16) == mc // 128 * 2 + 1)).astype(F32).astype(BF16)
    starts = dot(pick_start, w_start.astype(BF16))
    kind, ml = lax.rem(iota((512, 128), 0), 16), iota((512, 128), 1)
    bad = jnp.maximum(bad, (jnp.max(jnp.where(ml == 5, starts, 0.0)) > ROWS).astype(F32))
    high = (ml == 2) | (ml == 3)
    to_rows = ((kind == 0) | (kind == 2)) & high
    to_rows = to_rows | ((kind == 1) | (kind == 3)) & (high | (ml == 4))
    tail = jnp.where(to_rows, jnp.float32(ROWS), 0.0) + jnp.where(kind == 4, bad, 0.0)
    meta[...] = (starts + dot(pick_end, w_end.astype(BF16)) + tail).astype(BF16)

    def meta_copy(k):
        other = lax.rem(me + k, PEERS)
        return pltpu.make_async_remote_copy(
            src_ref=meta.at[pl.ds(pl.multiple_of(other * 16, 16), 16)],
            dst_ref=meta_in.at[pl.ds(pl.multiple_of(me * 16, 16), 16)],
            send_sem=meta_ssem.at[k],
            recv_sem=meta_rsem.at[k],
            device_id={"seq": other},
            device_id_type=MESH,
        )

    def ends(phase):
        return (send, recv) if phase < 2 else (recv, ret)

    def one(phase, half, d):
        g, src = phase % 2, ends(phase)[0]
        if half == 0:
            from_, to, other = src.at[g, ya(d), :, :, 0:HALF], mid.at[g, 0, y], dev(ya(d), z, c)
        else:
            from_, to, other = src.at[g, :, za(d), :, HALF:ROWS], mid.at[g, 1, z], dev(y, za(d), c)
        return pltpu.make_async_remote_copy(
            src_ref=from_,
            dst_ref=to,
            send_sem=one_ssem.at[phase, half, d],
            recv_sem=one_rsem.at[phase, half, d],
            device_id={"seq": other},
            device_id_type=MESH,
        )

    def one_own(phase, half):
        g, src = phase % 2, ends(phase)[0]
        sem = own_sem.at[phase, half, 0]
        if half == 0:
            return pltpu.make_async_copy(src.at[g, y, :, :, 0:HALF], mid.at[g, 0, y], sem)
        return pltpu.make_async_copy(src.at[g, :, z, :, HALF:ROWS], mid.at[g, 1, z], sem)

    def two(phase, half, d, e):
        g, dst = phase % 2, ends(phase)[1]
        cc = lax.rem(c + e, 2)
        if half == 0:
            from_, to = mid.at[g, 0, :, za(d), cc], dst.at[g, :, z, c, 0:HALF]
            other = dev(y, za(d), cc)
        else:
            from_, to = mid.at[g, 1, :, ya(d), cc], dst.at[g, y, :, c, HALF:ROWS]
            other = dev(ya(d), z, cc)
        return pltpu.make_async_remote_copy(
            src_ref=from_,
            dst_ref=to,
            send_sem=two_ssem.at[phase, half, d * 2 + e],
            recv_sem=two_rsem.at[phase, half, d * 2 + e],
            device_id={"seq": other},
            device_id_type=MESH,
        )

    def two_own(phase, half):
        g, dst = phase % 2, ends(phase)[1]
        sem = own_sem.at[phase, half, 1]
        if half == 0:
            return pltpu.make_async_copy(mid.at[g, 0, :, z, c], dst.at[g, :, z, c, 0:HALF], sem)
        return pltpu.make_async_copy(mid.at[g, 1, :, y, c], dst.at[g, y, :, c, HALF:ROWS], sem)

    def hot_copy(h):
        return pltpu.make_async_remote_copy(
            src_ref=send_hot.at[h // 2, pl.ds(h % 2 * 32, 32)],
            dst_ref=recv_hot.at[pl.ds(pl.multiple_of(me * 32, 32), 32)],
            send_sem=hot_ssem.at[h],
            recv_sem=hot_rsem.at[me],
            device_id={"seq": HOT_AT[h]},
            device_id_type=MESH,
        )

    def hot_from(h, s):
        return pltpu.make_async_remote_copy(
            src_ref=send_hot.at[h // 2, pl.ds(h % 2 * 32, 32)],
            dst_ref=recv_hot.at[pl.ds(s * 32, 32)],
            send_sem=hot_ssem.at[h],
            recv_sem=hot_rsem.at[s],
            device_id={"seq": HOT_AT[h]},
            device_id_type=MESH,
        )

    def hot_own(h):
        return pltpu.make_async_copy(
            send_hot.at[h // 2, pl.ds(h % 2 * 32, 32)],
            recv_hot.at[pl.ds(HOT_AT[h] * 32, 32)],
            hot_ssem.at[h],
        )

    def back_copy(h, s):
        return pltpu.make_async_remote_copy(
            src_ref=recv_hot.at[pl.ds(s * 32, 32)],
            dst_ref=ret_hot.at[h // 2, pl.ds(h % 2 * 32, 32)],
            send_sem=back_ssem.at[s],
            recv_sem=back_rsem.at[h],
            device_id={"seq": s},
            device_id_type=MESH,
        )

    def back_own(h):
        return pltpu.make_async_copy(
            recv_hot.at[pl.ds(HOT_AT[h] * 32, 32)],
            ret_hot.at[h // 2, pl.ds(h % 2 * 32, 32)],
            back_rsem.at[h],
        )

    def start_one(phase):
        if phase >= 2:
            pl.semaphore_wait(free_sem.at[phase % 2], 6)
        for d in (2, 1, 3):
            for half in (0, 1):
                one(phase, half, d).start()
        for half in (0, 1):
            one_own(phase, half).start()

    def hot_start(g):
        for h in (2 * g, 2 * g + 1):

            @pl.when(me != HOT_AT[h])
            def _():
                hot_copy(h).start()

            @pl.when(me == HOT_AT[h])
            def _():
                hot_own(h).start()

    def start_two(phase):
        for half in (0, 1):
            for d in (1, 2, 3):
                one(phase, half, d).wait_recv()
            one_own(phase, half).wait()
            for d, e in SECOND:
                two(phase, half, d, e).start()
            two_own(phase, half).start()

    def arrive(phase):
        for half in (0, 1):
            for d, e in SECOND:
                two(phase, half, d, e).wait_recv()
            two_own(phase, half).wait()

    def drain(phase):
        for half in (0, 1):
            for d in (1, 2, 3):
                one(phase, half, d).wait_send()
            for d, e in SECOND:
                two(phase, half, d, e).wait_send()
        if phase < 2:
            g = phase % 2
            for d in (1, 2, 3):
                for other in (dev(ya(d), z, c), dev(y, za(d), c)):
                    pl.semaphore_signal(
                        free_sem.at[g], inc=1, device_id={"seq": other}, device_id_type=MESH
                    )
            for h in (2 * g, 2 * g + 1):

                @pl.when(me != HOT_AT[h])
                def _():
                    hot_copy(h).wait_send()

    def back_start(h):
        for s in range(PEERS):
            if s != HOT_AT[h]:
                back_copy(h, s).start()
        back_own(h).start()

    def back_drain(g):
        for h in (2 * g, 2 * g + 1):

            @pl.when(me == HOT_AT[h])
            def _():
                for s in range(PEERS):
                    if s != HOT_AT[h]:
                        back_copy(h, s).wait_send()

    def hot_arrive(h):
        for s in range(PEERS):
            if s != HOT_AT[h]:
                hot_from(h, s).wait_recv()
        hot_own(h).wait()

    def back_arrive(g):
        for h in (2 * g, 2 * g + 1):

            @pl.when(me != HOT_AT[h])
            def _():
                back_copy(h, 0).wait_recv()

            @pl.when(me == HOT_AT[h])
            def _():
                back_own(h).wait()

    def picked(shape, at, first):
        index = iota(shape, 0)
        return (index // 32 * ROWS + lax.rem(index, 32) == at - first).astype(F32).astype(BF16)

    def pack(g):
        a, b = pos_row[2 * g : 2 * g + 1, :], pos_row[2 * g + 1 : 2 * g + 2, :]

        def body(m, _):
            first = m * 16 * ROWS
            two_y = pl.ds(m * 2, 2)
            shape = (2, 4, 2, 32, 512)
            p = picked((512, 1024), a, first)
            send[g, two_y, :, :, 0:32, :] = dot(p, x[2 * g]).astype(BF16).reshape(shape)
            p = picked((512, 1024), b, first + 64)
            send[g, two_y, :, :, 64:96, :] = dot(p, x[2 * g + 1]).astype(BF16).reshape(shape)
            p = picked((512, 1024), a, first + 32)
            t = dot(p, x[2 * g])
            p = picked((512, 1024), b, first + 32)
            t = t + dot(p, x[2 * g + 1])
            send[g, two_y, :, :, 32:64, :] = t.astype(BF16).reshape(shape)
            return 0

        lax.fori_loop(0, 2, body, 0)
        for k, at in ((0, a), (1, b)):
            pick = (iota((32, 1024), 0) + (SPAN + k * 32) == at).astype(F32).astype(BF16)
            send_hot[g, k * 32 : k * 32 + 32] = dot(pick, x[2 * g + k]).astype(BF16)

    def unpack(g):
        def body(m, _):
            t = pl.ds(pl.multiple_of(m * 512, 512), 512)
            for k in (0, 1):
                at = pos_col[t, 2 * g + k : 2 * g + k + 1]
                pick = (iota((512, WINDOWS), 1) == at).astype(F32).astype(BF16)
                hot_pick = (iota((512, 64), 1) + WINDOWS == at).astype(F32).astype(BF16)
                got = ret[g, :, :, :, k * 32 : k * 32 + 64, :].reshape(WINDOWS, 512)
                x[2 * g + k, t, :] = (dot(pick, got) + dot(hot_pick, ret_hot[g])).astype(BF16)
            return 0

        lax.fori_loop(0, 2, body, 0)

    def attend(rows_ref, span, coded, between):
        def after(j):
            return pl.ds(pl.multiple_of(SPAN + j * TK, TK), TK)

        def body(i, _):
            between(i)
            qs = pl.ds(pl.multiple_of(i * TQ, TQ), TQ)
            q_i = rows_ref[qs, 0:128]
            d_i = rows_ref[qs, 384:512]
            q_a = jnp.concatenate([q_i, aug_q[qs, :]], axis=1) if coded else q_i
            full_tiles = (i * TQ) // TK

            def weigh(j, sums, edge):
                top, total, delta = sums
                ks = pl.ds(pl.multiple_of(j * TK, TK), TK)
                k_j = rows_ref[ks, 128:256]
                if coded:
                    k_j = jnp.concatenate([k_j, aug_k[ks, :]], axis=1)
                s = dot(k_j, q_a, ((1,), (1,)))
                if edge:
                    gap = iota((TK, TQ), 0) - iota((TK, TQ), 1)
                    s = jnp.where(gap <= i * TQ - j * TK, s, -1e30)
                new = jnp.maximum(top, jnp.max(s, axis=0, keepdims=True))
                p = jnp.exp2((s - new) * to_exp2)
                dp = dot(rows_ref[ks, 256:384], d_i, ((1,), (1,)))
                p_buf[ks, :] = p
                dp_buf[ks, :] = dp
                tops[pl.ds(pl.multiple_of(j * 8, 8), 8), :] = jnp.broadcast_to(new, (8, TQ))
                keep = jnp.exp2((top - new) * to_exp2)
                return (
                    new,
                    total * keep + jnp.sum(p, axis=0, keepdims=True),
                    delta * keep + jnp.sum(p * dp, axis=0, keepdims=True),
                )

            none = jnp.zeros((1, TQ), F32)
            sums = (jnp.full((1, TQ), -1e30, F32), none, none)
            sums = lax.fori_loop(0, full_tiles, lambda j, a: weigh(j, a, False), sums)
            top, total, delta = weigh(full_tiles, sums, True)
            inv = 1.0 / total
            delta = delta * inv
            acc_o[...] = jnp.zeros_like(acc_o)
            acc_q[...] = jnp.zeros_like(acc_q)

            def spread(j, _):
                ks = pl.ds(pl.multiple_of(j * TK, TK), TK)
                here = tops[pl.ds(pl.multiple_of(j * 8, 8), 8), :][:1]
                w = p_buf[ks, :] * (jnp.exp2((here - top) * to_exp2) * inv)
                rounded = w.astype(BF16)
                ds = (w * (dp_buf[ks, :] - delta)).astype(BF16)
                acc_o[...] += dot(vt[:, ks], rounded)
                acc_q[...] += dot(kt[:, ks], ds)
                dkv[ks, :] += dot(ds, q_i)
                dkv[after(j), :] += dot(rounded, d_i)
                return 0

            lax.fori_loop(0, full_tiles + 1, spread, 0)
            rows_ref[qs, 0:128] = acc_o[...].T.astype(BF16)
            rows_ref[qs, 384:512] = (acc_q[...] * scale).T.astype(BF16)
            return 0

        def ready(j, _):
            ks = pl.ds(pl.multiple_of(j * TK, TK), TK)
            kt[:, ks] = rows_ref[ks, 128:256].astype(F32).T.astype(BF16)
            vt[:, ks] = rows_ref[ks, 256:384].astype(F32).T.astype(BF16)
            dkv[ks, :] = jnp.zeros((TK, 128), F32)
            dkv[after(j), :] = jnp.zeros((TK, 128), F32)
            return 0

        lax.fori_loop(0, span // TK, ready, 0)
        lax.fori_loop(0, span // TQ, body, 0)

        def finish(j, _):
            ks = pl.ds(pl.multiple_of(j * TK, TK), TK)
            rows_ref[ks, 128:256] = (dkv[ks, :] * scale).astype(BF16)
            rows_ref[ks, 256:384] = dkv[after(j), :].astype(BF16)
            return 0

        lax.fori_loop(0, span // TK, finish, 0)

    def codes(g):
        def body(s, _):
            note = meta_in[pl.ds(pl.multiple_of(s * 16, 16), 16), :].astype(F32)
            r = iota((ROWS, 128), 0).astype(F32)
            inside = (r >= note[2 * g : 2 * g + 1]) & (r < note[2 * g + 1 : 2 * g + 2])
            known = iota((ROWS, 128), 1) <= 4
            at = pl.ds(pl.multiple_of(s * ROWS, ROWS), ROWS)
            aug_q[at, :] = jnp.where(inside, 1.0, 0.0).astype(BF16)
            aug_k[at, :] = jnp.where(known & ~inside, -FAR, 0.0).astype(BF16)
            return 0

        lax.fori_loop(0, PEERS, body, 0)

    def hot_work():
        for h in range(4):

            @pl.when(me == HOT_AT[h])
            def _():
                hot_arrive(h)

        @pl.when((me == HOT_AT[0]) | (me == HOT_AT[1]) | (me == HOT_AT[2]) | (me == HOT_AT[3]))
        def _():
            attend(recv_hot, HOT_ROWS, False, lambda i: None)

        for h in range(4):

            @pl.when(me == HOT_AT[h])
            def _():
                back_start(h)

    def work(g, between):
        def load(yy, _):
            at = pl.ds(pl.multiple_of(yy * 768, 768), 768)
            rows_buf[at, :] = recv[g, yy].reshape(768, 512)
            return 0

        def store(yy, _):
            at = pl.ds(pl.multiple_of(yy * 768, 768), 768)
            recv[g, yy] = rows_buf[at, :].reshape(4, 2, ROWS, 512)
            return 0

        lax.fori_loop(0, 4, load, 0)
        attend(rows_buf, SPAN, True, between)
        lax.fori_loop(0, 4, store, 0)

    def at_block(index, act):
        def between(i):
            @pl.when(i == index)
            def _():
                act()

        return between

    pack(0)
    pl.semaphore_wait(barrier, PEERS - 1 + 3)
    start_one(0)
    hot_start(0)
    for k in range(1, PEERS):
        meta_copy(k).start()
    own_meta = pl.ds(pl.multiple_of(me * 16, 16), 16)
    meta_in[own_meta, :] = meta[own_meta, :]
    pack(1)
    hot_start(1)
    start_two(0)

    for k in range(1, PEERS):
        meta_copy(k).wait()
    noted = meta_in[...].astype(F32)
    noted = jnp.where(lax.rem(iota((512, 128), 0), 16) == 4, noted, 0.0)
    flags[0] = jnp.broadcast_to(jnp.max(noted, axis=0, keepdims=True), (16, 128)).astype(BF16)

    def flag_copy(step):
        return pltpu.make_async_remote_copy(
            src_ref=flags.at[0],
            dst_ref=flags.at[step],
            send_sem=flag_ssem.at[step],
            recv_sem=flag_rsem.at[step],
            device_id={"head": lax.rem(col + step, 4)},
            device_id_type=MESH,
        )

    for step in (1, 2, 3):
        flag_copy(step).start()

    codes(0)
    hot_work()
    arrive(0)
    start_one(1)
    drain(0)
    work(0, at_block(SWITCH[0], lambda: start_two(1)))
    start_one(2)
    codes(1)
    arrive(1)
    drain(1)
    work(1, at_block(SWITCH[1], lambda: start_two(2)))
    start_one(3)
    arrive(2)
    back_arrive(0)
    unpack(0)
    start_two(3)
    for step in (1, 2, 3):
        flag_copy(step).wait()
    any_flag = jnp.maximum(
        jnp.maximum(flags[0].astype(F32), flags[1].astype(F32)),
        jnp.maximum(flags[2].astype(F32), flags[3].astype(F32)),
    )
    flag_out[...] = any_flag[:8]
    drain(2)
    back_drain(0)
    arrive(3)
    back_arrive(1)
    unpack(1)
    drain(3)
    back_drain(1)


def settle_kernel(x, o_q, o_k, o_v, o_d, held, wide, done, in_sem, out_sem):
    def load(m):
        return pltpu.make_async_copy(x.at[:, pl.ds(m * 256, 256)], held.at[m], in_sem.at[m])

    outs = ((0, o_q), (3, o_k), (1, o_v), (2, o_d))

    def save(m, n):
        at = pl.ds(m * 1024, 1024)
        return pltpu.make_async_copy(done.at[n, at], outs[n][1].at[at], out_sem.at[m, n])

    for m in range(4):
        load(m).start()
    for m in range(4):
        load(m).wait()
        for n, (a, _) in enumerate(outs):
            for h in range(4):
                wide[n, pl.ds(h, 256, stride=4), :] = held[m, h, :, a * 128 : a * 128 + 128].astype(
                    F32
                )
            done[n, m * 1024 : m * 1024 + 1024, :] = wide[n].astype(BF16)
            save(m, n).start()
    for m in range(4):
        for n in range(4):
            save(m, n).wait()


def settle(x):
    outs = pl.pallas_call(
        settle_kernel,
        out_shape=[jax.ShapeDtypeStruct((4096, 128), BF16)] * 4,
        in_specs=[pl.BlockSpec(memory_space=pl.ANY)],
        out_specs=[pl.BlockSpec(memory_space=pl.ANY)] * 4,
        scratch_shapes=[
            pltpu.VMEM((4, 4, 256, 512), BF16),
            pltpu.VMEM((4, 1024, 128), F32),
            pltpu.VMEM((4, 4096, 128), BF16),
            pltpu.SemaphoreType.DMA((4,)),
            pltpu.SemaphoreType.DMA((4, 4)),
        ],
        compiler_params=pltpu.CompilerParams(vmem_limit_bytes=32 * 2**20),
        name="settle",
    )(x)
    return tuple(a.reshape(1024, 4, 128) for a in outs)


def quick(queries, key_rows, value_rows, out_grad, bucket_id):
    rows = [a.reshape(4096, 128) for a in (queries, key_rows, value_rows, out_grad)]
    vmem = pl.BlockSpec(memory_space=pltpu.VMEM)
    dma = pltpu.SemaphoreType.DMA
    outs = pl.pallas_call(
        kernel,
        out_shape=[
            jax.ShapeDtypeStruct((4, 1024, 512), BF16),
            jax.ShapeDtypeStruct((8, 128), F32),
        ],
        in_specs=[pl.BlockSpec(memory_space=pl.ANY)] * 4 + [vmem],
        out_specs=[vmem] * 2,
        scratch_shapes=[
            pltpu.VMEM((2, 4, 4, 2, ROWS, 512), BF16),
            pltpu.VMEM((2, 64, 512), BF16),
            pltpu.VMEM((2, 4, 4, 2, ROWS, 512), BF16),
            pltpu.VMEM((HOT_ROWS, 512), BF16),
            pltpu.VMEM((2, 4, 4, 2, ROWS, 512), BF16),
            pltpu.VMEM((2, 64, 512), BF16),
            pltpu.VMEM((2, 2, 4, 4, 2, HALF, 512), BF16),
            pltpu.VMEM((SPAN, 512), BF16),
            pltpu.VMEM((512, 128), BF16),
            pltpu.VMEM((512, 128), BF16),
            pltpu.VMEM((4, 16, 128), BF16),
            pltpu.VMEM((8, 1024), I32),
            pltpu.VMEM((1024, 128), I32),
            pltpu.VMEM((SPAN, 128), BF16),
            pltpu.VMEM((SPAN, 128), BF16),
            pltpu.VMEM((128, SPAN), BF16),
            pltpu.VMEM((128, SPAN), BF16),
            pltpu.VMEM((2 * SPAN, 128), F32),
            pltpu.VMEM((SPAN, TQ), F32),
            pltpu.VMEM((SPAN, TQ), F32),
            pltpu.VMEM((SPAN // TK * 8, TQ), F32),
            pltpu.VMEM((128, TQ), F32),
            pltpu.VMEM((128, TQ), F32),
            dma((4, 2, 4)), dma((4, 2, 4)), dma((4, 2, 8)), dma((4, 2, 8)), dma((4, 2, 2)),
            pltpu.SemaphoreType.REGULAR((2,)), dma((PEERS,)), dma((PEERS,)),
            dma((4,)), dma((PEERS,)), dma((PEERS,)), dma((4,)), dma((4,)), dma((4,)),
            dma((4, 4)),
        ],
        compiler_params=pltpu.CompilerParams(
            collective_id=0, has_side_effects=True, vmem_limit_bytes=60 * 2**20
        ),
        name="bucket_layer",
    )(*rows, bucket_id.T)
    return outs[0], outs[1][0, 0] > 0


def bucket_weights(q_part, k_part, valid, scale):
    span = q_part.shape[0]
    sorted_index = jnp.arange(span, dtype=I32)
    allowed = (sorted_index[None, :] <= sorted_index[:, None]) & (
        (valid[None, :] > 0) | (sorted_index[None, :] == sorted_index[:, None])
    )
    scores = jnp.dot(q_part, k_part.T, preferred_element_type=F32) * scale
    scores = jnp.where(allowed, scores, F32(-1e30))
    top = jnp.max(scores, axis=1, keepdims=True)
    expd = jnp.where(allowed, jnp.exp(scores - top), F32(0.0))
    return expd / jnp.sum(expd, axis=1, keepdims=True)


def bucket_forward(block, valid, width):
    scale = 1.0 / math.sqrt(width)
    weights = bucket_weights(block[:, :width], block[:, width : 2 * width], valid, scale)
    rounded = weights.astype(BF16)
    return jnp.dot(rounded, block[:, 2 * width :], preferred_element_type=F32).astype(
        BF16
    )


def bucket_backward(block, d_part, valid, width):
    scale = 1.0 / math.sqrt(width)
    q_part = block[:, :width]
    k_part = block[:, width : 2 * width]
    v_part = block[:, 2 * width : 3 * width]
    weights = bucket_weights(q_part, k_part, valid, scale)
    rounded = weights.astype(BF16)
    dprob = jnp.dot(d_part, v_part.T, preferred_element_type=F32)
    delta = jnp.sum(weights * dprob, axis=1, keepdims=True)
    dscore = (weights * (dprob - delta)).astype(BF16)
    grad_q = (jnp.dot(dscore, k_part, preferred_element_type=F32) * scale).astype(
        BF16
    )
    grad_k = (jnp.dot(dscore.T, q_part, preferred_element_type=F32) * scale).astype(
        BF16
    )
    grad_v = jnp.dot(rounded.T, d_part, preferred_element_type=F32).astype(BF16)
    return (rounded, v_part, grad_q, grad_k, grad_v)


def bucket_grads(block, d_part, valid, width):
    rounded, v_part, grad_q, grad_k, grad_v = bucket_backward(block, d_part, valid, width)
    return jnp.concatenate([grad_q, grad_k, grad_v], axis=1)


def slow(queries, key_rows, value_rows, out_grad, bucket_id, bucket_slot):
    peers = lax.axis_size("seq")
    tok_count, group, width = queries.shape
    per_owner = BUCKETS_PER_HEAD // peers
    span = peers * SLOTS_PER_SOURCE
    total = group * per_owner * span
    owner = bucket_id // per_owner
    local_bucket = bucket_id % per_owner
    head_index = jnp.arange(group, dtype=I32)[None, :]
    flat = (
        (head_index * per_owner + local_bucket) * span + owner * SLOTS_PER_SOURCE + bucket_slot
    ).reshape(-1)
    marks = (
        jnp.zeros((total,), BF16)
        .at[flat]
        .set(BF16(1.0))
        .reshape(group, per_owner, span)
    )

    def spread(rows):
        columns = rows.shape[-1]
        placed = jnp.zeros((total, columns), rows.dtype).at[flat].set(rows.reshape(-1, columns))
        return placed.reshape(group, per_owner, span, columns)

    def collect(buffer):
        columns = buffer.shape[-1]
        return buffer.reshape(total, columns)[flat].reshape(tok_count, group, columns)

    joined = jnp.concatenate([queries, key_rows, value_rows], axis=2)
    blocks, valid = (
        lax.all_to_all(spread(joined), "seq", split_axis=2, concat_axis=2, tiled=True),
        lax.all_to_all(marks, "seq", split_axis=2, concat_axis=2, tiled=True),
    )
    flat_blocks = blocks.reshape(-1, span, 3 * width)
    flat_valid = valid.reshape(-1, span)
    attended = lax.map(
        lambda item: bucket_forward(item[0], item[1], width), (flat_blocks, flat_valid)
    )
    attended = lax.all_to_all(
        attended.reshape(group, per_owner, span, width),
        "seq",
        split_axis=2,
        concat_axis=2,
        tiled=True,
    )
    incoming = lax.all_to_all(spread(out_grad), "seq", split_axis=2, concat_axis=2, tiled=True)
    grads = lax.map(
        lambda item: bucket_grads(item[0], item[1], item[2], width),
        (flat_blocks, incoming.reshape(-1, span, width), flat_valid),
    )
    grads = lax.all_to_all(
        grads.reshape(group, per_owner, span, 3 * width),
        "seq",
        split_axis=2,
        concat_axis=2,
        tiled=True,
    )
    gathered = collect(grads)
    return (
        collect(attended),
        gathered[:, :, :width],
        gathered[:, :, width : 2 * width],
        gathered[:, :, 2 * width :],
    )


def shards(queries, key_rows, value_rows, out_grad, bucket_id, bucket_slot):
    packed, crowded = quick(queries, key_rows, value_rows, out_grad, bucket_id)
    return lax.cond(
        crowded,
        lambda: slow(queries, key_rows, value_rows, out_grad, bucket_id, bucket_slot),
        lambda: settle(packed),
    )


def solution(mesh):
    in_specs = (
        P("seq", "head", None),
        P("seq", "head", None),
        P("seq", "head", None),
        P("seq", "head", None),
        P("seq", "head"),
        P("seq", "head"),
    )
    out_specs = (
        P("seq", "head", None),
        P("seq", "head", None),
        P("seq", "head", None),
        P("seq", "head", None),
    )
    return jax.shard_map(shards, mesh=mesh, in_specs=in_specs, out_specs=out_specs, check_vma=False)
```

```python
import functools
import math

import jax
import jax.numpy as jnp
from jax import lax
from jax.experimental import pallas as pl
from jax.experimental.pallas import tpu as pltpu
from jax.sharding import PartitionSpec as P

SLOTS_PER_SOURCE = 32
BUCKETS_PER_HEAD = 64
PEERS = 32
ROWS = 96
SPAN = PEERS * ROWS
HOT_ROWS = PEERS * SLOTS_PER_SOURCE
HOT_AT = (0, 10, 20, 30)
TQ, TK = 512, 512
HALF = ROWS // 2
WINDOWS = PEERS * 64
SECOND = (((2, 0), (1, 0), (3, 0)), ((2, 1), (1, 1), (3, 1), (0, 1)))
SWITCH = ((3, 4), (3, 4))
FAR = 2.0**100
MESH = pl.DeviceIdType.MESH
F32, BF16, I32 = jnp.float32, jnp.bfloat16, jnp.int32


def iota(shape, dim):
    return lax.broadcasted_iota(I32, shape, dim)


def dot(a, b, dims=((1,), (0,))):
    return lax.dot_general(a, b, (dims, ((), ())), preferred_element_type=F32)


def kernel(
    q_ref, k_ref, v_ref, d_ref, bid_ref,
    x, flag_out,
    send, send_hot, recv, recv_hot, ret, ret_hot, mid, rows_buf, meta, meta_in, flags,
    pos_row, pos_col, aug_q, aug_k, kt, vt, dkv, p_buf, dp_buf, tops, acc_o, acc_q,
    one_ssem, one_rsem, two_ssem, two_rsem, own_sem, free_sem, meta_ssem, meta_rsem,
    hot_ssem, hot_rsem, back_ssem, back_rsem, flag_ssem, flag_rsem, in_sem,
):
    me = lax.axis_index("seq")
    col = lax.axis_index("head")
    y, z, c = me // 8, lax.rem(me // 2, 4), lax.rem(me, 2)
    scale = 1.0 / math.sqrt(128)
    to_exp2 = scale * math.log2(math.e)

    def ya(d):
        return lax.rem(y + d, 4)

    def za(d):
        return lax.rem(z + d, 4)

    def dev(yy, zz, cc):
        return yy * 8 + zz * 2 + cc

    barrier = pltpu.get_barrier_semaphore()
    for k in range(1, PEERS):
        pl.semaphore_signal(
            barrier, inc=1, device_id={"seq": lax.rem(me + k, PEERS)}, device_id_type=MESH
        )
    for step in (1, 2, 3):
        pl.semaphore_signal(
            barrier, inc=1, device_id={"head": lax.rem(col + step, 4)}, device_id_type=MESH
        )

    inputs = (q_ref, k_ref, v_ref, d_ref)
    quarters = range(4)

    def load(a, part):
        return pltpu.make_async_copy(
            inputs[a].at[pl.ds(part * 1024, 1024)],
            rows_buf.at[pl.ds(a % 3 * 1024, 1024), pl.ds(part * 128, 128)],
            in_sem.at[a, part],
        )

    for a in range(3):
        for part in quarters:
            load(a, part).start()
    for a in range(4):
        for part in quarters:
            load(a, part).wait()
            dkv[part * 1024 : part * 1024 + 1024, :] = rows_buf[
                a % 3 * 1024 : a % 3 * 1024 + 1024, part * 128 : part * 128 + 128
            ].astype(F32)
        if a == 0:
            for part in quarters:
                load(3, part).start()
        for h in range(4):
            x[h, :, a * 128 : a * 128 + 128] = dkv[pl.ds(h, 1024, stride=4), :].astype(BF16)

    named = jnp.concatenate(
        [(iota((64, 1024), 0) == bid_ref[h : h + 1, :]).astype(F32) for h in range(4)], axis=0
    )
    named16 = named.astype(BF16)
    ranks = []
    for part in quarters:
        earlier = iota((1024, 256), 0) < iota((1024, 256), 1) + part * 256
        ranks.append(dot(named16, earlier.astype(F32).astype(BF16)))
    rank = jnp.concatenate(ranks, axis=1)
    count = jnp.sum(named, axis=1, keepdims=True)
    full = (count == 32.0).astype(F32)
    count = count * (1.0 - full)
    bad = jnp.float32(0.0)
    for h in range(4):
        n_full = jnp.sum(full[h * 64 : h * 64 + 64])
        bad = jnp.maximum(bad, (n_full != 1.0).astype(F32))
    r0, r1 = iota((256, 256), 0), iota((256, 256), 1)
    alike = r0 // 2 == r1 // 2
    lanes = jnp.broadcast_to(count, (256, 128))
    lanes16 = lanes.astype(BF16)
    start = dot((alike & (r1 < r0)).astype(F32).astype(BF16), lanes16)[:, :1]
    both = dot(alike.astype(F32).astype(BF16), lanes16)[:, :1]
    rows = iota((256, 1), 0)
    owner = lax.rem(rows, 64) // 2
    second = lax.rem(rows // 64, 2)
    inside = start + jnp.where(second == 1, ROWS - both, 0.0)
    at_hot = (second * 32).astype(F32)
    base = jnp.where(full > 0, SPAN + at_hot, (owner * ROWS).astype(F32) + inside)
    back = jnp.where(full > 0, WINDOWS + at_hot, (owner * 64 - second * 32).astype(F32) + inside)

    def per_head(table):
        landed = named * (rank + table)
        return jnp.concatenate(
            [jnp.sum(landed[h * 64 : h * 64 + 64], axis=0, keepdims=True) for h in range(4)],
            axis=0,
        )

    pos_row[0:4, :] = per_head(base).astype(I32)
    place = jnp.concatenate([per_head(back), jnp.zeros((124, 1024), F32)], axis=0)
    pos_col[...] = place.T.astype(I32)

    lane, r2 = iota((256, 128), 1), iota((256, 128), 0)
    code = lax.rem(r2 // 64, 2) * 2 + lax.rem(r2, 2)
    front, rear = code < 2, code >= 2
    low = (lane < 2) | (lane == 4)
    high = (lane == 2) | (lane == 3)
    w_start = jnp.where((low & front & (code < lane)) | (lane == 5), lanes, 0.0)
    w_start = w_start - jnp.where(high & rear & (code >= lane), lanes, 0.0)
    w_end = jnp.where((lane < 2) & front & (code <= lane), lanes, 0.0)
    w_end = w_end - jnp.where((high & (code > lane)) | (lane == 4) & rear, lanes, 0.0)
    mr, mc = iota((512, 256), 0), iota((512, 256), 1)
    mine = mr // 16 == lax.rem(mc, 64) // 2
    pick_start = (mine & (lax.rem(mr, 16) == mc // 128 * 2)).astype(F32).astype(BF16)
    pick_end = (mine & (lax.rem(mr, 16) == mc // 128 * 2 + 1)).astype(F32).astype(BF16)
    starts = dot(pick_start, w_start.astype(BF16))
    kind, ml = lax.rem(iota((512, 128), 0), 16), iota((512, 128), 1)
    bad = jnp.maximum(bad, (jnp.max(jnp.where(ml == 5, starts, 0.0)) > ROWS).astype(F32))
    high = (ml == 2) | (ml == 3)
    to_rows = ((kind == 0) | (kind == 2)) & high
    to_rows = to_rows | ((kind == 1) | (kind == 3)) & (high | (ml == 4))
    tail = jnp.where(to_rows, jnp.float32(ROWS), 0.0) + jnp.where(kind == 4, bad, 0.0)
    meta[...] = (starts + dot(pick_end, w_end.astype(BF16)) + tail).astype(BF16)

    def meta_copy(k):
        other = lax.rem(me + k, PEERS)
        return pltpu.make_async_remote_copy(
            src_ref=meta.at[pl.ds(pl.multiple_of(other * 16, 16), 16)],
            dst_ref=meta_in.at[pl.ds(pl.multiple_of(me * 16, 16), 16)],
            send_sem=meta_ssem.at[k],
            recv_sem=meta_rsem.at[k],
            device_id={"seq": other},
            device_id_type=MESH,
        )

    def ends(phase):
        return (send, recv) if phase < 2 else (recv, ret)

    def one(phase, half, d, e):
        g, src, cc = phase % 2, ends(phase)[0], lax.rem(c + e, 2)
        if half == 0:
            from_, to = src.at[g, ya(d), :, cc, 0:HALF], mid.at[g, 0, y, :, cc]
            other = dev(ya(d), z, c)
        else:
            from_, to = src.at[g, :, za(d), cc, HALF:ROWS], mid.at[g, 1, z, :, cc]
            other = dev(y, za(d), c)
        return pltpu.make_async_remote_copy(
            src_ref=from_,
            dst_ref=to,
            send_sem=one_ssem.at[phase, half, d * 2 + e],
            recv_sem=one_rsem.at[phase, half, d * 2 + e],
            device_id={"seq": other},
            device_id_type=MESH,
        )

    def one_own(phase, half):
        g, src = phase % 2, ends(phase)[0]
        sem = own_sem.at[phase, half, 0]
        if half == 0:
            return pltpu.make_async_copy(src.at[g, y, :, :, 0:HALF], mid.at[g, 0, y], sem)
        return pltpu.make_async_copy(src.at[g, :, z, :, HALF:ROWS], mid.at[g, 1, z], sem)

    def two(phase, half, d, e):
        g, dst = phase % 2, ends(phase)[1]
        cc = lax.rem(c + e, 2)
        if half == 0:
            from_, to = mid.at[g, 0, :, za(d), cc], dst.at[g, :, z, c, 0:HALF]
            other = dev(y, za(d), cc)
        else:
            from_, to = mid.at[g, 1, :, ya(d), cc], dst.at[g, y, :, c, HALF:ROWS]
            other = dev(ya(d), z, cc)
        return pltpu.make_async_remote_copy(
            src_ref=from_,
            dst_ref=to,
            send_sem=two_ssem.at[phase, half, d * 2 + e],
            recv_sem=two_rsem.at[phase, half, d * 2 + e],
            device_id={"seq": other},
            device_id_type=MESH,
        )

    def two_own(phase, half):
        g, dst = phase % 2, ends(phase)[1]
        sem = own_sem.at[phase, half, 1]
        if half == 0:
            return pltpu.make_async_copy(mid.at[g, 0, :, z, c], dst.at[g, :, z, c, 0:HALF], sem)
        return pltpu.make_async_copy(mid.at[g, 1, :, y, c], dst.at[g, y, :, c, HALF:ROWS], sem)

    def hot_copy(h):
        return pltpu.make_async_remote_copy(
            src_ref=send_hot.at[h // 2, pl.ds(h % 2 * 32, 32)],
            dst_ref=recv_hot.at[pl.ds(pl.multiple_of(me * 32, 32), 32)],
            send_sem=hot_ssem.at[h],
            recv_sem=hot_rsem.at[me],
            device_id={"seq": HOT_AT[h]},
            device_id_type=MESH,
        )

    def hot_from(h, s):
        return pltpu.make_async_remote_copy(
            src_ref=send_hot.at[h // 2, pl.ds(h % 2 * 32, 32)],
            dst_ref=recv_hot.at[pl.ds(s * 32, 32)],
            send_sem=hot_ssem.at[h],
            recv_sem=hot_rsem.at[s],
            device_id={"seq": HOT_AT[h]},
            device_id_type=MESH,
        )

    def hot_own(h):
        return pltpu.make_async_copy(
            send_hot.at[h // 2, pl.ds(h % 2 * 32, 32)],
            recv_hot.at[pl.ds(HOT_AT[h] * 32, 32)],
            hot_ssem.at[h],
        )

    def back_copy(h, s):
        return pltpu.make_async_remote_copy(
            src_ref=recv_hot.at[pl.ds(s * 32, 32)],
            dst_ref=ret_hot.at[h // 2, pl.ds(h % 2 * 32, 32)],
            send_sem=back_ssem.at[s],
            recv_sem=back_rsem.at[h],
            device_id={"seq": s},
            device_id_type=MESH,
        )

    def back_own(h):
        return pltpu.make_async_copy(
            recv_hot.at[pl.ds(HOT_AT[h] * 32, 32)],
            ret_hot.at[h // 2, pl.ds(h % 2 * 32, 32)],
            back_rsem.at[h],
        )

    def start_one(phase):
        if phase >= 2:
            pl.semaphore_wait(free_sem.at[phase % 2], 6)
        for e in (0, 1):
            for d in (2, 1, 3):
                for half in (0, 1):
                    one(phase, half, d, e).start()
        for half in (0, 1):
            one_own(phase, half).start()

    def hot_start(g):
        for h in (2 * g, 2 * g + 1):

            @pl.when(me != HOT_AT[h])
            def _():
                hot_copy(h).start()

            @pl.when(me == HOT_AT[h])
            def _():
                hot_own(h).start()

    def start_two(phase, e):
        for half in (0, 1):
            for d in (1, 2, 3):
                one(phase, half, d, e).wait_recv()
            if e == 0:
                one_own(phase, half).wait()
        for d, _ in SECOND[e]:
            for half in (0, 1):
                two(phase, half, d, e).start()
        if e == 0:
            for half in (0, 1):
                two_own(phase, half).start()

    def arrive(phase):
        for half in (0, 1):
            for d, e in SECOND[0] + SECOND[1]:
                two(phase, half, d, e).wait_recv()
            two_own(phase, half).wait()

    def drain(phase):
        for half in (0, 1):
            for d in (1, 2, 3):
                for e in (0, 1):
                    one(phase, half, d, e).wait_send()
            for d, e in SECOND[0] + SECOND[1]:
                two(phase, half, d, e).wait_send()
        if phase < 2:
            g = phase % 2
            for d in (1, 2, 3):
                for other in (dev(ya(d), z, c), dev(y, za(d), c)):
                    pl.semaphore_signal(
                        free_sem.at[g], inc=1, device_id={"seq": other}, device_id_type=MESH
                    )
            for h in (2 * g, 2 * g + 1):

                @pl.when(me != HOT_AT[h])
                def _():
                    hot_copy(h).wait_send()

    def back_start(h):
        for s in range(PEERS):
            if s != HOT_AT[h]:
                back_copy(h, s).start()
        back_own(h).start()

    def back_drain(g):
        for h in (2 * g, 2 * g + 1):

            @pl.when(me == HOT_AT[h])
            def _():
                for s in range(PEERS):
                    if s != HOT_AT[h]:
                        back_copy(h, s).wait_send()

    def hot_arrive(h):
        for s in range(PEERS):
            if s != HOT_AT[h]:
                hot_from(h, s).wait_recv()
        hot_own(h).wait()

    def back_arrive(g):
        for h in (2 * g, 2 * g + 1):

            @pl.when(me != HOT_AT[h])
            def _():
                back_copy(h, 0).wait_recv()

            @pl.when(me == HOT_AT[h])
            def _():
                back_own(h).wait()

    def picked(shape, at, first):
        index = iota(shape, 0)
        return (index // 32 * ROWS + lax.rem(index, 32) == at - first).astype(F32).astype(BF16)

    def pack(g):
        a, b = pos_row[2 * g : 2 * g + 1, :], pos_row[2 * g + 1 : 2 * g + 2, :]

        def body(m, _):
            first = m * 16 * ROWS
            two_y = pl.ds(m * 2, 2)
            shape = (2, 4, 2, 32, 512)
            p = picked((512, 1024), a, first)
            send[g, two_y, :, :, 0:32, :] = dot(p, x[2 * g]).astype(BF16).reshape(shape)
            p = picked((512, 1024), b, first + 64)
            send[g, two_y, :, :, 64:96, :] = dot(p, x[2 * g + 1]).astype(BF16).reshape(shape)
            p = picked((512, 1024), a, first + 32)
            t = dot(p, x[2 * g])
            p = picked((512, 1024), b, first + 32)
            t = t + dot(p, x[2 * g + 1])
            send[g, two_y, :, :, 32:64, :] = t.astype(BF16).reshape(shape)
            return 0

        lax.fori_loop(0, 2, body, 0)
        for k, at in ((0, a), (1, b)):
            pick = (iota((32, 1024), 0) + (SPAN + k * 32) == at).astype(F32).astype(BF16)
            send_hot[g, k * 32 : k * 32 + 32] = dot(pick, x[2 * g + k]).astype(BF16)

    def unpack(g):
        def body(m, _):
            t = pl.ds(pl.multiple_of(m * 512, 512), 512)
            for k in (0, 1):
                at = pos_col[t, 2 * g + k : 2 * g + k + 1]
                pick = (iota((512, WINDOWS), 1) == at).astype(F32).astype(BF16)
                hot_pick = (iota((512, 64), 1) + WINDOWS == at).astype(F32).astype(BF16)
                got = ret[g, :, :, :, k * 32 : k * 32 + 64, :].reshape(WINDOWS, 512)
                x[2 * g + k, t, :] = (dot(pick, got) + dot(hot_pick, ret_hot[g])).astype(BF16)
            return 0

        lax.fori_loop(0, 2, body, 0)

    def attend(rows_ref, span, coded, between):
        def after(j):
            return pl.ds(pl.multiple_of(SPAN + j * TK, TK), TK)

        def body(i, _):
            between(i)
            qs = pl.ds(pl.multiple_of(i * TQ, TQ), TQ)
            q_i = rows_ref[qs, 0:128]
            d_i = rows_ref[qs, 384:512]
            q_a = jnp.concatenate([q_i, aug_q[qs, :]], axis=1) if coded else q_i
            full_tiles = (i * TQ) // TK

            def weigh(j, sums, edge):
                top, total, delta = sums
                ks = pl.ds(pl.multiple_of(j * TK, TK), TK)
                k_j = rows_ref[ks, 128:256]
                if coded:
                    k_j = jnp.concatenate([k_j, aug_k[ks, :]], axis=1)
                s = dot(k_j, q_a, ((1,), (1,)))
                if edge:
                    gap = iota((TK, TQ), 0) - iota((TK, TQ), 1)
                    s = jnp.where(gap <= i * TQ - j * TK, s, -1e30)
                new = jnp.maximum(top, jnp.max(s, axis=0, keepdims=True))
                p = jnp.exp2((s - new) * to_exp2)
                dp = dot(rows_ref[ks, 256:384], d_i, ((1,), (1,)))
                p_buf[ks, :] = p
                dp_buf[ks, :] = dp
                tops[pl.ds(pl.multiple_of(j * 8, 8), 8), :] = jnp.broadcast_to(new, (8, TQ))
                keep = jnp.exp2((top - new) * to_exp2)
                return (
                    new,
                    total * keep + jnp.sum(p, axis=0, keepdims=True),
                    delta * keep + jnp.sum(p * dp, axis=0, keepdims=True),
                )

            none = jnp.zeros((1, TQ), F32)
            sums = (jnp.full((1, TQ), -1e30, F32), none, none)
            sums = lax.fori_loop(0, full_tiles, lambda j, a: weigh(j, a, False), sums)
            top, total, delta = weigh(full_tiles, sums, True)
            inv = 1.0 / total
            delta = delta * inv
            acc_o[...] = jnp.zeros_like(acc_o)
            acc_q[...] = jnp.zeros_like(acc_q)

            def spread(j, _):
                ks = pl.ds(pl.multiple_of(j * TK, TK), TK)
                here = tops[pl.ds(pl.multiple_of(j * 8, 8), 8), :][:1]
                w = p_buf[ks, :] * (jnp.exp2((here - top) * to_exp2) * inv)
                rounded = w.astype(BF16)
                ds = (w * (dp_buf[ks, :] - delta)).astype(BF16)
                acc_o[...] += dot(vt[:, ks], rounded)
                acc_q[...] += dot(kt[:, ks], ds)
                dkv[ks, :] += dot(ds, q_i)
                dkv[after(j), :] += dot(rounded, d_i)
                return 0

            lax.fori_loop(0, full_tiles + 1, spread, 0)
            rows_ref[qs, 0:128] = acc_o[...].T.astype(BF16)
            rows_ref[qs, 384:512] = (acc_q[...] * scale).T.astype(BF16)
            return 0

        def ready(j, _):
            ks = pl.ds(pl.multiple_of(j * TK, TK), TK)
            kt[:, ks] = rows_ref[ks, 128:256].astype(F32).T.astype(BF16)
            vt[:, ks] = rows_ref[ks, 256:384].astype(F32).T.astype(BF16)
            dkv[ks, :] = jnp.zeros((TK, 128), F32)
            dkv[after(j), :] = jnp.zeros((TK, 128), F32)
            return 0

        lax.fori_loop(0, span // TK, ready, 0)
        lax.fori_loop(0, span // TQ, body, 0)

        def finish(j, _):
            ks = pl.ds(pl.multiple_of(j * TK, TK), TK)
            rows_ref[ks, 128:256] = (dkv[ks, :] * scale).astype(BF16)
            rows_ref[ks, 256:384] = dkv[after(j), :].astype(BF16)
            return 0

        lax.fori_loop(0, span // TK, finish, 0)

    def codes(g):
        def body(s, _):
            note = meta_in[pl.ds(pl.multiple_of(s * 16, 16), 16), :].astype(F32)
            r = iota((ROWS, 128), 0).astype(F32)
            inside = (r >= note[2 * g : 2 * g + 1]) & (r < note[2 * g + 1 : 2 * g + 2])
            known = iota((ROWS, 128), 1) <= 4
            at = pl.ds(pl.multiple_of(s * ROWS, ROWS), ROWS)
            aug_q[at, :] = jnp.where(inside, 1.0, 0.0).astype(BF16)
            aug_k[at, :] = jnp.where(known & ~inside, -FAR, 0.0).astype(BF16)
            return 0

        lax.fori_loop(0, PEERS, body, 0)

    def hot_work():
        for h in range(4):

            @pl.when(me == HOT_AT[h])
            def _():
                hot_arrive(h)

        @pl.when((me == HOT_AT[0]) | (me == HOT_AT[1]) | (me == HOT_AT[2]) | (me == HOT_AT[3]))
        def _():
            attend(recv_hot, HOT_ROWS, False, lambda i: None)

        for h in range(4):

            @pl.when(me == HOT_AT[h])
            def _():
                back_start(h)

    def work(g, between):
        def load(yy, _):
            at = pl.ds(pl.multiple_of(yy * 768, 768), 768)
            rows_buf[at, :] = recv[g, yy].reshape(768, 512)
            return 0

        def store(yy, _):
            at = pl.ds(pl.multiple_of(yy * 768, 768), 768)
            recv[g, yy] = rows_buf[at, :].reshape(4, 2, ROWS, 512)
            return 0

        lax.fori_loop(0, 4, load, 0)
        attend(rows_buf, SPAN, True, between)
        lax.fori_loop(0, 4, store, 0)

    def ahead(phase, blocks):
        def between(i):
            for e in (0, 1):

                @pl.when(i == blocks[e])
                def _():
                    start_two(phase, e)

        return between

    pack(0)
    pl.semaphore_wait(barrier, PEERS - 1 + 3)
    start_one(0)
    hot_start(0)
    for k in range(1, PEERS):
        meta_copy(k).start()
    own_meta = pl.ds(pl.multiple_of(me * 16, 16), 16)
    meta_in[own_meta, :] = meta[own_meta, :]
    pack(1)
    hot_start(1)
    start_two(0, 0)
    start_two(0, 1)
    start_one(1)

    for k in range(1, PEERS):
        meta_copy(k).wait()
    noted = meta_in[...].astype(F32)
    noted = jnp.where(lax.rem(iota((512, 128), 0), 16) == 4, noted, 0.0)
    flags[0] = jnp.broadcast_to(jnp.max(noted, axis=0, keepdims=True), (16, 128)).astype(BF16)

    def flag_copy(step):
        return pltpu.make_async_remote_copy(
            src_ref=flags.at[0],
            dst_ref=flags.at[step],
            send_sem=flag_ssem.at[step],
            recv_sem=flag_rsem.at[step],
            device_id={"head": lax.rem(col + step, 4)},
            device_id_type=MESH,
        )

    for step in (1, 2, 3):
        flag_copy(step).start()

    codes(0)
    hot_work()
    arrive(0)
    drain(0)
    work(0, ahead(1, SWITCH[0]))
    start_one(2)
    codes(1)
    arrive(1)
    drain(1)
    work(1, ahead(2, SWITCH[1]))
    start_one(3)
    arrive(2)
    start_two(3, 0)
    back_arrive(0)
    unpack(0)
    start_two(3, 1)
    for step in (1, 2, 3):
        flag_copy(step).wait()
    any_flag = jnp.maximum(
        jnp.maximum(flags[0].astype(F32), flags[1].astype(F32)),
        jnp.maximum(flags[2].astype(F32), flags[3].astype(F32)),
    )
    flag_out[...] = any_flag[:8]
    drain(2)
    back_drain(0)
    arrive(3)
    back_arrive(1)
    unpack(1)
    drain(3)
    back_drain(1)


def settle_kernel(x, o_q, o_k, o_v, o_d, held, wide, done, in_sem, out_sem):
    def load(m):
        return pltpu.make_async_copy(x.at[:, pl.ds(m * 256, 256)], held.at[m], in_sem.at[m])

    outs = ((0, o_q), (3, o_k), (1, o_v), (2, o_d))

    def save(m, n):
        at = pl.ds(m * 1024, 1024)
        return pltpu.make_async_copy(done.at[n, at], outs[n][1].at[at], out_sem.at[m, n])

    for m in range(4):
        load(m).start()
    for m in range(4):
        load(m).wait()
        for n, (a, _) in enumerate(outs):
            for h in range(4):
                wide[n, pl.ds(h, 256, stride=4), :] = held[m, h, :, a * 128 : a * 128 + 128].astype(
                    F32
                )
            done[n, m * 1024 : m * 1024 + 1024, :] = wide[n].astype(BF16)
            save(m, n).start()
    for m in range(4):
        for n in range(4):
            save(m, n).wait()


def settle(x):
    outs = pl.pallas_call(
        settle_kernel,
        out_shape=[jax.ShapeDtypeStruct((4096, 128), BF16)] * 4,
        in_specs=[pl.BlockSpec(memory_space=pl.ANY)],
        out_specs=[pl.BlockSpec(memory_space=pl.ANY)] * 4,
        scratch_shapes=[
            pltpu.VMEM((4, 4, 256, 512), BF16),
            pltpu.VMEM((4, 1024, 128), F32),
            pltpu.VMEM((4, 4096, 128), BF16),
            pltpu.SemaphoreType.DMA((4,)),
            pltpu.SemaphoreType.DMA((4, 4)),
        ],
        compiler_params=pltpu.CompilerParams(vmem_limit_bytes=32 * 2**20),
        name="settle",
    )(x)
    return tuple(a.reshape(1024, 4, 128) for a in outs)


def quick(queries, key_rows, value_rows, out_grad, bucket_id):
    rows = [a.reshape(4096, 128) for a in (queries, key_rows, value_rows, out_grad)]
    vmem = pl.BlockSpec(memory_space=pltpu.VMEM)
    dma = pltpu.SemaphoreType.DMA
    outs = pl.pallas_call(
        kernel,
        out_shape=[
            jax.ShapeDtypeStruct((4, 1024, 512), BF16),
            jax.ShapeDtypeStruct((8, 128), F32),
        ],
        in_specs=[pl.BlockSpec(memory_space=pl.ANY)] * 4 + [vmem],
        out_specs=[vmem] * 2,
        scratch_shapes=[
            pltpu.VMEM((2, 4, 4, 2, ROWS, 512), BF16),
            pltpu.VMEM((2, 64, 512), BF16),
            pltpu.VMEM((2, 4, 4, 2, ROWS, 512), BF16),
            pltpu.VMEM((HOT_ROWS, 512), BF16),
            pltpu.VMEM((2, 4, 4, 2, ROWS, 512), BF16),
            pltpu.VMEM((2, 64, 512), BF16),
            pltpu.VMEM((2, 2, 4, 4, 2, HALF, 512), BF16),
            pltpu.VMEM((SPAN, 512), BF16),
            pltpu.VMEM((512, 128), BF16),
            pltpu.VMEM((512, 128), BF16),
            pltpu.VMEM((4, 16, 128), BF16),
            pltpu.VMEM((8, 1024), I32),
            pltpu.VMEM((1024, 128), I32),
            pltpu.VMEM((SPAN, 128), BF16),
            pltpu.VMEM((SPAN, 128), BF16),
            pltpu.VMEM((128, SPAN), BF16),
            pltpu.VMEM((128, SPAN), BF16),
            pltpu.VMEM((2 * SPAN, 128), F32),
            pltpu.VMEM((SPAN, TQ), F32),
            pltpu.VMEM((SPAN, TQ), F32),
            pltpu.VMEM((SPAN // TK * 8, TQ), F32),
            pltpu.VMEM((128, TQ), F32),
            pltpu.VMEM((128, TQ), F32),
            dma((4, 2, 8)), dma((4, 2, 8)), dma((4, 2, 8)), dma((4, 2, 8)), dma((4, 2, 2)),
            pltpu.SemaphoreType.REGULAR((2,)), dma((PEERS,)), dma((PEERS,)),
            dma((4,)), dma((PEERS,)), dma((PEERS,)), dma((4,)), dma((4,)), dma((4,)),
            dma((4, 4)),
        ],
        compiler_params=pltpu.CompilerParams(
            collective_id=0, has_side_effects=True, vmem_limit_bytes=60 * 2**20
        ),
        name="bucket_layer",
    )(*rows, bucket_id.T)
    return outs[0], outs[1][0, 0] > 0


def bucket_weights(q_part, k_part, valid, scale):
    span = q_part.shape[0]
    sorted_index = jnp.arange(span, dtype=I32)
    allowed = (sorted_index[None, :] <= sorted_index[:, None]) & (
        (valid[None, :] > 0) | (sorted_index[None, :] == sorted_index[:, None])
    )
    scores = jnp.dot(q_part, k_part.T, preferred_element_type=F32) * scale
    scores = jnp.where(allowed, scores, F32(-1e30))
    top = jnp.max(scores, axis=1, keepdims=True)
    expd = jnp.where(allowed, jnp.exp(scores - top), F32(0.0))
    return expd / jnp.sum(expd, axis=1, keepdims=True)


def bucket_forward(block, valid, width):
    scale = 1.0 / math.sqrt(width)
    weights = bucket_weights(block[:, :width], block[:, width : 2 * width], valid, scale)
    rounded = weights.astype(BF16)
    return jnp.dot(rounded, block[:, 2 * width :], preferred_element_type=F32).astype(
        BF16
    )


def bucket_backward(block, d_part, valid, width):
    scale = 1.0 / math.sqrt(width)
    q_part = block[:, :width]
    k_part = block[:, width : 2 * width]
    v_part = block[:, 2 * width : 3 * width]
    weights = bucket_weights(q_part, k_part, valid, scale)
    rounded = weights.astype(BF16)
    dprob = jnp.dot(d_part, v_part.T, preferred_element_type=F32)
    delta = jnp.sum(weights * dprob, axis=1, keepdims=True)
    dscore = (weights * (dprob - delta)).astype(BF16)
    grad_q = (jnp.dot(dscore, k_part, preferred_element_type=F32) * scale).astype(
        BF16
    )
    grad_k = (jnp.dot(dscore.T, q_part, preferred_element_type=F32) * scale).astype(
        BF16
    )
    grad_v = jnp.dot(rounded.T, d_part, preferred_element_type=F32).astype(BF16)
    return (rounded, v_part, grad_q, grad_k, grad_v)


def bucket_grads(block, d_part, valid, width):
    rounded, v_part, grad_q, grad_k, grad_v = bucket_backward(block, d_part, valid, width)
    return jnp.concatenate([grad_q, grad_k, grad_v], axis=1)


def slow(queries, key_rows, value_rows, out_grad, bucket_id, bucket_slot):
    peers = lax.axis_size("seq")
    tok_count, group, width = queries.shape
    per_owner = BUCKETS_PER_HEAD // peers
    span = peers * SLOTS_PER_SOURCE
    total = group * per_owner * span
    owner = bucket_id // per_owner
    local_bucket = bucket_id % per_owner
    head_index = jnp.arange(group, dtype=I32)[None, :]
    flat = (
        (head_index * per_owner + local_bucket) * span + owner * SLOTS_PER_SOURCE + bucket_slot
    ).reshape(-1)
    marks = (
        jnp.zeros((total,), BF16)
        .at[flat]
        .set(BF16(1.0))
        .reshape(group, per_owner, span)
    )

    def spread(rows):
        columns = rows.shape[-1]
        placed = jnp.zeros((total, columns), rows.dtype).at[flat].set(rows.reshape(-1, columns))
        return placed.reshape(group, per_owner, span, columns)

    def collect(buffer):
        columns = buffer.shape[-1]
        return buffer.reshape(total, columns)[flat].reshape(tok_count, group, columns)

    joined = jnp.concatenate([queries, key_rows, value_rows], axis=2)
    blocks, valid = (
        lax.all_to_all(spread(joined), "seq", split_axis=2, concat_axis=2, tiled=True),
        lax.all_to_all(marks, "seq", split_axis=2, concat_axis=2, tiled=True),
    )
    flat_blocks = blocks.reshape(-1, span, 3 * width)
    flat_valid = valid.reshape(-1, span)
    attended = lax.map(
        lambda item: bucket_forward(item[0], item[1], width), (flat_blocks, flat_valid)
    )
    attended = lax.all_to_all(
        attended.reshape(group, per_owner, span, width),
        "seq",
        split_axis=2,
        concat_axis=2,
        tiled=True,
    )
    incoming = lax.all_to_all(spread(out_grad), "seq", split_axis=2, concat_axis=2, tiled=True)
    grads = lax.map(
        lambda item: bucket_grads(item[0], item[1], item[2], width),
        (flat_blocks, incoming.reshape(-1, span, width), flat_valid),
    )
    grads = lax.all_to_all(
        grads.reshape(group, per_owner, span, 3 * width),
        "seq",
        split_axis=2,
        concat_axis=2,
        tiled=True,
    )
    gathered = collect(grads)
    return (
        collect(attended),
        gathered[:, :, :width],
        gathered[:, :, width : 2 * width],
        gathered[:, :, 2 * width :],
    )


def shards(queries, key_rows, value_rows, out_grad, bucket_id, bucket_slot):
    packed, crowded = quick(queries, key_rows, value_rows, out_grad, bucket_id)
    return lax.cond(
        crowded,
        lambda: slow(queries, key_rows, value_rows, out_grad, bucket_id, bucket_slot),
        lambda: settle(packed),
    )


def solution(mesh):
    in_specs = (
        P("seq", "head", None),
        P("seq", "head", None),
        P("seq", "head", None),
        P("seq", "head", None),
        P("seq", "head"),
        P("seq", "head"),
    )
    out_specs = (
        P("seq", "head", None),
        P("seq", "head", None),
        P("seq", "head", None),
        P("seq", "head", None),
    )
    return jax.shard_map(shards, mesh=mesh, in_specs=in_specs, out_specs=out_specs, check_vma=False)
```

```python
import functools
import math

import jax
import jax.numpy as jnp
from jax import lax
from jax.experimental import pallas as pl
from jax.experimental.pallas import tpu as pltpu
from jax.sharding import PartitionSpec as P

SLOTS_PER_SOURCE = 32
BUCKETS_PER_HEAD = 64
PEERS = 32
ROWS = 96
SPAN = PEERS * ROWS
HOT_ROWS = PEERS * SLOTS_PER_SOURCE
HOT_AT = (0, 10, 20, 30)
TQ, TK = 512, 512
HALF = ROWS // 2
WINDOWS = PEERS * 64
SECOND = (((2, 0), (1, 0), (3, 0)), ((2, 1), (1, 1), (3, 1), (0, 1)))
SWITCH = ((3, 4), (3, 4))
FAR = 2.0**100
MESH = pl.DeviceIdType.MESH
F32, BF16, I32 = jnp.float32, jnp.bfloat16, jnp.int32


def iota(shape, dim):
    return lax.broadcasted_iota(I32, shape, dim)


def dot(a, b, dims=((1,), (0,))):
    return lax.dot_general(a, b, (dims, ((), ())), preferred_element_type=F32)


def kernel(
    q_ref, k_ref, v_ref, d_ref, bid_ref,
    x, flag_out,
    send, send_hot, recv, recv_hot, ret, ret_hot, mid, rows_buf, meta, meta_in, flags,
    pos_row, pos_col, aug_q, aug_k, kt, vt, dkv, p_buf, dp_buf, tops, acc_o, acc_q,
    one_ssem, one_rsem, two_ssem, two_rsem, own_sem, free_sem, meta_ssem, meta_rsem,
    hot_ssem, hot_rsem, back_ssem, back_rsem, flag_ssem, flag_rsem, in_sem,
):
    me = lax.axis_index("seq")
    col = lax.axis_index("head")
    y, z, c = me // 8, lax.rem(me // 2, 4), lax.rem(me, 2)
    scale = 1.0 / math.sqrt(128)
    to_exp2 = scale * math.log2(math.e)

    def ya(d):
        return lax.rem(y + d, 4)

    def za(d):
        return lax.rem(z + d, 4)

    def dev(yy, zz, cc):
        return yy * 8 + zz * 2 + cc

    barrier = pltpu.get_barrier_semaphore()
    for k in range(1, PEERS):
        pl.semaphore_signal(
            barrier, inc=1, device_id={"seq": lax.rem(me + k, PEERS)}, device_id_type=MESH
        )
    for step in (1, 2, 3):
        pl.semaphore_signal(
            barrier, inc=1, device_id={"head": lax.rem(col + step, 4)}, device_id_type=MESH
        )

    inputs = (q_ref, k_ref, v_ref, d_ref)
    quarters = range(4)

    def load(a, part):
        return pltpu.make_async_copy(
            inputs[a].at[pl.ds(part * 1024, 1024)],
            rows_buf.at[pl.ds(a % 3 * 1024, 1024), pl.ds(part * 128, 128)],
            in_sem.at[a, part],
        )

    for a in range(3):
        for part in quarters:
            load(a, part).start()
    for a in range(4):
        for part in quarters:
            load(a, part).wait()
            dkv[part * 1024 : part * 1024 + 1024, :] = rows_buf[
                a % 3 * 1024 : a % 3 * 1024 + 1024, part * 128 : part * 128 + 128
            ].astype(F32)
        if a == 0:
            for part in quarters:
                load(3, part).start()
        for h in range(4):
            x[h, :, a * 128 : a * 128 + 128] = dkv[pl.ds(h, 1024, stride=4), :].astype(BF16)

    named = jnp.concatenate(
        [(iota((64, 1024), 0) == bid_ref[h : h + 1, :]).astype(F32) for h in range(4)], axis=0
    )
    named16 = named.astype(BF16)
    ranks = []
    for part in quarters:
        earlier = iota((1024, 256), 0) < iota((1024, 256), 1) + part * 256
        ranks.append(dot(named16, earlier.astype(F32).astype(BF16)))
    rank = jnp.concatenate(ranks, axis=1)
    count = jnp.sum(named, axis=1, keepdims=True)
    full = (count == 32.0).astype(F32)
    count = count * (1.0 - full)
    bad = jnp.float32(0.0)
    for h in range(4):
        n_full = jnp.sum(full[h * 64 : h * 64 + 64])
        bad = jnp.maximum(bad, (n_full != 1.0).astype(F32))
    r0, r1 = iota((256, 256), 0), iota((256, 256), 1)
    alike = r0 // 2 == r1 // 2
    lanes = jnp.broadcast_to(count, (256, 128))
    lanes16 = lanes.astype(BF16)
    start = dot((alike & (r1 < r0)).astype(F32).astype(BF16), lanes16)[:, :1]
    both = dot(alike.astype(F32).astype(BF16), lanes16)[:, :1]
    rows = iota((256, 1), 0)
    owner = lax.rem(rows, 64) // 2
    second = lax.rem(rows // 64, 2)
    inside = start + jnp.where(second == 1, ROWS - both, 0.0)
    at_hot = (second * 32).astype(F32)
    base = jnp.where(full > 0, SPAN + at_hot, (owner * ROWS).astype(F32) + inside)
    back = jnp.where(full > 0, WINDOWS + at_hot, (lax.rem(owner, 2) * 1024 + owner // 2 * 64 - second * 32).astype(F32) + inside)

    def per_head(table):
        landed = named * (rank + table)
        return jnp.concatenate(
            [jnp.sum(landed[h * 64 : h * 64 + 64], axis=0, keepdims=True) for h in range(4)],
            axis=0,
        )

    pos_row[0:4, :] = per_head(base).astype(I32)
    place = jnp.concatenate([per_head(back), jnp.zeros((124, 1024), F32)], axis=0)
    pos_col[...] = place.T.astype(I32)

    lane, r2 = iota((256, 128), 1), iota((256, 128), 0)
    code = lax.rem(r2 // 64, 2) * 2 + lax.rem(r2, 2)
    front, rear = code < 2, code >= 2
    low = (lane < 2) | (lane == 4)
    high = (lane == 2) | (lane == 3)
    w_start = jnp.where((low & front & (code < lane)) | (lane == 5), lanes, 0.0)
    w_start = w_start - jnp.where(high & rear & (code >= lane), lanes, 0.0)
    w_end = jnp.where((lane < 2) & front & (code <= lane), lanes, 0.0)
    w_end = w_end - jnp.where((high & (code > lane)) | (lane == 4) & rear, lanes, 0.0)
    mr, mc = iota((512, 256), 0), iota((512, 256), 1)
    mine = mr // 16 == lax.rem(mc, 64) // 2
    pick_start = (mine & (lax.rem(mr, 16) == mc // 128 * 2)).astype(F32).astype(BF16)
    pick_end = (mine & (lax.rem(mr, 16) == mc // 128 * 2 + 1)).astype(F32).astype(BF16)
    starts = dot(pick_start, w_start.astype(BF16))
    kind, ml = lax.rem(iota((512, 128), 0), 16), iota((512, 128), 1)
    bad = jnp.maximum(bad, (jnp.max(jnp.where(ml == 5, starts, 0.0)) > ROWS).astype(F32))
    high = (ml == 2) | (ml == 3)
    to_rows = ((kind == 0) | (kind == 2)) & high
    to_rows = to_rows | ((kind == 1) | (kind == 3)) & (high | (ml == 4))
    tail = jnp.where(to_rows, jnp.float32(ROWS), 0.0) + jnp.where(kind == 4, bad, 0.0)
    meta[...] = (starts + dot(pick_end, w_end.astype(BF16)) + tail).astype(BF16)

    def meta_copy(k):
        other = lax.rem(me + k, PEERS)
        return pltpu.make_async_remote_copy(
            src_ref=meta.at[pl.ds(pl.multiple_of(other * 16, 16), 16)],
            dst_ref=meta_in.at[pl.ds(pl.multiple_of(me * 16, 16), 16)],
            send_sem=meta_ssem.at[k],
            recv_sem=meta_rsem.at[k],
            device_id={"seq": other},
            device_id_type=MESH,
        )

    def ends(phase):
        return (send, recv) if phase < 2 else (recv, ret)

    def one(phase, half, d, e):
        g, src, cc = phase % 2, ends(phase)[0], lax.rem(c + e, 2)
        if half == 0:
            from_, to = src.at[g, ya(d), :, cc, 0:HALF], mid.at[g, 0, y, :, cc]
            other = dev(ya(d), z, c)
        else:
            from_, to = src.at[g, :, za(d), cc, HALF:ROWS], mid.at[g, 1, z, :, cc]
            other = dev(y, za(d), c)
        return pltpu.make_async_remote_copy(
            src_ref=from_,
            dst_ref=to,
            send_sem=one_ssem.at[phase, half, d * 2 + e],
            recv_sem=one_rsem.at[phase, half, d * 2 + e],
            device_id={"seq": other},
            device_id_type=MESH,
        )

    def one_own(phase, half):
        g, src = phase % 2, ends(phase)[0]
        sem = own_sem.at[phase, half, 0]
        if half == 0:
            return pltpu.make_async_copy(src.at[g, y, :, :, 0:HALF], mid.at[g, 0, y], sem)
        return pltpu.make_async_copy(src.at[g, :, z, :, HALF:ROWS], mid.at[g, 1, z], sem)

    def two(phase, half, d, e):
        g, dst = phase % 2, ends(phase)[1]
        cc = lax.rem(c + e, 2)
        if half == 0:
            from_, to = mid.at[g, 0, :, za(d), cc], dst.at[g, :, z, c, 0:HALF]
            other = dev(y, za(d), cc)
        else:
            from_, to = mid.at[g, 1, :, ya(d), cc], dst.at[g, y, :, c, HALF:ROWS]
            other = dev(ya(d), z, cc)
        return pltpu.make_async_remote_copy(
            src_ref=from_,
            dst_ref=to,
            send_sem=two_ssem.at[phase, half, d * 2 + e],
            recv_sem=two_rsem.at[phase, half, d * 2 + e],
            device_id={"seq": other},
            device_id_type=MESH,
        )

    def two_own(phase, half):
        g, dst = phase % 2, ends(phase)[1]
        sem = own_sem.at[phase, half, 1]
        if half == 0:
            return pltpu.make_async_copy(mid.at[g, 0, :, z, c], dst.at[g, :, z, c, 0:HALF], sem)
        return pltpu.make_async_copy(mid.at[g, 1, :, y, c], dst.at[g, y, :, c, HALF:ROWS], sem)

    def hot_copy(h):
        return pltpu.make_async_remote_copy(
            src_ref=send_hot.at[h // 2, pl.ds(h % 2 * 32, 32)],
            dst_ref=recv_hot.at[pl.ds(pl.multiple_of(me * 32, 32), 32)],
            send_sem=hot_ssem.at[h],
            recv_sem=hot_rsem.at[me],
            device_id={"seq": HOT_AT[h]},
            device_id_type=MESH,
        )

    def hot_from(h, s):
        return pltpu.make_async_remote_copy(
            src_ref=send_hot.at[h // 2, pl.ds(h % 2 * 32, 32)],
            dst_ref=recv_hot.at[pl.ds(s * 32, 32)],
            send_sem=hot_ssem.at[h],
            recv_sem=hot_rsem.at[s],
            device_id={"seq": HOT_AT[h]},
            device_id_type=MESH,
        )

    def hot_own(h):
        return pltpu.make_async_copy(
            send_hot.at[h // 2, pl.ds(h % 2 * 32, 32)],
            recv_hot.at[pl.ds(HOT_AT[h] * 32, 32)],
            hot_ssem.at[h],
        )

    def back_copy(h, s):
        return pltpu.make_async_remote_copy(
            src_ref=recv_hot.at[pl.ds(s * 32, 32)],
            dst_ref=ret_hot.at[h // 2, pl.ds(h % 2 * 32, 32)],
            send_sem=back_ssem.at[s],
            recv_sem=back_rsem.at[h],
            device_id={"seq": s},
            device_id_type=MESH,
        )

    def back_own(h):
        return pltpu.make_async_copy(
            recv_hot.at[pl.ds(HOT_AT[h] * 32, 32)],
            ret_hot.at[h // 2, pl.ds(h % 2 * 32, 32)],
            back_rsem.at[h],
        )

    def start_one(phase, e):
        if phase >= 2 and e == 0:
            pl.semaphore_wait(free_sem.at[phase % 2], 6)
        for d in (2, 1, 3):
            for half in (0, 1):
                one(phase, half, d, e).start()
        if e == 1:
            for half in (0, 1):
                one_own(phase, half).start()

    def hot_start(g):
        for h in (2 * g, 2 * g + 1):

            @pl.when(me != HOT_AT[h])
            def _():
                hot_copy(h).start()

            @pl.when(me == HOT_AT[h])
            def _():
                hot_own(h).start()

    def start_two(phase, e):
        for half in (0, 1):
            for d in (1, 2, 3):
                one(phase, half, d, e).wait_recv()
            if e == 0:
                one_own(phase, half).wait()
        for d, _ in SECOND[e]:
            for half in (0, 1):
                two(phase, half, d, e).start()
        if e == 0:
            for half in (0, 1):
                two_own(phase, half).start()

    def arrive(phase, e):
        for half in (0, 1):
            for d, _ in SECOND[e]:
                two(phase, half, d, e).wait_recv()
            if e == 0:
                two_own(phase, half).wait()

    def drain(phase):
        for half in (0, 1):
            for d in (1, 2, 3):
                for e in (0, 1):
                    one(phase, half, d, e).wait_send()
            for d, e in SECOND[0] + SECOND[1]:
                two(phase, half, d, e).wait_send()
        if phase < 2:
            g = phase % 2
            for d in (1, 2, 3):
                for other in (dev(ya(d), z, c), dev(y, za(d), c)):
                    pl.semaphore_signal(
                        free_sem.at[g], inc=1, device_id={"seq": other}, device_id_type=MESH
                    )
            for h in (2 * g, 2 * g + 1):

                @pl.when(me != HOT_AT[h])
                def _():
                    hot_copy(h).wait_send()

    def back_start(h):
        for s in range(PEERS):
            if s != HOT_AT[h]:
                back_copy(h, s).start()
        back_own(h).start()

    def back_drain(g):
        for h in (2 * g, 2 * g + 1):

            @pl.when(me == HOT_AT[h])
            def _():
                for s in range(PEERS):
                    if s != HOT_AT[h]:
                        back_copy(h, s).wait_send()

    def hot_arrive(h):
        for s in range(PEERS):
            if s != HOT_AT[h]:
                hot_from(h, s).wait_recv()
        hot_own(h).wait()

    def back_arrive(g):
        for h in (2 * g, 2 * g + 1):

            @pl.when(me != HOT_AT[h])
            def _():
                back_copy(h, 0).wait_recv()

            @pl.when(me == HOT_AT[h])
            def _():
                back_own(h).wait()

    def picked(shape, at, first):
        index = iota(shape, 0)
        return (index // 32 * (2 * ROWS) + lax.rem(index, 32) == at - first).astype(F32).astype(BF16)

    def pack(g, core):
        a, b = pos_row[2 * g : 2 * g + 1, :], pos_row[2 * g + 1 : 2 * g + 2, :]

        shape = (4, 4, 32, 512)
        first = core * ROWS
        p = picked((512, 1024), a, first)
        send[g, :, :, core, 0:32, :] = dot(p, x[2 * g]).astype(BF16).reshape(shape)
        p = picked((512, 1024), b, first + 64)
        send[g, :, :, core, 64:96, :] = dot(p, x[2 * g + 1]).astype(BF16).reshape(shape)
        p = picked((512, 1024), a, first + 32)
        t = dot(p, x[2 * g])
        p = picked((512, 1024), b, first + 32)
        t = t + dot(p, x[2 * g + 1])
        send[g, :, :, core, 32:64, :] = t.astype(BF16).reshape(shape)

    def pack_hot(g):
        a, b = pos_row[2 * g : 2 * g + 1, :], pos_row[2 * g + 1 : 2 * g + 2, :]
        for k, at in ((0, a), (1, b)):
            pick = (iota((32, 1024), 0) + (SPAN + k * 32) == at).astype(F32).astype(BF16)
            send_hot[g, k * 32 : k * 32 + 32] = dot(pick, x[2 * g + k]).astype(BF16)

    def unpack(g, core, last):
        def body(m, _):
            t = pl.ds(pl.multiple_of(m * 512, 512), 512)
            for k in (0, 1):
                at = pos_col[t, 2 * g + k : 2 * g + k + 1]
                pick = (iota((512, 1024), 1) == at - core * 1024).astype(F32).astype(BF16)
                got = ret[g, :, :, core, k * 32 : k * 32 + 64, :].reshape(1024, 512)
                got = dot(pick, got)
                kept = pl.ds(pl.multiple_of(k * 1024 + m * 512, 512), 512)
                if last:
                    x[2 * g + k, t, :] = (p_buf[kept, :] + got).astype(BF16)
                else:
                    hot_pick = (iota((512, 64), 1) + WINDOWS == at).astype(F32).astype(BF16)
                    p_buf[kept, :] = got + dot(hot_pick, ret_hot[g])
            return 0

        lax.fori_loop(0, 2, body, 0)

    def attend(rows_ref, span, coded, between):
        def after(j):
            return pl.ds(pl.multiple_of(SPAN + j * TK, TK), TK)

        def body(i, _):
            between(i)
            qs = pl.ds(pl.multiple_of(i * TQ, TQ), TQ)
            q_i = rows_ref[qs, 0:128]
            d_i = rows_ref[qs, 384:512]
            q_a = jnp.concatenate([q_i, aug_q[qs, :]], axis=1) if coded else q_i
            full_tiles = (i * TQ) // TK

            def weigh(j, sums, edge):
                top, total, delta = sums
                ks = pl.ds(pl.multiple_of(j * TK, TK), TK)
                k_j = rows_ref[ks, 128:256]
                if coded:
                    k_j = jnp.concatenate([k_j, aug_k[ks, :]], axis=1)
                s = dot(k_j, q_a, ((1,), (1,)))
                if edge:
                    gap = iota((TK, TQ), 0) - iota((TK, TQ), 1)
                    s = jnp.where(gap <= i * TQ - j * TK, s, -1e30)
                new = jnp.maximum(top, jnp.max(s, axis=0, keepdims=True))
                p = jnp.exp2((s - new) * to_exp2)
                dp = dot(rows_ref[ks, 256:384], d_i, ((1,), (1,)))
                p_buf[ks, :] = p
                dp_buf[ks, :] = dp
                tops[pl.ds(pl.multiple_of(j * 8, 8), 8), :] = jnp.broadcast_to(new, (8, TQ))
                keep = jnp.exp2((top - new) * to_exp2)
                return (
                    new,
                    total * keep + jnp.sum(p, axis=0, keepdims=True),
                    delta * keep + jnp.sum(p * dp, axis=0, keepdims=True),
                )

            none = jnp.zeros((1, TQ), F32)
            sums = (jnp.full((1, TQ), -1e30, F32), none, none)
            sums = lax.fori_loop(0, full_tiles, lambda j, a: weigh(j, a, False), sums)
            top, total, delta = weigh(full_tiles, sums, True)
            inv = 1.0 / total
            delta = delta * inv
            acc_o[...] = jnp.zeros_like(acc_o)
            acc_q[...] = jnp.zeros_like(acc_q)

            def spread(j, _):
                ks = pl.ds(pl.multiple_of(j * TK, TK), TK)
                here = tops[pl.ds(pl.multiple_of(j * 8, 8), 8), :][:1]
                w = p_buf[ks, :] * (jnp.exp2((here - top) * to_exp2) * inv)
                rounded = w.astype(BF16)
                ds = (w * (dp_buf[ks, :] - delta)).astype(BF16)
                acc_o[...] += dot(vt[:, ks], rounded)
                acc_q[...] += dot(kt[:, ks], ds)
                dkv[ks, :] += dot(ds, q_i)
                dkv[after(j), :] += dot(rounded, d_i)
                return 0

            lax.fori_loop(0, full_tiles + 1, spread, 0)
            rows_ref[qs, 0:128] = acc_o[...].T.astype(BF16)
            rows_ref[qs, 384:512] = (acc_q[...] * scale).T.astype(BF16)
            return 0

        def ready(j, _):
            ks = pl.ds(pl.multiple_of(j * TK, TK), TK)
            kt[:, ks] = rows_ref[ks, 128:256].astype(F32).T.astype(BF16)
            vt[:, ks] = rows_ref[ks, 256:384].astype(F32).T.astype(BF16)
            dkv[ks, :] = jnp.zeros((TK, 128), F32)
            dkv[after(j), :] = jnp.zeros((TK, 128), F32)
            return 0

        lax.fori_loop(0, span // TK, ready, 0)
        lax.fori_loop(0, span // TQ, body, 0)

        def finish(j, _):
            ks = pl.ds(pl.multiple_of(j * TK, TK), TK)
            rows_ref[ks, 128:256] = (dkv[ks, :] * scale).astype(BF16)
            rows_ref[ks, 256:384] = dkv[after(j), :].astype(BF16)
            return 0

        lax.fori_loop(0, span // TK, finish, 0)

    def codes(g):
        def body(s, _):
            note = meta_in[pl.ds(pl.multiple_of(s * 16, 16), 16), :].astype(F32)
            r = iota((ROWS, 128), 0).astype(F32)
            inside = (r >= note[2 * g : 2 * g + 1]) & (r < note[2 * g + 1 : 2 * g + 2])
            known = iota((ROWS, 128), 1) <= 4
            at = pl.ds(pl.multiple_of(s * ROWS, ROWS), ROWS)
            aug_q[at, :] = jnp.where(inside, 1.0, 0.0).astype(BF16)
            aug_k[at, :] = jnp.where(known & ~inside, -FAR, 0.0).astype(BF16)
            return 0

        lax.fori_loop(0, PEERS, body, 0)

    def hot_work():
        for h in range(4):

            @pl.when(me == HOT_AT[h])
            def _():
                hot_arrive(h)

        @pl.when((me == HOT_AT[0]) | (me == HOT_AT[1]) | (me == HOT_AT[2]) | (me == HOT_AT[3]))
        def _():
            attend(recv_hot, HOT_ROWS, False, lambda i: None)

        for h in range(4):

            @pl.when(me == HOT_AT[h])
            def _():
                back_start(h)

    def work(g, between):
        def load(yy, _):
            at = pl.ds(pl.multiple_of(yy * 768, 768), 768)
            rows_buf[at, :] = recv[g, yy].reshape(768, 512)
            return 0

        def store(yy, _):
            at = pl.ds(pl.multiple_of(yy * 768, 768), 768)
            recv[g, yy] = rows_buf[at, :].reshape(4, 2, ROWS, 512)
            return 0

        lax.fori_loop(0, 4, load, 0)
        attend(rows_buf, SPAN, True, between)
        lax.fori_loop(0, 4, store, 0)

    def ahead(phase, blocks):
        def between(i):
            for e in (0, 1):

                @pl.when(i == blocks[e])
                def _():
                    start_two(phase, e)

        return between

    pack(0, c)
    pl.semaphore_wait(barrier, PEERS - 1 + 3)
    start_one(0, 0)
    pack(0, 1 - c)
    start_one(0, 1)
    pack_hot(0)
    hot_start(0)
    for k in range(1, PEERS):
        meta_copy(k).start()
    own_meta = pl.ds(pl.multiple_of(me * 16, 16), 16)
    meta_in[own_meta, :] = meta[own_meta, :]
    start_two(0, 0)
    pack(1, c)
    start_two(0, 1)
    start_one(1, 0)
    pack(1, 1 - c)
    start_one(1, 1)
    pack_hot(1)
    hot_start(1)

    for k in range(1, PEERS):
        meta_copy(k).wait()
    noted = meta_in[...].astype(F32)
    noted = jnp.where(lax.rem(iota((512, 128), 0), 16) == 4, noted, 0.0)
    flags[0] = jnp.broadcast_to(jnp.max(noted, axis=0, keepdims=True), (16, 128)).astype(BF16)

    def flag_copy(step):
        return pltpu.make_async_remote_copy(
            src_ref=flags.at[0],
            dst_ref=flags.at[step],
            send_sem=flag_ssem.at[step],
            recv_sem=flag_rsem.at[step],
            device_id={"head": lax.rem(col + step, 4)},
            device_id_type=MESH,
        )

    for step in (1, 2, 3):
        flag_copy(step).start()

    codes(0)
    hot_work()
    arrive(0, 0)
    arrive(0, 1)
    drain(0)
    work(0, ahead(1, SWITCH[0]))
    start_one(2, 0)
    start_one(2, 1)
    codes(1)
    arrive(1, 0)
    arrive(1, 1)
    drain(1)
    work(1, ahead(2, SWITCH[1]))
    start_one(3, 0)
    start_one(3, 1)
    arrive(2, 0)
    arrive(2, 1)
    start_two(3, 0)
    back_arrive(0)
    unpack(0, c, False)
    start_two(3, 1)
    unpack(0, 1 - c, True)
    for step in (1, 2, 3):
        flag_copy(step).wait()
    any_flag = jnp.maximum(
        jnp.maximum(flags[0].astype(F32), flags[1].astype(F32)),
        jnp.maximum(flags[2].astype(F32), flags[3].astype(F32)),
    )
    flag_out[...] = any_flag[:8]
    drain(2)
    back_drain(0)
    back_arrive(1)
    arrive(3, 0)
    unpack(1, c, False)
    arrive(3, 1)
    unpack(1, 1 - c, True)
    drain(3)
    back_drain(1)


def settle_kernel(x, o_q, o_k, o_v, o_d, held, wide, done, in_sem, out_sem):
    def load(m):
        return pltpu.make_async_copy(x.at[:, pl.ds(m * 256, 256)], held.at[m], in_sem.at[m])

    outs = ((0, o_q), (3, o_k), (1, o_v), (2, o_d))

    def save(m, n):
        at = pl.ds(m * 1024, 1024)
        return pltpu.make_async_copy(done.at[n, at], outs[n][1].at[at], out_sem.at[m, n])

    for m in range(4):
        load(m).start()
    for m in range(4):
        load(m).wait()
        for n, (a, _) in enumerate(outs):
            for h in range(4):
                wide[n, pl.ds(h, 256, stride=4), :] = held[m, h, :, a * 128 : a * 128 + 128].astype(
                    F32
                )
            done[n, m * 1024 : m * 1024 + 1024, :] = wide[n].astype(BF16)
            save(m, n).start()
    for m in range(4):
        for n in range(4):
            save(m, n).wait()


def settle(x):
    outs = pl.pallas_call(
        settle_kernel,
        out_shape=[jax.ShapeDtypeStruct((4096, 128), BF16)] * 4,
        in_specs=[pl.BlockSpec(memory_space=pl.ANY)],
        out_specs=[pl.BlockSpec(memory_space=pl.ANY)] * 4,
        scratch_shapes=[
            pltpu.VMEM((4, 4, 256, 512), BF16),
            pltpu.VMEM((4, 1024, 128), F32),
            pltpu.VMEM((4, 4096, 128), BF16),
            pltpu.SemaphoreType.DMA((4,)),
            pltpu.SemaphoreType.DMA((4, 4)),
        ],
        compiler_params=pltpu.CompilerParams(vmem_limit_bytes=32 * 2**20),
        name="settle",
    )(x)
    return tuple(a.reshape(1024, 4, 128) for a in outs)


def quick(queries, key_rows, value_rows, out_grad, bucket_id):
    rows = [a.reshape(4096, 128) for a in (queries, key_rows, value_rows, out_grad)]
    vmem = pl.BlockSpec(memory_space=pltpu.VMEM)
    dma = pltpu.SemaphoreType.DMA
    outs = pl.pallas_call(
        kernel,
        out_shape=[
            jax.ShapeDtypeStruct((4, 1024, 512), BF16),
            jax.ShapeDtypeStruct((8, 128), F32),
        ],
        in_specs=[pl.BlockSpec(memory_space=pl.ANY)] * 4 + [vmem],
        out_specs=[vmem] * 2,
        scratch_shapes=[
            pltpu.VMEM((2, 4, 4, 2, ROWS, 512), BF16),
            pltpu.VMEM((2, 64, 512), BF16),
            pltpu.VMEM((2, 4, 4, 2, ROWS, 512), BF16),
            pltpu.VMEM((HOT_ROWS, 512), BF16),
            pltpu.VMEM((2, 4, 4, 2, ROWS, 512), BF16),
            pltpu.VMEM((2, 64, 512), BF16),
            pltpu.VMEM((2, 2, 4, 4, 2, HALF, 512), BF16),
            pltpu.VMEM((SPAN, 512), BF16),
            pltpu.VMEM((512, 128), BF16),
            pltpu.VMEM((512, 128), BF16),
            pltpu.VMEM((4, 16, 128), BF16),
            pltpu.VMEM((8, 1024), I32),
            pltpu.VMEM((1024, 128), I32),
            pltpu.VMEM((SPAN, 128), BF16),
            pltpu.VMEM((SPAN, 128), BF16),
            pltpu.VMEM((128, SPAN), BF16),
            pltpu.VMEM((128, SPAN), BF16),
            pltpu.VMEM((2 * SPAN, 128), F32),
            pltpu.VMEM((SPAN, TQ), F32),
            pltpu.VMEM((SPAN, TQ), F32),
            pltpu.VMEM((SPAN // TK * 8, TQ), F32),
            pltpu.VMEM((128, TQ), F32),
            pltpu.VMEM((128, TQ), F32),
            dma((4, 2, 8)), dma((4, 2, 8)), dma((4, 2, 8)), dma((4, 2, 8)), dma((4, 2, 2)),
            pltpu.SemaphoreType.REGULAR((2,)), dma((PEERS,)), dma((PEERS,)),
            dma((4,)), dma((PEERS,)), dma((PEERS,)), dma((4,)), dma((4,)), dma((4,)),
            dma((4, 4)),
        ],
        compiler_params=pltpu.CompilerParams(
            collective_id=0, has_side_effects=True, vmem_limit_bytes=60 * 2**20
        ),
        name="bucket_layer",
    )(*rows, bucket_id.T)
    return outs[0], outs[1][0, 0] > 0


def bucket_weights(q_part, k_part, valid, scale):
    span = q_part.shape[0]
    sorted_index = jnp.arange(span, dtype=I32)
    allowed = (sorted_index[None, :] <= sorted_index[:, None]) & (
        (valid[None, :] > 0) | (sorted_index[None, :] == sorted_index[:, None])
    )
    scores = jnp.dot(q_part, k_part.T, preferred_element_type=F32) * scale
    scores = jnp.where(allowed, scores, F32(-1e30))
    top = jnp.max(scores, axis=1, keepdims=True)
    expd = jnp.where(allowed, jnp.exp(scores - top), F32(0.0))
    return expd / jnp.sum(expd, axis=1, keepdims=True)


def bucket_forward(block, valid, width):
    scale = 1.0 / math.sqrt(width)
    weights = bucket_weights(block[:, :width], block[:, width : 2 * width], valid, scale)
    rounded = weights.astype(BF16)
    return jnp.dot(rounded, block[:, 2 * width :], preferred_element_type=F32).astype(
        BF16
    )


def bucket_backward(block, d_part, valid, width):
    scale = 1.0 / math.sqrt(width)
    q_part = block[:, :width]
    k_part = block[:, width : 2 * width]
    v_part = block[:, 2 * width : 3 * width]
    weights = bucket_weights(q_part, k_part, valid, scale)
    rounded = weights.astype(BF16)
    dprob = jnp.dot(d_part, v_part.T, preferred_element_type=F32)
    delta = jnp.sum(weights * dprob, axis=1, keepdims=True)
    dscore = (weights * (dprob - delta)).astype(BF16)
    grad_q = (jnp.dot(dscore, k_part, preferred_element_type=F32) * scale).astype(
        BF16
    )
    grad_k = (jnp.dot(dscore.T, q_part, preferred_element_type=F32) * scale).astype(
        BF16
    )
    grad_v = jnp.dot(rounded.T, d_part, preferred_element_type=F32).astype(BF16)
    return (rounded, v_part, grad_q, grad_k, grad_v)


def bucket_grads(block, d_part, valid, width):
    rounded, v_part, grad_q, grad_k, grad_v = bucket_backward(block, d_part, valid, width)
    return jnp.concatenate([grad_q, grad_k, grad_v], axis=1)


def slow(queries, key_rows, value_rows, out_grad, bucket_id, bucket_slot):
    peers = lax.axis_size("seq")
    tok_count, group, width = queries.shape
    per_owner = BUCKETS_PER_HEAD // peers
    span = peers * SLOTS_PER_SOURCE
    total = group * per_owner * span
    owner = bucket_id // per_owner
    local_bucket = bucket_id % per_owner
    head_index = jnp.arange(group, dtype=I32)[None, :]
    flat = (
        (head_index * per_owner + local_bucket) * span + owner * SLOTS_PER_SOURCE + bucket_slot
    ).reshape(-1)
    marks = (
        jnp.zeros((total,), BF16)
        .at[flat]
        .set(BF16(1.0))
        .reshape(group, per_owner, span)
    )

    def spread(rows):
        columns = rows.shape[-1]
        placed = jnp.zeros((total, columns), rows.dtype).at[flat].set(rows.reshape(-1, columns))
        return placed.reshape(group, per_owner, span, columns)

    def collect(buffer):
        columns = buffer.shape[-1]
        return buffer.reshape(total, columns)[flat].reshape(tok_count, group, columns)

    joined = jnp.concatenate([queries, key_rows, value_rows], axis=2)
    blocks, valid = (
        lax.all_to_all(spread(joined), "seq", split_axis=2, concat_axis=2, tiled=True),
        lax.all_to_all(marks, "seq", split_axis=2, concat_axis=2, tiled=True),
    )
    flat_blocks = blocks.reshape(-1, span, 3 * width)
    flat_valid = valid.reshape(-1, span)
    attended = lax.map(
        lambda item: bucket_forward(item[0], item[1], width), (flat_blocks, flat_valid)
    )
    attended = lax.all_to_all(
        attended.reshape(group, per_owner, span, width),
        "seq",
        split_axis=2,
        concat_axis=2,
        tiled=True,
    )
    incoming = lax.all_to_all(spread(out_grad), "seq", split_axis=2, concat_axis=2, tiled=True)
    grads = lax.map(
        lambda item: bucket_grads(item[0], item[1], item[2], width),
        (flat_blocks, incoming.reshape(-1, span, width), flat_valid),
    )
    grads = lax.all_to_all(
        grads.reshape(group, per_owner, span, 3 * width),
        "seq",
        split_axis=2,
        concat_axis=2,
        tiled=True,
    )
    gathered = collect(grads)
    return (
        collect(attended),
        gathered[:, :, :width],
        gathered[:, :, width : 2 * width],
        gathered[:, :, 2 * width :],
    )


def shards(queries, key_rows, value_rows, out_grad, bucket_id, bucket_slot):
    packed, crowded = quick(queries, key_rows, value_rows, out_grad, bucket_id)
    return lax.cond(
        crowded,
        lambda: slow(queries, key_rows, value_rows, out_grad, bucket_id, bucket_slot),
        lambda: settle(packed),
    )


def solution(mesh):
    in_specs = (
        P("seq", "head", None),
        P("seq", "head", None),
        P("seq", "head", None),
        P("seq", "head", None),
        P("seq", "head"),
        P("seq", "head"),
    )
    out_specs = (
        P("seq", "head", None),
        P("seq", "head", None),
        P("seq", "head", None),
        P("seq", "head", None),
    )
    return jax.shard_map(shards, mesh=mesh, in_specs=in_specs, out_specs=out_specs, check_vma=False)
```

```python
import functools
import math

import jax
import jax.numpy as jnp
from jax import lax
from jax.experimental import pallas as pl
from jax.experimental.pallas import tpu as pltpu
from jax.sharding import PartitionSpec as P

SLOTS_PER_SOURCE = 32
BUCKETS_PER_HEAD = 64
PEERS = 32
ROWS = 96
SPAN = PEERS * ROWS
HOT_ROWS = PEERS * SLOTS_PER_SOURCE
HOT_AT = (0, 10, 20, 30)
TQ, TK = 512, 512
HALF = ROWS // 2
WINDOWS = PEERS * 64
SECOND = (((2, 0), (1, 0), (3, 0)), ((2, 1), (1, 1), (3, 1), (0, 1)))
SWITCH = ((3, 4), (3, 4))
FAR = 2.0**100
MESH = pl.DeviceIdType.MESH
F32, BF16, I32 = jnp.float32, jnp.bfloat16, jnp.int32


def iota(shape, dim):
    return lax.broadcasted_iota(I32, shape, dim)


def dot(a, b, dims=((1,), (0,))):
    return lax.dot_general(a, b, (dims, ((), ())), preferred_element_type=F32)


def kernel(
    q_ref, k_ref, v_ref, d_ref, bid_ref,
    x, flag_out,
    send, send_hot, recv, recv_hot, ret, ret_hot, mid, rows_buf, meta, meta_in, flags,
    pos_row, pos_col, aug_q, aug_k, kt, vt, dkv, p_buf, dp_buf, tops, acc_o, acc_q,
    one_ssem, one_rsem, two_ssem, two_rsem, own_sem, free_sem, meta_ssem, meta_rsem,
    hot_ssem, hot_rsem, back_ssem, back_rsem, flag_ssem, flag_rsem, in_sem,
):
    me = lax.axis_index("seq")
    col = lax.axis_index("head")
    y, z, c = me // 8, lax.rem(me // 2, 4), lax.rem(me, 2)
    scale = 1.0 / math.sqrt(128)
    to_exp2 = scale * math.log2(math.e)

    def ya(d):
        return lax.rem(y + d, 4)

    def za(d):
        return lax.rem(z + d, 4)

    def dev(yy, zz, cc):
        return yy * 8 + zz * 2 + cc

    barrier = pltpu.get_barrier_semaphore()
    for k in range(1, PEERS):
        pl.semaphore_signal(
            barrier, inc=1, device_id={"seq": lax.rem(me + k, PEERS)}, device_id_type=MESH
        )
    for step in (1, 2, 3):
        pl.semaphore_signal(
            barrier, inc=1, device_id={"head": lax.rem(col + step, 4)}, device_id_type=MESH
        )

    inputs = (q_ref, k_ref, v_ref, d_ref)
    quarters = range(4)

    def load(a, part):
        return pltpu.make_async_copy(
            inputs[a].at[pl.ds(part * 1024, 1024)],
            rows_buf.at[pl.ds(a % 3 * 1024, 1024), pl.ds(part * 128, 128)],
            in_sem.at[a, part],
        )

    for a in range(3):
        for part in quarters:
            load(a, part).start()
    for a in range(4):
        for part in quarters:
            load(a, part).wait()
            dkv[part * 1024 : part * 1024 + 1024, :] = rows_buf[
                a % 3 * 1024 : a % 3 * 1024 + 1024, part * 128 : part * 128 + 128
            ].astype(F32)
        if a == 0:
            for part in quarters:
                load(3, part).start()
        for h in range(4):
            x[h, :, a * 128 : a * 128 + 128] = dkv[pl.ds(h, 1024, stride=4), :].astype(BF16)

    named = jnp.concatenate(
        [(iota((64, 1024), 0) == bid_ref[h : h + 1, :]).astype(F32) for h in range(4)], axis=0
    )
    named16 = named.astype(BF16)
    ranks = []
    for part in quarters:
        earlier = iota((1024, 256), 0) < iota((1024, 256), 1) + part * 256
        ranks.append(dot(named16, earlier.astype(F32).astype(BF16)))
    rank = jnp.concatenate(ranks, axis=1)
    count = jnp.sum(named, axis=1, keepdims=True)
    full = (count == 32.0).astype(F32)
    count = count * (1.0 - full)
    bad = jnp.float32(0.0)
    for h in range(4):
        n_full = jnp.sum(full[h * 64 : h * 64 + 64])
        bad = jnp.maximum(bad, (n_full != 1.0).astype(F32))
    r0, r1 = iota((256, 256), 0), iota((256, 256), 1)
    alike = r0 // 2 == r1 // 2
    lanes = jnp.broadcast_to(count, (256, 128))
    lanes16 = lanes.astype(BF16)
    start = dot((alike & (r1 < r0)).astype(F32).astype(BF16), lanes16)[:, :1]
    both = dot(alike.astype(F32).astype(BF16), lanes16)[:, :1]
    rows = iota((256, 1), 0)
    owner = lax.rem(rows, 64) // 2
    second = lax.rem(rows // 64, 2)
    inside = start + jnp.where(second == 1, ROWS - both, 0.0)
    at_hot = (second * 32).astype(F32)
    base = jnp.where(full > 0, SPAN + at_hot, (owner * ROWS).astype(F32) + inside)
    back = jnp.where(full > 0, WINDOWS + at_hot, (lax.rem(owner, 2) * 1024 + owner // 2 * 64 - second * 32).astype(F32) + inside)

    def per_head(table):
        landed = named * (rank + table)
        return jnp.concatenate(
            [jnp.sum(landed[h * 64 : h * 64 + 64], axis=0, keepdims=True) for h in range(4)],
            axis=0,
        )

    pos_row[0:4, :] = per_head(base).astype(I32)
    place = jnp.concatenate([per_head(back), jnp.zeros((124, 1024), F32)], axis=0)
    pos_col[...] = place.T.astype(I32)

    lane, r2 = iota((256, 128), 1), iota((256, 128), 0)
    code = lax.rem(r2 // 64, 2) * 2 + lax.rem(r2, 2)
    front, rear = code < 2, code >= 2
    low = (lane < 2) | (lane == 4)
    high = (lane == 2) | (lane == 3)
    w_start = jnp.where((low & front & (code < lane)) | (lane == 5), lanes, 0.0)
    w_start = w_start - jnp.where(high & rear & (code >= lane), lanes, 0.0)
    w_end = jnp.where((lane < 2) & front & (code <= lane), lanes, 0.0)
    w_end = w_end - jnp.where((high & (code > lane)) | (lane == 4) & rear, lanes, 0.0)
    mr, mc = iota((512, 256), 0), iota((512, 256), 1)
    mine = mr // 16 == lax.rem(mc, 64) // 2
    pick_start = (mine & (lax.rem(mr, 16) == mc // 128 * 2)).astype(F32).astype(BF16)
    pick_end = (mine & (lax.rem(mr, 16) == mc // 128 * 2 + 1)).astype(F32).astype(BF16)
    starts = dot(pick_start, w_start.astype(BF16))
    kind, ml = lax.rem(iota((512, 128), 0), 16), iota((512, 128), 1)
    bad = jnp.maximum(bad, (jnp.max(jnp.where(ml == 5, starts, 0.0)) > ROWS).astype(F32))
    high = (ml == 2) | (ml == 3)
    to_rows = ((kind == 0) | (kind == 2)) & high
    to_rows = to_rows | ((kind == 1) | (kind == 3)) & (high | (ml == 4))
    tail = jnp.where(to_rows, jnp.float32(ROWS), 0.0) + jnp.where(kind == 4, bad, 0.0)
    meta[...] = (starts + dot(pick_end, w_end.astype(BF16)) + tail).astype(BF16)

    def meta_copy(k):
        other = lax.rem(me + k, PEERS)
        return pltpu.make_async_remote_copy(
            src_ref=meta.at[pl.ds(pl.multiple_of(other * 16, 16), 16)],
            dst_ref=meta_in.at[pl.ds(pl.multiple_of(me * 16, 16), 16)],
            send_sem=meta_ssem.at[k],
            recv_sem=meta_rsem.at[k],
            device_id={"seq": other},
            device_id_type=MESH,
        )

    def ends(phase):
        return (send, recv) if phase < 2 else (recv, ret)

    def one(phase, half, d, e):
        g, src, cc = phase % 2, ends(phase)[0], lax.rem(c + e, 2)
        if half == 0:
            from_, to = src.at[g, ya(d), :, cc, 0:HALF], mid.at[g, 0, y, :, cc]
            other = dev(ya(d), z, c)
        else:
            from_, to = src.at[g, :, za(d), cc, HALF:ROWS], mid.at[g, 1, z, :, cc]
            other = dev(y, za(d), c)
        return pltpu.make_async_remote_copy(
            src_ref=from_,
            dst_ref=to,
            send_sem=one_ssem.at[phase, half, d * 2 + e],
            recv_sem=one_rsem.at[phase, half, d * 2 + e],
            device_id={"seq": other},
            device_id_type=MESH,
        )

    def one_own(phase, half):
        g, src = phase % 2, ends(phase)[0]
        sem = own_sem.at[phase, half, 0]
        if half == 0:
            return pltpu.make_async_copy(src.at[g, y, :, :, 0:HALF], mid.at[g, 0, y], sem)
        return pltpu.make_async_copy(src.at[g, :, z, :, HALF:ROWS], mid.at[g, 1, z], sem)

    def two(phase, half, d, e):
        g, dst = phase % 2, ends(phase)[1]
        cc = lax.rem(c + e, 2)
        if half == 0:
            from_, to = mid.at[g, 0, :, za(d), cc], dst.at[g, :, z, c, 0:HALF]
            other = dev(y, za(d), cc)
        else:
            from_, to = mid.at[g, 1, :, ya(d), cc], dst.at[g, y, :, c, HALF:ROWS]
            other = dev(ya(d), z, cc)
        return pltpu.make_async_remote_copy(
            src_ref=from_,
            dst_ref=to,
            send_sem=two_ssem.at[phase, half, d * 2 + e],
            recv_sem=two_rsem.at[phase, half, d * 2 + e],
            device_id={"seq": other},
            device_id_type=MESH,
        )

    def two_own(phase, half):
        g, dst = phase % 2, ends(phase)[1]
        sem = own_sem.at[phase, half, 1]
        if half == 0:
            return pltpu.make_async_copy(mid.at[g, 0, :, z, c], dst.at[g, :, z, c, 0:HALF], sem)
        return pltpu.make_async_copy(mid.at[g, 1, :, y, c], dst.at[g, y, :, c, HALF:ROWS], sem)

    def hot_copy(h):
        return pltpu.make_async_remote_copy(
            src_ref=send_hot.at[h // 2, pl.ds(h % 2 * 32, 32)],
            dst_ref=recv_hot.at[pl.ds(pl.multiple_of(me * 32, 32), 32)],
            send_sem=hot_ssem.at[h],
            recv_sem=hot_rsem.at[me],
            device_id={"seq": HOT_AT[h]},
            device_id_type=MESH,
        )

    def hot_from(h, s):
        return pltpu.make_async_remote_copy(
            src_ref=send_hot.at[h // 2, pl.ds(h % 2 * 32, 32)],
            dst_ref=recv_hot.at[pl.ds(s * 32, 32)],
            send_sem=hot_ssem.at[h],
            recv_sem=hot_rsem.at[s],
            device_id={"seq": HOT_AT[h]},
            device_id_type=MESH,
        )

    def hot_own(h):
        return pltpu.make_async_copy(
            send_hot.at[h // 2, pl.ds(h % 2 * 32, 32)],
            recv_hot.at[pl.ds(HOT_AT[h] * 32, 32)],
            hot_ssem.at[h],
        )

    def back_copy(h, s):
        return pltpu.make_async_remote_copy(
            src_ref=recv_hot.at[pl.ds(s * 32, 32)],
            dst_ref=ret_hot.at[h // 2, pl.ds(h % 2 * 32, 32)],
            send_sem=back_ssem.at[s],
            recv_sem=back_rsem.at[h],
            device_id={"seq": s},
            device_id_type=MESH,
        )

    def back_own(h):
        return pltpu.make_async_copy(
            recv_hot.at[pl.ds(HOT_AT[h] * 32, 32)],
            ret_hot.at[h // 2, pl.ds(h % 2 * 32, 32)],
            back_rsem.at[h],
        )

    def start_one(phase, e):
        if phase >= 2 and e == 0:
            pl.semaphore_wait(free_sem.at[phase % 2], 6)
        for d in (2, 1, 3):
            for half in (0, 1):
                one(phase, half, d, e).start()
        if e == 1:
            for half in (0, 1):
                one_own(phase, half).start()

    def hot_start(g):
        for h in (2 * g, 2 * g + 1):

            @pl.when(me != HOT_AT[h])
            def _():
                hot_copy(h).start()

            @pl.when(me == HOT_AT[h])
            def _():
                hot_own(h).start()

    def start_two(phase, e):
        for half in (0, 1):
            for d in (1, 2, 3):
                one(phase, half, d, e).wait_recv()
            if e == 0:
                one_own(phase, half).wait()
        for d, _ in SECOND[e]:
            for half in (0, 1):
                two(phase, half, d, e).start()
        if e == 0:
            for half in (0, 1):
                two_own(phase, half).start()

    def arrive(phase, e):
        for half in (0, 1):
            for d, _ in SECOND[e]:
                two(phase, half, d, e).wait_recv()
            if e == 0:
                two_own(phase, half).wait()

    def drain(phase):
        for half in (0, 1):
            for d in (1, 2, 3):
                for e in (0, 1):
                    one(phase, half, d, e).wait_send()
            for d, e in SECOND[0] + SECOND[1]:
                two(phase, half, d, e).wait_send()
        if phase < 2:
            g = phase % 2
            for d in (1, 2, 3):
                for other in (dev(ya(d), z, c), dev(y, za(d), c)):
                    pl.semaphore_signal(
                        free_sem.at[g], inc=1, device_id={"seq": other}, device_id_type=MESH
                    )
            for h in (2 * g, 2 * g + 1):

                @pl.when(me != HOT_AT[h])
                def _():
                    hot_copy(h).wait_send()

    def back_start(h):
        for s in range(PEERS):
            if s != HOT_AT[h]:
                back_copy(h, s).start()
        back_own(h).start()

    def back_drain(g):
        for h in (2 * g, 2 * g + 1):

            @pl.when(me == HOT_AT[h])
            def _():
                for s in range(PEERS):
                    if s != HOT_AT[h]:
                        back_copy(h, s).wait_send()

    def hot_arrive(h):
        for s in range(PEERS):
            if s != HOT_AT[h]:
                hot_from(h, s).wait_recv()
        hot_own(h).wait()

    def back_arrive(g):
        for h in (2 * g, 2 * g + 1):

            @pl.when(me != HOT_AT[h])
            def _():
                back_copy(h, 0).wait_recv()

            @pl.when(me == HOT_AT[h])
            def _():
                back_own(h).wait()

    def picked(shape, at, first):
        index = iota(shape, 0)
        return (index // 32 * (2 * ROWS) + lax.rem(index, 32) == at - first).astype(F32).astype(BF16)

    def pack(g, core):
        a, b = pos_row[2 * g : 2 * g + 1, :], pos_row[2 * g + 1 : 2 * g + 2, :]

        shape = (4, 4, 32, 512)
        first = core * ROWS
        p = picked((512, 1024), a, first)
        send[g, :, :, core, 0:32, :] = dot(p, x[2 * g]).astype(BF16).reshape(shape)
        p = picked((512, 1024), b, first + 64)
        send[g, :, :, core, 64:96, :] = dot(p, x[2 * g + 1]).astype(BF16).reshape(shape)
        p = picked((512, 1024), a, first + 32)
        t = dot(p, x[2 * g])
        p = picked((512, 1024), b, first + 32)
        t = t + dot(p, x[2 * g + 1])
        send[g, :, :, core, 32:64, :] = t.astype(BF16).reshape(shape)

    def pack_hot(g):
        a, b = pos_row[2 * g : 2 * g + 1, :], pos_row[2 * g + 1 : 2 * g + 2, :]
        for k, at in ((0, a), (1, b)):
            pick = (iota((32, 1024), 0) + (SPAN + k * 32) == at).astype(F32).astype(BF16)
            send_hot[g, k * 32 : k * 32 + 32] = dot(pick, x[2 * g + k]).astype(BF16)

    def unpack(g, core, last):
        def body(m, _):
            t = pl.ds(pl.multiple_of(m * 512, 512), 512)
            for k in (0, 1):
                at = pos_col[t, 2 * g + k : 2 * g + k + 1]
                pick = (iota((512, 1024), 1) == at - core * 1024).astype(F32).astype(BF16)
                got = ret[g, :, :, core, k * 32 : k * 32 + 64, :].reshape(1024, 512)
                got = dot(pick, got)
                kept = pl.ds(pl.multiple_of(k * 1024 + m * 512, 512), 512)
                if last:
                    x[2 * g + k, t, :] = (p_buf[kept, :] + got).astype(BF16)
                else:
                    hot_pick = (iota((512, 64), 1) + WINDOWS == at).astype(F32).astype(BF16)
                    p_buf[kept, :] = got + dot(hot_pick, ret_hot[g])
            return 0

        lax.fori_loop(0, 2, body, 0)

    def attend(rows_ref, span, coded, between):
        def after(j):
            return pl.ds(pl.multiple_of(SPAN + j * TK, TK), TK)

        def body(i, _):
            between(i)
            qs = pl.ds(pl.multiple_of(i * TQ, TQ), TQ)
            q_i = rows_ref[qs, 0:128]
            d_i = rows_ref[qs, 384:512]
            q_a = jnp.concatenate([q_i, aug_q[qs, :]], axis=1) if coded else q_i
            full_tiles = (i * TQ) // TK

            def weigh(j, sums, edge):
                top, total, delta = sums
                ks = pl.ds(pl.multiple_of(j * TK, TK), TK)
                k_j = rows_ref[ks, 128:256]
                if coded:
                    k_j = jnp.concatenate([k_j, aug_k[ks, :]], axis=1)
                s = dot(k_j, q_a, ((1,), (1,)))
                if edge:
                    gap = iota((TK, TQ), 0) - iota((TK, TQ), 1)
                    s = jnp.where(gap <= i * TQ - j * TK, s, -1e30)
                new = jnp.maximum(top, jnp.max(s, axis=0, keepdims=True))
                p = jnp.exp2((s - new) * to_exp2)
                dp = dot(rows_ref[ks, 256:384], d_i, ((1,), (1,)))
                p_buf[ks, :] = p
                dp_buf[ks, :] = dp
                tops[pl.ds(pl.multiple_of(j * 8, 8), 8), :] = jnp.broadcast_to(new, (8, TQ))
                keep = jnp.exp2((top - new) * to_exp2)
                return (
                    new,
                    total * keep + jnp.sum(p, axis=0, keepdims=True),
                    delta * keep + jnp.sum(p * dp, axis=0, keepdims=True),
                )

            none = jnp.zeros((1, TQ), F32)
            sums = (jnp.full((1, TQ), -1e30, F32), none, none)
            sums = lax.fori_loop(0, full_tiles, lambda j, a: weigh(j, a, False), sums)
            top, total, delta = weigh(full_tiles, sums, True)
            inv = 1.0 / total
            delta = delta * inv
            acc_o[...] = jnp.zeros_like(acc_o)
            acc_q[...] = jnp.zeros_like(acc_q)

            def spread(j, _):
                ks = pl.ds(pl.multiple_of(j * TK, TK), TK)
                here = tops[pl.ds(pl.multiple_of(j * 8, 8), 8), :][:1]
                w = p_buf[ks, :] * (jnp.exp2((here - top) * to_exp2) * inv)
                rounded = w.astype(BF16)
                ds = (w * (dp_buf[ks, :] - delta)).astype(BF16)
                acc_o[...] += dot(vt[:, ks], rounded)
                acc_q[...] += dot(kt[:, ks], ds)
                dkv[ks, :] += dot(ds, q_i)
                dkv[after(j), :] += dot(rounded, d_i)
                return 0

            lax.fori_loop(0, full_tiles + 1, spread, 0)
            rows_ref[qs, 0:128] = acc_o[...].T.astype(BF16)
            rows_ref[qs, 384:512] = (acc_q[...] * scale).T.astype(BF16)
            return 0

        def ready(j, _):
            ks = pl.ds(pl.multiple_of(j * TK, TK), TK)
            kt[:, ks] = rows_ref[ks, 128:256].astype(F32).T.astype(BF16)
            vt[:, ks] = rows_ref[ks, 256:384].astype(F32).T.astype(BF16)
            dkv[ks, :] = jnp.zeros((TK, 128), F32)
            dkv[after(j), :] = jnp.zeros((TK, 128), F32)
            return 0

        lax.fori_loop(0, span // TK, ready, 0)
        lax.fori_loop(0, span // TQ, body, 0)

        def finish(j, _):
            ks = pl.ds(pl.multiple_of(j * TK, TK), TK)
            rows_ref[ks, 128:256] = (dkv[ks, :] * scale).astype(BF16)
            rows_ref[ks, 256:384] = dkv[after(j), :].astype(BF16)
            return 0

        lax.fori_loop(0, span // TK, finish, 0)

    def codes(g):
        def body(s, _):
            note = meta_in[pl.ds(pl.multiple_of(s * 16, 16), 16), :].astype(F32)
            r = iota((ROWS, 128), 0).astype(F32)
            inside = (r >= note[2 * g : 2 * g + 1]) & (r < note[2 * g + 1 : 2 * g + 2])
            known = iota((ROWS, 128), 1) <= 4
            at = pl.ds(pl.multiple_of(s * ROWS, ROWS), ROWS)
            aug_q[at, :] = jnp.where(inside, 1.0, 0.0).astype(BF16)
            aug_k[at, :] = jnp.where(known & ~inside, -FAR, 0.0).astype(BF16)
            return 0

        lax.fori_loop(0, PEERS, body, 0)

    def hot_work():
        for h in range(4):

            @pl.when(me == HOT_AT[h])
            def _():
                hot_arrive(h)

        @pl.when((me == HOT_AT[0]) | (me == HOT_AT[1]) | (me == HOT_AT[2]) | (me == HOT_AT[3]))
        def _():
            attend(recv_hot, HOT_ROWS, False, lambda i: None)

        for h in range(4):

            @pl.when(me == HOT_AT[h])
            def _():
                back_start(h)

    def work(g, between):
        def load(yy, _):
            at = pl.ds(pl.multiple_of(yy * 768, 768), 768)
            rows_buf[at, :] = recv[g, yy].reshape(768, 512)
            return 0

        def store(yy, _):
            at = pl.ds(pl.multiple_of(yy * 768, 768), 768)
            recv[g, yy] = rows_buf[at, :].reshape(4, 2, ROWS, 512)
            return 0

        lax.fori_loop(0, 4, load, 0)
        attend(rows_buf, SPAN, True, between)
        lax.fori_loop(0, 4, store, 0)

    def ahead(phase, blocks):
        def between(i):
            for e in (0, 1):

                @pl.when(i == blocks[e])
                def _():
                    start_two(phase, e)

        return between

    pack(0, c)
    pl.semaphore_wait(barrier, PEERS - 1 + 3)
    start_one(0, 0)
    pack(0, 1 - c)
    start_one(0, 1)
    pack_hot(0)
    pack_hot(1)
    hot_start(0)
    hot_start(1)
    for k in range(1, PEERS):
        meta_copy(k).start()
    own_meta = pl.ds(pl.multiple_of(me * 16, 16), 16)
    meta_in[own_meta, :] = meta[own_meta, :]
    pack(1, c)
    pack(1, 1 - c)
    start_two(0, 0)
    start_two(0, 1)
    start_one(1, 0)
    start_one(1, 1)

    for k in range(1, PEERS):
        meta_copy(k).wait()
    noted = meta_in[...].astype(F32)
    noted = jnp.where(lax.rem(iota((512, 128), 0), 16) == 4, noted, 0.0)
    flags[0] = jnp.broadcast_to(jnp.max(noted, axis=0, keepdims=True), (16, 128)).astype(BF16)

    def flag_copy(step):
        return pltpu.make_async_remote_copy(
            src_ref=flags.at[0],
            dst_ref=flags.at[step],
            send_sem=flag_ssem.at[step],
            recv_sem=flag_rsem.at[step],
            device_id={"head": lax.rem(col + step, 4)},
            device_id_type=MESH,
        )

    for step in (1, 2, 3):
        flag_copy(step).start()

    codes(0)
    hot_work()
    arrive(0, 0)
    arrive(0, 1)
    drain(0)
    work(0, ahead(1, SWITCH[0]))
    start_one(2, 0)
    start_one(2, 1)
    codes(1)
    arrive(1, 0)
    arrive(1, 1)
    drain(1)
    work(1, ahead(2, SWITCH[1]))
    start_one(3, 0)
    start_one(3, 1)
    arrive(2, 0)
    arrive(2, 1)
    start_two(3, 0)
    back_arrive(0)
    unpack(0, c, False)
    start_two(3, 1)
    unpack(0, 1 - c, True)
    for step in (1, 2, 3):
        flag_copy(step).wait()
    any_flag = jnp.maximum(
        jnp.maximum(flags[0].astype(F32), flags[1].astype(F32)),
        jnp.maximum(flags[2].astype(F32), flags[3].astype(F32)),
    )
    flag_out[...] = any_flag[:8]
    drain(2)
    back_drain(0)
    back_arrive(1)
    arrive(3, 0)
    unpack(1, c, False)
    arrive(3, 1)
    unpack(1, 1 - c, True)
    drain(3)
    back_drain(1)


def settle_kernel(x, o_q, o_k, o_v, o_d, held, wide, done, in_sem, out_sem):
    def load(m):
        return pltpu.make_async_copy(x.at[:, pl.ds(m * 256, 256)], held.at[m], in_sem.at[m])

    outs = ((0, o_q), (3, o_k), (1, o_v), (2, o_d))

    def save(m, n):
        at = pl.ds(m * 1024, 1024)
        return pltpu.make_async_copy(done.at[n, at], outs[n][1].at[at], out_sem.at[m, n])

    for m in range(4):
        load(m).start()
    for m in range(4):
        load(m).wait()
        for n, (a, _) in enumerate(outs):
            for h in range(4):
                wide[n, pl.ds(h, 256, stride=4), :] = held[m, h, :, a * 128 : a * 128 + 128].astype(
                    F32
                )
            done[n, m * 1024 : m * 1024 + 1024, :] = wide[n].astype(BF16)
            save(m, n).start()
    for m in range(4):
        for n in range(4):
            save(m, n).wait()


def settle(x):
    outs = pl.pallas_call(
        settle_kernel,
        out_shape=[jax.ShapeDtypeStruct((4096, 128), BF16)] * 4,
        in_specs=[pl.BlockSpec(memory_space=pl.ANY)],
        out_specs=[pl.BlockSpec(memory_space=pl.ANY)] * 4,
        scratch_shapes=[
            pltpu.VMEM((4, 4, 256, 512), BF16),
            pltpu.VMEM((4, 1024, 128), F32),
            pltpu.VMEM((4, 4096, 128), BF16),
            pltpu.SemaphoreType.DMA((4,)),
            pltpu.SemaphoreType.DMA((4, 4)),
        ],
        compiler_params=pltpu.CompilerParams(vmem_limit_bytes=32 * 2**20),
        name="settle",
    )(x)
    return tuple(a.reshape(1024, 4, 128) for a in outs)


def quick(queries, key_rows, value_rows, out_grad, bucket_id):
    rows = [a.reshape(4096, 128) for a in (queries, key_rows, value_rows, out_grad)]
    vmem = pl.BlockSpec(memory_space=pltpu.VMEM)
    dma = pltpu.SemaphoreType.DMA
    outs = pl.pallas_call(
        kernel,
        out_shape=[
            jax.ShapeDtypeStruct((4, 1024, 512), BF16),
            jax.ShapeDtypeStruct((8, 128), F32),
        ],
        in_specs=[pl.BlockSpec(memory_space=pl.ANY)] * 4 + [vmem],
        out_specs=[vmem] * 2,
        scratch_shapes=[
            pltpu.VMEM((2, 4, 4, 2, ROWS, 512), BF16),
            pltpu.VMEM((2, 64, 512), BF16),
            pltpu.VMEM((2, 4, 4, 2, ROWS, 512), BF16),
            pltpu.VMEM((HOT_ROWS, 512), BF16),
            pltpu.VMEM((2, 4, 4, 2, ROWS, 512), BF16),
            pltpu.VMEM((2, 64, 512), BF16),
            pltpu.VMEM((2, 2, 4, 4, 2, HALF, 512), BF16),
            pltpu.VMEM((SPAN, 512), BF16),
            pltpu.VMEM((512, 128), BF16),
            pltpu.VMEM((512, 128), BF16),
            pltpu.VMEM((4, 16, 128), BF16),
            pltpu.VMEM((8, 1024), I32),
            pltpu.VMEM((1024, 128), I32),
            pltpu.VMEM((SPAN, 128), BF16),
            pltpu.VMEM((SPAN, 128), BF16),
            pltpu.VMEM((128, SPAN), BF16),
            pltpu.VMEM((128, SPAN), BF16),
            pltpu.VMEM((2 * SPAN, 128), F32),
            pltpu.VMEM((SPAN, TQ), F32),
            pltpu.VMEM((SPAN, TQ), F32),
            pltpu.VMEM((SPAN // TK * 8, TQ), F32),
            pltpu.VMEM((128, TQ), F32),
            pltpu.VMEM((128, TQ), F32),
            dma((4, 2, 8)), dma((4, 2, 8)), dma((4, 2, 8)), dma((4, 2, 8)), dma((4, 2, 2)),
            pltpu.SemaphoreType.REGULAR((2,)), dma((PEERS,)), dma((PEERS,)),
            dma((4,)), dma((PEERS,)), dma((PEERS,)), dma((4,)), dma((4,)), dma((4,)),
            dma((4, 4)),
        ],
        compiler_params=pltpu.CompilerParams(
            collective_id=0, has_side_effects=True, vmem_limit_bytes=60 * 2**20
        ),
        name="bucket_layer",
    )(*rows, bucket_id.T)
    return outs[0], outs[1][0, 0] > 0


def bucket_weights(q_part, k_part, valid, scale):
    span = q_part.shape[0]
    sorted_index = jnp.arange(span, dtype=I32)
    allowed = (sorted_index[None, :] <= sorted_index[:, None]) & (
        (valid[None, :] > 0) | (sorted_index[None, :] == sorted_index[:, None])
    )
    scores = jnp.dot(q_part, k_part.T, preferred_element_type=F32) * scale
    scores = jnp.where(allowed, scores, F32(-1e30))
    top = jnp.max(scores, axis=1, keepdims=True)
    expd = jnp.where(allowed, jnp.exp(scores - top), F32(0.0))
    return expd / jnp.sum(expd, axis=1, keepdims=True)


def bucket_forward(block, valid, width):
    scale = 1.0 / math.sqrt(width)
    weights = bucket_weights(block[:, :width], block[:, width : 2 * width], valid, scale)
    rounded = weights.astype(BF16)
    return jnp.dot(rounded, block[:, 2 * width :], preferred_element_type=F32).astype(
        BF16
    )


def bucket_backward(block, d_part, valid, width):
    scale = 1.0 / math.sqrt(width)
    q_part = block[:, :width]
    k_part = block[:, width : 2 * width]
    v_part = block[:, 2 * width : 3 * width]
    weights = bucket_weights(q_part, k_part, valid, scale)
    rounded = weights.astype(BF16)
    dprob = jnp.dot(d_part, v_part.T, preferred_element_type=F32)
    delta = jnp.sum(weights * dprob, axis=1, keepdims=True)
    dscore = (weights * (dprob - delta)).astype(BF16)
    grad_q = (jnp.dot(dscore, k_part, preferred_element_type=F32) * scale).astype(
        BF16
    )
    grad_k = (jnp.dot(dscore.T, q_part, preferred_element_type=F32) * scale).astype(
        BF16
    )
    grad_v = jnp.dot(rounded.T, d_part, preferred_element_type=F32).astype(BF16)
    return (rounded, v_part, grad_q, grad_k, grad_v)


def bucket_grads(block, d_part, valid, width):
    rounded, v_part, grad_q, grad_k, grad_v = bucket_backward(block, d_part, valid, width)
    return jnp.concatenate([grad_q, grad_k, grad_v], axis=1)


def slow(queries, key_rows, value_rows, out_grad, bucket_id, bucket_slot):
    peers = lax.axis_size("seq")
    tok_count, group, width = queries.shape
    per_owner = BUCKETS_PER_HEAD // peers
    span = peers * SLOTS_PER_SOURCE
    total = group * per_owner * span
    owner = bucket_id // per_owner
    local_bucket = bucket_id % per_owner
    head_index = jnp.arange(group, dtype=I32)[None, :]
    flat = (
        (head_index * per_owner + local_bucket) * span + owner * SLOTS_PER_SOURCE + bucket_slot
    ).reshape(-1)
    marks = (
        jnp.zeros((total,), BF16)
        .at[flat]
        .set(BF16(1.0))
        .reshape(group, per_owner, span)
    )

    def spread(rows):
        columns = rows.shape[-1]
        placed = jnp.zeros((total, columns), rows.dtype).at[flat].set(rows.reshape(-1, columns))
        return placed.reshape(group, per_owner, span, columns)

    def collect(buffer):
        columns = buffer.shape[-1]
        return buffer.reshape(total, columns)[flat].reshape(tok_count, group, columns)

    joined = jnp.concatenate([queries, key_rows, value_rows], axis=2)
    blocks, valid = (
        lax.all_to_all(spread(joined), "seq", split_axis=2, concat_axis=2, tiled=True),
        lax.all_to_all(marks, "seq", split_axis=2, concat_axis=2, tiled=True),
    )
    flat_blocks = blocks.reshape(-1, span, 3 * width)
    flat_valid = valid.reshape(-1, span)
    attended = lax.map(
        lambda item: bucket_forward(item[0], item[1], width), (flat_blocks, flat_valid)
    )
    attended = lax.all_to_all(
        attended.reshape(group, per_owner, span, width),
        "seq",
        split_axis=2,
        concat_axis=2,
        tiled=True,
    )
    incoming = lax.all_to_all(spread(out_grad), "seq", split_axis=2, concat_axis=2, tiled=True)
    grads = lax.map(
        lambda item: bucket_grads(item[0], item[1], item[2], width),
        (flat_blocks, incoming.reshape(-1, span, width), flat_valid),
    )
    grads = lax.all_to_all(
        grads.reshape(group, per_owner, span, 3 * width),
        "seq",
        split_axis=2,
        concat_axis=2,
        tiled=True,
    )
    gathered = collect(grads)
    return (
        collect(attended),
        gathered[:, :, :width],
        gathered[:, :, width : 2 * width],
        gathered[:, :, 2 * width :],
    )


def shards(queries, key_rows, value_rows, out_grad, bucket_id, bucket_slot):
    packed, crowded = quick(queries, key_rows, value_rows, out_grad, bucket_id)
    return lax.cond(
        crowded,
        lambda: slow(queries, key_rows, value_rows, out_grad, bucket_id, bucket_slot),
        lambda: settle(packed),
    )


def solution(mesh):
    in_specs = (
        P("seq", "head", None),
        P("seq", "head", None),
        P("seq", "head", None),
        P("seq", "head", None),
        P("seq", "head"),
        P("seq", "head"),
    )
    out_specs = (
        P("seq", "head", None),
        P("seq", "head", None),
        P("seq", "head", None),
        P("seq", "head", None),
    )
    return jax.shard_map(shards, mesh=mesh, in_specs=in_specs, out_specs=out_specs, check_vma=False)
```
